32 devices in a mesh: seq: 16 (over z, y, x), mp: 2 (over core).
Axes of the slice: x: 2, y: 2, z: 4, core: 2. Of those that a mesh axis runs over, the one named last changes fastest.
Arguments:
- tokens: bfloat16 [2, 6144, 768], P(None, 'seq'), may hold values from -6 to 6
- out_grad: bfloat16 [2, 6144, 768], P(None, 'seq'), may hold values from -6 to 6
- gains: float32 [768, 2], replicated, may hold values from 0.5 to 1.5
- routers: float32 [768, 3], replicated, may hold values from -0.21875 to 0.21875
- light_query_key_value_weight: bfloat16 [768, 3, 768], P(None, None, 'mp'), may hold values from -0.21875 to 0.21875
- light_attention_output_weight: bfloat16 [768, 768], P(None, 'mp'), may hold values from -1.75 to 1.75
- heavy_qkv: bfloat16 [768, 3, 768], P(None, None, 'mp'), may hold values from -0.21875 to 0.21875
- heavy_out: bfloat16 [768, 768], P(None, 'mp'), may hold values from -6 to 6
- light_feedforward_input_weight: bfloat16 [768, 2, 1024], P(None, None, 'mp'), may hold values from -0.21875 to 0.21875
- light_feedforward_output_weight: bfloat16 [768, 1024], P(None, 'mp'), may hold values from -0.1875 to 0.1875
- heavy_mlp_in: bfloat16 [768, 2, 4096], P(None, None, 'mp'), may hold values from -0.21875 to 0.21875
- heavy_mlp_out: bfloat16 [768, 4096], P(None, 'mp'), may hold values from -0.09375 to 0.09375
- routed_queries: int32 [2, 1536], P(None, 'seq'), may hold values from 0 to 6143, as said below
- routed_keys: int32 [2, 1536], P(None, 'seq'), may hold values from 0 to 6143, as said below
- routed_mlp: int32 [2, 1536], P(None, 'seq'), may hold values from 0 to 6143, as said below
- block_counts: int32 [2, 16, 3], P(None, 'seq'), may hold values from 1 to 96, as said below
Outputs:
- mixed: bfloat16 [2, 6144, 768], P(None, 'seq')
- input_grad: float32 [2, 6144, 768], P(None, 'seq')
- light_qkv_grad: float32 [768, 3, 768], P(None, None, 'mp')
- light_out_grad: float32 [768, 768], P(None, 'mp')
- heavy_qkv_grad: float32 [768, 3, 768], P(None, None, 'mp')
- heavy_out_grad: float32 [768, 768], P(None, 'mp')
- light_mlp_in_grad: float32 [768, 2, 1024], P(None, None, 'mp')
- light_mlp_out_grad: float32 [768, 1024], P(None, 'mp')
- heavy_mlp_in_grad: float32 [768, 2, 4096], P(None, None, 'mp')
- heavy_mlp_out_grad: float32 [768, 4096], P(None, 'mp')
- gains_grad: float32 [768, 2], replicated
- routers_grad: float32 [768, 3], replicated
The draws below stay inside these ranges and needn't reach their ends.
Inputs may be any that keep to these rules, and one draw needn't show every extreme that they name: block_counts[s,b,k] slots of block b of sequence s are used for kind k; in every draw some block of each kind uses all 96 slots and some uses one. `routed_queries`: slots c * 96 to c * 96 + 95 belong to block c, positions c * 384 to c * 384 + 383 of the sequence; used slots hold distinct positions in rising order, unused slots repeat the block's first slot. `routed_keys`: as for routed_queries, with kind 1 of block_counts. `routed_mlp`: as for routed_queries, with kind 2 of block_counts.
All inputs are finite; a program needn't handle non-finite values.
Results may differ from the reference program's by a relative error of at most 0.022.
Values may be sent and summed in bfloat16 or wider, within the bound.
No kernel may reach another device: no remote copies, remote signals or barrier semaphores. Data moves between devices by JAX's collectives and lax.ppermute only.
A program may use at most 512 MiB of HBM per device.

```python
import math
import jax
import jax.numpy as jnp
from jax import lax

D = 768
LH = 8
LHD = 96
HH = 12
HHD = 64
FFL = 1024
FFH = 4096
WIN = 128
SEQS = 2
SEQ_TOK = 384
CAP = 96
LEN = 6144
N_SEQ = 16


def count_table(key):
    key = jax.random.fold_in(key, 11)
    total_blocks = SEQS * N_SEQ
    key_busy, key_small, key_full, key_single = jax.random.split(key, 4)
    busy = jax.random.randint(key_busy, (3, total_blocks), 0, 3) == 0
    small = jax.random.randint(key_small, (3, total_blocks), 1, CAP // 2 + 1)
    table = jnp.where(busy, CAP, small)
    full_block = jax.random.randint(key_full, (3,), 0, total_blocks)
    single_block = (full_block + jax.random.randint(key_single, (3,), 1, total_blocks)) % total_blocks
    block_ids = jnp.arange(total_blocks, dtype=jnp.int32)
    table = jnp.where(block_ids[None, :] == full_block[:, None], CAP, table)
    table = jnp.where(block_ids[None, :] == single_block[:, None], 1, table)
    return table.reshape(3, SEQS, N_SEQ).transpose(1, 2, 0).astype(jnp.int32)


def route_rows(key, column):
    table = count_table(key)
    total_blocks = SEQS * N_SEQ
    own_key = jax.random.fold_in(key, 20 + column)
    block_keys = jax.random.split(own_key, total_blocks)
    picks = jax.vmap(lambda block_key: jax.random.permutation(block_key, SEQ_TOK))(block_keys)[:, :CAP]
    ordered = jnp.sort(picks, axis=-1)
    used = table[:, :, column].reshape(total_blocks)
    slot_ids = jnp.arange(CAP, dtype=jnp.int32)
    filled = jnp.where(slot_ids[None, :] < used[:, None], ordered, ordered[:, :1])
    offsets = jnp.arange(total_blocks, dtype=jnp.int32) % N_SEQ * SEQ_TOK
    return (filled + offsets[:, None]).reshape(SEQS, N_SEQ * CAP).astype(jnp.int32)


def draw_routed_queries(key, part):
    return route_rows(key, 0)


def draw_routed_keys(key, part):
    return route_rows(key, 1)


def draw_routed_mlp(key, part):
    return route_rows(key, 2)


def draw_block_counts(key, part):
    return count_table(key)


def levels(key, shape, shards, least, high):
    factor_of = 1.0
    for axis_at, blocks in shards:
        draws = jax.random.uniform(jax.random.fold_in(jax.random.fold_in(key, 6), axis_at), (blocks,), jnp.float32, least / len(shards), high / len(shards))
        factor_of = factor_of * jnp.repeat(jnp.exp(draws), shape[axis_at] // blocks).reshape((-1,) + (1,) * (len(shape) - 1 - axis_at))
    return factor_of


def gaussian(key, extent, width, limit, cuts=(), kind=jnp.bfloat16):
    values = jax.random.normal(key, extent, jnp.float32) * width
    if len(cuts) > 0:
        values = levels(key, extent, cuts, -0.22, 0.18) * values
    return jnp.clip(values, min=-limit, max=limit).astype(kind)


def setup_inputs(seed: int = 0) -> dict:
    keys = jax.random.split(jax.random.key(seed), 17)
    tokens = gaussian(keys[0], (SEQS, LEN, D), 1.0, 6.0, ((1, 16),))
    out_grad = gaussian(keys[1], (SEQS, LEN, D), 1.0, 6.0, ((1, 16),))
    gains = jnp.clip(1.0 + 0.1 * jax.random.normal(keys[2], (D, 2), jnp.float32), 0.5, 1.5)
    routers = gaussian(keys[3], (D, 3), D ** -0.5, 0.21875, (), jnp.float32)
    light_query_key_value_weight = gaussian(keys[4], (D, 3, LH * LHD), D ** -0.5, 0.21875, ((2, 2),))
    light_attention_output_weight = gaussian(keys[5], (D, LH * LHD), (LH * LHD // 64) ** -0.5, 1.75, ((1, 2),))
    heavy_qkv = gaussian(keys[6], (D, 3, HH * HHD), D ** -0.5, 0.21875, ((2, 2),))
    heavy_out = gaussian(keys[7], (D, HH * HHD), 1 ** -0.5, 6.0, ((1, 2),))
    light_feedforward_input_weight = gaussian(keys[8], (D, 2, FFL), D ** -0.5, 0.21875, ((2, 2),))
    light_feedforward_output_weight = gaussian(keys[9], (D, FFL), FFL ** -0.5, 0.1875, ((1, 2),))
    heavy_mlp_in = gaussian(keys[10], (D, 2, FFH), D ** -0.5, 0.21875, ((2, 2),))
    heavy_mlp_out = gaussian(keys[11], (D, FFH), FFH ** -0.5, 0.09375, ((1, 2),))
    routed_queries = draw_routed_queries(jax.random.fold_in(keys[16], 71), 0)
    routed_keys = draw_routed_keys(jax.random.fold_in(keys[16], 71), 0)
    routed_mlp = draw_routed_mlp(jax.random.fold_in(keys[16], 71), 0)
    block_counts = draw_block_counts(jax.random.fold_in(keys[16], 71), 0)
    return dict(tokens=tokens, out_grad=out_grad, gains=gains, routers=routers, light_query_key_value_weight=light_query_key_value_weight, light_attention_output_weight=light_attention_output_weight, heavy_qkv=heavy_qkv, heavy_out=heavy_out, light_feedforward_input_weight=light_feedforward_input_weight, light_feedforward_output_weight=light_feedforward_output_weight, heavy_mlp_in=heavy_mlp_in, heavy_mlp_out=heavy_mlp_out, routed_queries=routed_queries, routed_keys=routed_keys, routed_mlp=routed_mlp, block_counts=block_counts)


EPSILON = 1e-06
MASKED = -1e+30
TOP_PRECISION = lax.Precision.HIGHEST

@jax.custom_vjp
def low(v):
    return lax.optimization_barrier(v.astype(jnp.bfloat16)).astype(jnp.float32)

@jax.custom_vjp
def lower_precision_backward(v):
    return v

def low_keep(v):
    return (low(v), None)

def low_pass(kept, grad):
    return (grad,)

def back_keep(v):
    return (v, None)

def back_low(kept, grad):
    return (low(grad),)
low.defvjp(low_keep, low_pass)
lower_precision_backward.defvjp(back_keep, back_low)

def rounded_pair_values(values):
    return low(lower_precision_backward(values))

def norm_rows(values, gain_vec):
    factor = lax.rsqrt(lax.optimization_barrier(jnp.mean(values * values, axis=-1, keepdims=True)) + EPSILON)
    return values * factor * gain_vec

def gated_gelu(gate_in, up_in):
    return jax.nn.gelu(gate_in, approximate=True) * up_in

def slot_valid(block_counts, column):
    per_slot = jnp.repeat(block_counts[:, :, column], CAP, axis=1)
    slot_ids = jnp.tile(jnp.arange(CAP, dtype=jnp.int32), N_SEQ)
    return slot_ids[None, :] < per_slot

def light_sequence(query_all, key_all, value_all):
    blocks = LEN // WIN
    query_tiles = query_all.reshape(blocks, WIN, LH, LHD)
    margin = ((WIN, WIN), (0, 0))
    key_pad = jnp.pad(key_all, margin).reshape(blocks + 2, WIN, LH, LHD)
    value_pad = jnp.pad(value_all, margin).reshape(blocks + 2, WIN, LH, LHD)
    key_tiles = jnp.concatenate([key_pad[:-2], key_pad[1:-1], key_pad[2:]], axis=1)
    value_tiles = jnp.concatenate([value_pad[:-2], value_pad[1:-1], value_pad[2:]], axis=1)
    row_ids = jnp.arange(WIN, dtype=jnp.int32)
    col_ids = jnp.arange(3 * WIN, dtype=jnp.int32)
    within = jnp.abs(col_ids[None, :] - WIN - row_ids[:, None]) < WIN

    def one_block(block_items):
        query_block, key_block, value_block, block_index = block_items
        key_place = block_index * WIN + col_ids - WIN
        allowed = within & ((key_place >= 0) & (key_place < LEN))[None, :]
        scores = lower_precision_backward(jnp.einsum('ihd,jhd->hij', query_block, key_block, precision=TOP_PRECISION) * (1.0 / math.sqrt(LHD)))
        probs_block = jax.nn.softmax(jnp.where(allowed[None], scores, MASKED), axis=-1)
        return jnp.einsum('hij,jhd->ihd', low(probs_block), value_block, precision=TOP_PRECISION)
    mixed_rows = lax.map(jax.checkpoint(one_block), (query_tiles, key_tiles, value_tiles, jnp.arange(blocks, dtype=jnp.int32)))
    return rounded_pair_values(mixed_rows.reshape(LEN, LH * LHD))

def heavy_sequence(low_in, normed_in, query_ids, key_ids, query_ok, key_ok, weights_q, weights_kv, weights_out, router_q, router_kv):
    query_in = low_in[query_ids]
    query_heads = rounded_pair_values(jnp.einsum('cd,dk->ck', query_in, weights_q, precision=TOP_PRECISION)).reshape(-1, HH, HHD)
    key_in = low_in[key_ids]
    key_heads = rounded_pair_values(jnp.einsum('cd,dk->ck', key_in, weights_kv[:, 0], precision=TOP_PRECISION)).reshape(-1, HH, HHD)
    raw_value = lower_precision_backward(jnp.einsum('cd,dk->ck', key_in, weights_kv[:, 1], precision=TOP_PRECISION))
    key_gate = jax.nn.sigmoid(jnp.dot(normed_in[key_ids], router_kv, precision=TOP_PRECISION))
    value_heads = rounded_pair_values(key_gate[:, None] * raw_value).reshape(-1, HH, HHD)
    query_gate = jax.nn.sigmoid(jnp.dot(normed_in[query_ids], router_q, precision=TOP_PRECISION))
    rows_block = math.gcd(N_SEQ * CAP, 512)

    def one_block(query_block):
        scores = lower_precision_backward(jnp.einsum('qhd,khd->hqk', query_block, key_heads, precision=TOP_PRECISION) * (1.0 / math.sqrt(HHD)))
        probs_block = jax.nn.softmax(jnp.where(key_ok[None, None, :], scores, MASKED), axis=-1)
        return jnp.einsum('hqk,khd->qhd', low(probs_block), value_heads, precision=TOP_PRECISION)
    mixed_rows = lax.map(jax.checkpoint(one_block), query_heads.reshape(-1, rows_block, HH, HHD)).reshape(-1, HH * HHD)
    heavy_part = lower_precision_backward(jnp.einsum('ck,dk->cd', rounded_pair_values(mixed_rows), weights_out, precision=TOP_PRECISION))
    weight = jnp.where(query_ok, query_gate, 0.0)
    return jnp.zeros((LEN, D), jnp.float32).at[query_ids].add(weight[:, None] * heavy_part)

def heavy_mlp(low_in, normed_in, row_ids, row_ok, weights_in, weights_out, router_vec):
    rows_in = low_in[row_ids]
    paired_gate_values = lower_precision_backward(jnp.einsum('cd,dkf->ckf', rows_in, weights_in, precision=TOP_PRECISION))
    hidden_activations = low(gated_gelu(paired_gate_values[:, 0], paired_gate_values[:, 1]))
    heavy_part = lower_precision_backward(jnp.einsum('cf,df->cd', hidden_activations, weights_out, precision=TOP_PRECISION))
    gate_value = jax.nn.sigmoid(jnp.dot(normed_in[row_ids], router_vec, precision=TOP_PRECISION))
    weight = jnp.where(row_ok, gate_value, 0.0)
    return jnp.zeros((LEN, D), jnp.float32).at[row_ids].add(weight[:, None] * heavy_part)

def forward(inputs, gains, routers, light_query_key_value_weight, light_attention_output_weight, heavy_qkv, heavy_out, light_feedforward_input_weight, light_feedforward_output_weight, heavy_mlp_in, heavy_mlp_out, routed_queries, routed_keys, routed_mlp, block_counts):
    normed = norm_rows(inputs, gains[:, 0])
    normalized_lower_precision = low(normed)
    light_projected_rows = rounded_pair_values(jnp.einsum('pnz,zwu->pnwu', normalized_lower_precision, light_query_key_value_weight, precision=TOP_PRECISION))
    light_blended_rows = jax.vmap(light_sequence)(light_projected_rows[:, :, 0], light_projected_rows[:, :, 1], light_projected_rows[:, :, 2])
    attention_layer = jnp.einsum('nqk,mk->nqm', light_blended_rows, light_attention_output_weight, precision=TOP_PRECISION)
    query_ok = slot_valid(block_counts, 0)
    key_ok = slot_valid(block_counts, 1)
    mlp_ok = slot_valid(block_counts, 2)
    heavy_part = jax.vmap(heavy_sequence, in_axes=(0, 0, 0, 0, 0, 0, None, None, None, None, None))(normalized_lower_precision, normed, routed_queries, routed_keys, query_ok, key_ok, heavy_qkv[:, 0], heavy_qkv[:, 1:], heavy_out, routers[:, 0], routers[:, 1])
    middle = inputs + lower_precision_backward(attention_layer + heavy_part)
    normed_two = norm_rows(middle, gains[:, 1])
    lower_precision_second = low(normed_two)
    paired_gate_values = lower_precision_backward(jnp.einsum('ntu,uhy->nthy', lower_precision_second, light_feedforward_input_weight, precision=TOP_PRECISION))
    hidden_activations = low(gated_gelu(paired_gate_values[:, :, 0], paired_gate_values[:, :, 1]))
    feedforward_portion = jnp.einsum('euo,wo->euw', hidden_activations, light_feedforward_output_weight, precision=TOP_PRECISION)
    heavy_two = jax.vmap(heavy_mlp, in_axes=(0, 0, 0, 0, None, None, None))(lower_precision_second, normed_two, routed_mlp, mlp_ok, heavy_mlp_in, heavy_mlp_out, routers[:, 2])
    return middle + feedforward_portion + heavy_two

def reference(tokens, out_grad, gains, routers, light_query_key_value_weight, light_attention_output_weight, heavy_qkv, heavy_out, light_feedforward_input_weight, light_feedforward_output_weight, heavy_mlp_in, heavy_mlp_out, routed_queries, routed_keys, routed_mlp, block_counts):
    floats = [array_in.astype(jnp.float32) for array_in in (tokens, gains, routers, light_query_key_value_weight, light_attention_output_weight, heavy_qkv, heavy_out, light_feedforward_input_weight, light_feedforward_output_weight, heavy_mlp_in, heavy_mlp_out)]

    def wrapped(*values):
        return forward(*values, routed_queries, routed_keys, routed_mlp, block_counts)
    result, pull_back = jax.vjp(wrapped, *floats)
    gradients = pull_back(out_grad.astype(jnp.float32))
    return (result.astype(jnp.bfloat16), gradients[0], gradients[3], gradients[4], gradients[5], gradients[6], gradients[7], gradients[8], gradients[9], gradients[10], gradients[1], gradients[2])
```

```python
import math

import jax
import jax.numpy as jnp
from jax import lax
from jax.experimental import pallas as pl
from jax.experimental.pallas import tpu as pltpu
from jax.sharding import PartitionSpec as P

LHD = 96
HHD = 64
WIN = 128


EPSILON = 1e-06
MASKED = -1e30
TOP_PRECISION = lax.Precision.HIGHEST


def padded(value, sides, width):
    for axis, dim in sides:
        peers, length = (lax.axis_size(axis), value.shape[dim])
        up = [(i, (i + 1) % peers) for i in range(peers - 1)]
        down = [(j, i) for i, j in up]
        last = lax.slice_in_dim(value, length - width, length, axis=dim)
        leading = lax.slice_in_dim(value, 0, width, axis=dim)
        before = lax.ppermute(last, axis, up)
        after = lax.ppermute(leading, axis, down)
        value = jnp.concatenate([before, value, after], axis=dim)
    return value


def norm_rows(values, gain_vec):
    factor = lax.rsqrt(jnp.mean(values * values, axis=-1, keepdims=True) + EPSILON)
    return (values * factor * gain_vec, factor)


def norm_back(values, factor, gain_vec, grad_in):
    weighted = grad_in * gain_vec
    inner = jnp.mean(weighted * values, axis=-1, keepdims=True)
    return factor * weighted - values * (factor * factor * factor) * inner


def gated_gelu(gate_in, up_in):
    return jax.nn.gelu(gate_in, approximate=True) * up_in


def one_hot_rows(where_rows, length):
    places = jnp.arange(length, dtype=jnp.int32)
    return (where_rows[:, :, None] == places[None, None, :]).astype(jnp.bfloat16)


def pick_rows(source, hot):
    return jnp.einsum("sct,std->scd", hot, source, preferred_element_type=jnp.float32).astype(
        source.dtype
    )


def pick_values(source, hot):
    return jnp.sum(hot.astype(jnp.float32) * source[:, None, :], axis=-1)


def place_values(values, hot):
    return jnp.sum(hot.astype(jnp.float32) * values[:, :, None], axis=1)


def add_rows(target, hot, values):
    high = values.astype(jnp.bfloat16)
    rest = (values - high.astype(jnp.float32)).astype(jnp.bfloat16)
    return target + jnp.einsum(
        "sct,scd->std",
        jnp.concatenate([hot, hot], axis=1),
        jnp.concatenate([high, rest], axis=1),
        preferred_element_type=jnp.float32,
    )


def other_core(value):
    return lax.ppermute(value, "mp", [(0, 1), (1, 0)])


def core_sum(value):
    low_value = value.astype(jnp.bfloat16)
    return low_value.astype(jnp.float32) + other_core(low_value).astype(jnp.float32)


def lanes_of(shape):
    return lax.broadcasted_iota(jnp.int32, shape, len(shape) - 1)


def rows_dot(a, b):
    return lax.dot_general(a, b, (((1,), (1,)), ((), ())), preferred_element_type=jnp.float32)


def cols_dot(a, b):
    return lax.dot_general(a, b, (((0,), (0,)), ((), ())), preferred_element_type=jnp.float32)


def key_operand(pair, extra):
    lane = lanes_of(pair.shape)
    moved = pltpu.roll(pair.astype(jnp.float32), HHD, 1)
    bias = extra[:, HHD : HHD + 1].astype(jnp.float32)
    return jnp.where(lane < HHD, moved, jnp.where(lane == HHD, bias, 0.0)).astype(jnp.bfloat16)


def query_operand(pair, scale):
    lane = lanes_of(pair.shape)
    scaled = pair.astype(jnp.float32) * scale
    return jnp.where(lane < HHD, scaled, jnp.where(lane == HHD, 1.0, 0.0)).astype(jnp.bfloat16)


def heavy_forward_kernel(tile, scale, pair_ref, extra_ref, kept_ref, key_ref):
    @pl.when(pl.program_id(1) == 0)
    def _():
        key_ref[...] = key_operand(pair_ref[0], extra_ref[0])

    start = pl.multiple_of(pl.program_id(1) * tile, tile)
    query = query_operand(pair_ref[0, pl.ds(start, tile), :], scale)
    scores = rows_dot(query, key_ref[...])
    top = jnp.max(scores, axis=-1, keepdims=True)
    expo = jnp.exp(scores - top)
    total = jnp.sum(expo, axis=-1, keepdims=True)
    mix = jnp.dot(
        expo.astype(jnp.bfloat16), extra_ref[0], preferred_element_type=jnp.float32
    ) / total
    lane = lanes_of(mix.shape)
    kept_ref[0] = jnp.where(lane < HHD, mix, top + jnp.log(total))


def heavy_backward_kernel(
    tile, scale, pair_ref, extra_ref, kept_ref, grad_ref, both_ref, value_ref, key_ref, dk_ref, dv_ref
):
    step = pl.program_id(1)

    @pl.when(step == 0)
    def _():
        key_ref[...] = key_operand(pair_ref[0], extra_ref[0])
        dk_ref[...] = jnp.zeros_like(dk_ref)
        dv_ref[...] = jnp.zeros_like(dv_ref)

    start = pl.multiple_of(step * tile, tile)
    query = query_operand(pair_ref[0, pl.ds(start, tile), :], scale)
    lane = lanes_of(query.shape)
    kept = kept_ref[0]
    grad = grad_ref[0]
    lse = kept[:, HHD : HHD + 1]
    delta = jnp.sum(
        kept[:, :HHD] * grad[:, :HHD].astype(jnp.float32), axis=-1, keepdims=True
    )
    probs = jnp.exp(rows_dot(query, key_ref[...]) - lse)
    prob_grad = rows_dot(grad, extra_ref[0])
    score_grad = (probs * (prob_grad - delta)).astype(jnp.bfloat16)
    query_grad = jnp.dot(score_grad, key_ref[...], preferred_element_type=jnp.float32) * scale
    both_ref[0, pl.ds(start, tile), :] = jnp.where(lane < HHD, query_grad, 0.0).astype(jnp.bfloat16)
    dk_ref[...] += cols_dot(score_grad, query)
    dv_ref[...] += cols_dot(probs.astype(jnp.bfloat16), grad)

    @pl.when(step == pl.num_programs(1) - 1)
    def _():
        spot = lanes_of(dk_ref.shape)
        moved = pltpu.roll(dk_ref[...], HHD, 1)
        query_part = both_ref[0].astype(jnp.float32)
        both_ref[0] = jnp.where(spot < HHD, query_part, moved).astype(jnp.bfloat16)
        value_ref[0] = dv_ref[...].astype(jnp.bfloat16)


def query_tile(length):
    return 256 if length % 256 == 0 else 96


def heavy_forward(pair, extra, scale):
    pairs, length, lanes = pair.shape
    tile = query_tile(length)
    whole = pl.BlockSpec((1, length, lanes), lambda p, i: (p, 0, 0))
    return pl.pallas_call(
        lambda *refs: heavy_forward_kernel(tile, scale, *refs),
        grid=(pairs, length // tile),
        in_specs=[whole, whole],
        out_specs=pl.BlockSpec((1, tile, lanes), lambda p, i: (p, i, 0)),
        out_shape=jax.ShapeDtypeStruct(pair.shape, jnp.float32),
        scratch_shapes=[pltpu.VMEM((length, lanes), jnp.bfloat16)],
        compiler_params=pltpu.CompilerParams(vmem_limit_bytes=60 * 2**20),
        name="heavy_forward",
    )(pair, extra)


def heavy_backward(pair, extra, kept, grad, scale):
    pairs, length, lanes = pair.shape
    tile = query_tile(length)
    whole = pl.BlockSpec((1, length, lanes), lambda p, i: (p, 0, 0))
    rows = pl.BlockSpec((1, tile, lanes), lambda p, i: (p, i, 0))
    return pl.pallas_call(
        lambda *refs: heavy_backward_kernel(tile, scale, *refs),
        grid=(pairs, length // tile),
        in_specs=[whole, whole, rows, rows],
        out_specs=[whole, whole],
        out_shape=[jax.ShapeDtypeStruct(pair.shape, jnp.bfloat16)] * 2,
        scratch_shapes=[
            pltpu.VMEM((length, lanes), jnp.bfloat16),
            pltpu.VMEM((length, lanes), jnp.float32),
            pltpu.VMEM((length, lanes), jnp.float32),
        ],
        compiler_params=pltpu.CompilerParams(vmem_limit_bytes=60 * 2**20),
        name="heavy_backward",
    )(pair, extra, kept, grad)


def windows(extended, blocks, tile_width):
    dims_in = extended.shape
    tile_view = extended.reshape((dims_in[0], blocks + 2, tile_width) + dims_in[2:])
    return jnp.concatenate([tile_view[:, :-2], tile_view[:, 1:-1], tile_view[:, 2:]], axis=2)


def unwindows(tiled, tile_width):
    first_part = tiled[:, :, :tile_width]
    second_part = tiled[:, :, tile_width : 2 * tile_width]
    third_part = tiled[:, :, 2 * tile_width :]
    zero_tile = jnp.zeros_like(first_part[:, :1])
    summed_tiles = (
        jnp.concatenate([first_part, zero_tile, zero_tile], axis=1)
        + jnp.concatenate([zero_tile, second_part, zero_tile], axis=1)
        + jnp.concatenate([zero_tile, zero_tile, third_part], axis=1)
    )
    dims_in = summed_tiles.shape
    return summed_tiles.reshape((dims_in[0], dims_in[1] * dims_in[2]) + dims_in[3:])


def window_mask(blocks, tile_width, row_base, length):
    row_ids = jnp.arange(tile_width, dtype=jnp.int32)
    col_ids = jnp.arange(3 * tile_width, dtype=jnp.int32)
    tile_ids = jnp.arange(blocks, dtype=jnp.int32)
    within = jnp.abs(col_ids[None, :] - tile_width - row_ids[:, None]) < tile_width
    key_place = row_base + tile_ids[:, None] * tile_width + col_ids[None, :] - tile_width
    inside = (key_place >= 0) & (key_place < length)
    return within[None, :, :] & inside[:, None, :]


def shards(
    tokens,
    out_grad,
    gains,
    routers,
    light_query_key_value_weight,
    light_attention_output_weight,
    heavy_qkv,
    heavy_out,
    light_feedforward_input_weight,
    light_feedforward_output_weight,
    heavy_mlp_in,
    heavy_mlp_out,
    routed_queries,
    routed_keys,
    routed_mlp,
    block_counts,
):
    seq_count, local_len, model_width = tokens.shape
    seq_devices = lax.axis_size("seq")
    row_base = lax.axis_index("seq") * local_len
    full_len = seq_devices * local_len
    blocks = local_len // WIN
    light_cols = light_query_key_value_weight.shape[2]
    light_heads = light_cols // LHD
    heavy_cols = heavy_qkv.shape[2]
    heavy_heads = heavy_cols // HHD
    capacity = routed_queries.shape[1]
    light_scale = 1.0 / math.sqrt(LHD)
    heavy_scale = 1.0 / math.sqrt(HHD)
    inputs = tokens.astype(jnp.float32)
    normed, factor_one = norm_rows(inputs, gains[:, 0])
    normalized_lower_precision = normed.astype(jnp.bfloat16)
    light_projected_rows = jnp.einsum(
        "std,djc->stjc",
        normalized_lower_precision,
        light_query_key_value_weight,
        preferred_element_type=jnp.float32,
    ).astype(jnp.bfloat16)
    extended = padded(light_projected_rows[:, :, 1:], (("seq", 1),), WIN)
    query_tiles = light_projected_rows[:, :, 0].reshape(seq_count, blocks, WIN, light_heads, LHD)
    key_tiles = windows(extended[:, :, 0], blocks, WIN).reshape(
        seq_count, blocks, 3 * WIN, light_heads, LHD
    )
    value_tiles = windows(extended[:, :, 1], blocks, WIN).reshape(
        seq_count, blocks, 3 * WIN, light_heads, LHD
    )
    allowed = window_mask(blocks, WIN, row_base, full_len)[None, :, None]
    light_scores = (
        jnp.einsum("sbihd,sbjhd->sbhij", query_tiles, key_tiles, preferred_element_type=jnp.float32)
        * light_scale
    )
    light_scores = jnp.where(allowed, light_scores, MASKED)
    top_light = jnp.max(light_scores, axis=-1, keepdims=True)
    expo_light = jnp.exp(light_scores - top_light)
    sum_light = jnp.sum(expo_light, axis=-1, keepdims=True)
    light_probs = expo_light / sum_light
    light_lse = top_light + jnp.log(sum_light)
    light_blended_rows = jnp.einsum(
        "sbhij,sbjhd->sbihd",
        light_probs.astype(jnp.bfloat16),
        value_tiles,
        preferred_element_type=jnp.float32,
    )
    light_blended_rows = light_blended_rows.astype(jnp.bfloat16).reshape(
        seq_count, local_len, light_cols
    )
    attn_part = jnp.einsum(
        "stc,dc->std",
        light_blended_rows,
        light_attention_output_weight,
        preferred_element_type=jnp.float32,
    )
    counts_here = block_counts[:, 0, :]
    slot_ids = jnp.arange(capacity, dtype=jnp.int32)[None, :]
    valid_query = slot_ids < counts_here[:, 0:1]
    valid_key = slot_ids < counts_here[:, 1:2]
    valid_mlp = slot_ids < counts_here[:, 2:3]
    query_rows = routed_queries - row_base
    key_rows = routed_keys - row_base
    mlp_rows = routed_mlp - row_base
    query_hot = one_hot_rows(query_rows, local_len)
    key_hot = one_hot_rows(key_rows, local_len)
    mlp_hot = one_hot_rows(mlp_rows, local_len)
    logits_one = jnp.einsum("std,dk->kst", normed, routers[:, :2], precision=TOP_PRECISION)
    query_in = pick_rows(normalized_lower_precision, query_hot)
    query_gate = jax.nn.sigmoid(pick_values(logits_one[0], query_hot))
    heavy_query = jnp.einsum(
        "scd,dk->sck", query_in, heavy_qkv[:, 0], preferred_element_type=jnp.float32
    ).astype(jnp.bfloat16)
    key_in = pick_rows(normalized_lower_precision, key_hot)
    key_gate = jax.nn.sigmoid(pick_values(logits_one[1], key_hot))
    key_both = jnp.einsum(
        "scd,djk->scjk", key_in, heavy_qkv[:, 1:], preferred_element_type=jnp.float32
    )
    heavy_key = key_both[:, :, 0].astype(jnp.bfloat16)
    raw_value = key_both[:, :, 1]
    heavy_value = (key_gate[..., None] * raw_value).astype(jnp.bfloat16)
    key_bias = jnp.where(valid_key, 0.0, MASKED).astype(jnp.bfloat16)

    def to_pairs(parts):
        split = jnp.concatenate(
            [p.reshape(seq_count, capacity, heavy_heads, HHD) for p in parts], axis=-1
        )
        pairs = split.transpose(0, 2, 1, 3).reshape(
            seq_count * heavy_heads, capacity, HHD * len(parts)
        )
        return pairs

    def across(pairs):
        spare = pairs_here * seq_devices - pairs.shape[0]
        sent = jnp.pad(pairs, ((0, spare), (0, 0), (0, 0)))
        return lax.all_to_all(sent, "seq", split_axis=0, concat_axis=1, tiled=True)

    def back(per_pair):
        got = lax.all_to_all(per_pair, "seq", split_axis=1, concat_axis=0, tiled=True)
        return got[: seq_count * heavy_heads].reshape(seq_count, heavy_heads, capacity, -1)

    pairs_here = -(-(seq_count * heavy_heads) // seq_devices)
    bias_column = jnp.broadcast_to(
        key_bias[:, None, :, None], (seq_count, heavy_heads, capacity, HHD)
    ).reshape(seq_count * heavy_heads, capacity, HHD)
    pair_in = across(
        jnp.concatenate([to_pairs([heavy_query, heavy_key, heavy_value]), bias_column], axis=-1)
    )
    pair_both, pair_extra = pair_in[:, :, : 2 * HHD], pair_in[:, :, 2 * HHD :]
    pair_kept = heavy_forward(pair_both, pair_extra, heavy_scale)
    heavy_mix = back(pair_kept[:, :, :HHD].astype(jnp.bfloat16))
    heavy_mix = heavy_mix.transpose(0, 2, 1, 3).reshape(seq_count, capacity, heavy_cols)
    heavy_rows = jnp.einsum("sck,dk->scd", heavy_mix, heavy_out, preferred_element_type=jnp.float32)
    query_weight = jnp.where(valid_query, query_gate, 0.0)
    attn_part = add_rows(attn_part, query_hot, query_weight[..., None] * heavy_rows)
    attention_layer = core_sum(attn_part)
    middle = inputs + attention_layer
    normed_two, factor_two = norm_rows(middle, gains[:, 1])
    lower_precision_second = normed_two.astype(jnp.bfloat16)
    paired_gate_values = jnp.einsum(
        "std,dkf->stkf",
        lower_precision_second,
        light_feedforward_input_weight,
        preferred_element_type=jnp.float32,
    )
    hidden_activations = gated_gelu(
        paired_gate_values[:, :, 0], paired_gate_values[:, :, 1]
    ).astype(jnp.bfloat16)
    feedforward_portion = jnp.einsum(
        "stf,df->std",
        hidden_activations,
        light_feedforward_output_weight,
        preferred_element_type=jnp.float32,
    )
    mlp_in = pick_rows(lower_precision_second, mlp_hot)
    logits_two = jnp.einsum("std,d->st", normed_two, routers[:, 2], precision=TOP_PRECISION)
    mlp_gate = jax.nn.sigmoid(pick_values(logits_two, mlp_hot))
    heavy_gates = jnp.einsum(
        "scd,dkf->sckf", mlp_in, heavy_mlp_in, preferred_element_type=jnp.float32
    )
    heavy_hidden = gated_gelu(heavy_gates[:, :, 0], heavy_gates[:, :, 1]).astype(jnp.bfloat16)
    heavy_mlp_rows = jnp.einsum(
        "scf,df->scd", heavy_hidden, heavy_mlp_out, preferred_element_type=jnp.float32
    )
    mlp_weight = jnp.where(valid_mlp, mlp_gate, 0.0)
    feedforward_portion = add_rows(
        feedforward_portion, mlp_hot, mlp_weight[..., None] * heavy_mlp_rows
    )
    mlp_total = core_sum(feedforward_portion)
    result = (middle + mlp_total).astype(jnp.bfloat16)
    upstream = out_grad.astype(jnp.float32)
    hidden_grad = jnp.einsum(
        "std,df->stf", out_grad, light_feedforward_output_weight, preferred_element_type=jnp.float32
    )
    unused_light, pull_light = jax.vjp(
        gated_gelu, paired_gate_values[:, :, 0], paired_gate_values[:, :, 1]
    )
    gate_grad, up_grad = pull_light(hidden_grad)
    gates_grad = jnp.stack([gate_grad, up_grad], axis=2).astype(jnp.bfloat16)
    light_mlp_out_grad = jnp.einsum(
        "std,stf->df", out_grad, hidden_activations, preferred_element_type=jnp.float32
    )
    light_mlp_in_grad = jnp.einsum(
        "std,stkf->dkf", lower_precision_second, gates_grad, preferred_element_type=jnp.float32
    )
    low_two_grad = jnp.einsum(
        "stkf,dkf->std",
        gates_grad,
        light_feedforward_input_weight,
        preferred_element_type=jnp.float32,
    )
    mlp_upstream = pick_rows(out_grad, mlp_hot).astype(jnp.float32)
    slot_mlp_grad = (mlp_weight[..., None] * mlp_upstream).astype(jnp.bfloat16)
    mlp_gate_grad = jnp.sum(mlp_upstream * heavy_mlp_rows, axis=-1)
    heavy_hidden_grad = jnp.einsum(
        "scd,df->scf", slot_mlp_grad, heavy_mlp_out, preferred_element_type=jnp.float32
    )
    unused_heavy, pull_heavy = jax.vjp(gated_gelu, heavy_gates[:, :, 0], heavy_gates[:, :, 1])
    heavy_gate_grad, heavy_up_grad = pull_heavy(heavy_hidden_grad)
    heavy_gates_grad = jnp.stack([heavy_gate_grad, heavy_up_grad], axis=2).astype(jnp.bfloat16)
    all_slots = seq_count * capacity * seq_devices
    gather_heavy = 2 * all_slots * model_width < 4 * (heavy_mlp_in.size + heavy_mlp_out.size)
    if gather_heavy:
        first_core = lax.axis_index("mp") == 0
        here = lax.all_gather(
            jnp.where(first_core, mlp_in, slot_mlp_grad), "seq", axis=1, tiled=True
        )
        there = other_core(here)
        slot_in = jnp.where(first_core, here, there)
        slot_grad_all = jnp.where(first_core, there, here)
        gates_all = jnp.einsum(
            "scd,dkf->sckf", slot_in, heavy_mlp_in, preferred_element_type=jnp.float32
        )
        hidden_grad_all = jnp.einsum(
            "scd,df->scf", slot_grad_all, heavy_mlp_out, preferred_element_type=jnp.float32
        )
        hidden_all, pull_all = jax.vjp(gated_gelu, gates_all[:, :, 0], gates_all[:, :, 1])
        gate_grad_all, up_grad_all = pull_all(hidden_grad_all)
        hidden_all = hidden_all.astype(jnp.bfloat16)
        gates_grad_all = jnp.stack([gate_grad_all, up_grad_all], axis=2).astype(jnp.bfloat16)
    else:
        slot_in, slot_grad_all, hidden_all = mlp_in, slot_mlp_grad, heavy_hidden
        gates_grad_all = heavy_gates_grad
    heavy_mlp_out_grad = jnp.einsum(
        "scd,scf->df", slot_grad_all, hidden_all, preferred_element_type=jnp.float32
    )
    heavy_mlp_in_grad = jnp.einsum(
        "scd,sckf->dkf", slot_in, gates_grad_all, preferred_element_type=jnp.float32
    )
    low_two_grad = add_rows(
        low_two_grad,
        mlp_hot,
        jnp.einsum(
            "sckf,dkf->scd", heavy_gates_grad, heavy_mlp_in, preferred_element_type=jnp.float32
        ),
    )
    normed_two_grad, mlp_gate_sum = core_sum(low_two_grad), core_sum(mlp_gate_grad)
    mlp_logit_grad = jnp.where(valid_mlp, mlp_gate_sum * mlp_gate * (1.0 - mlp_gate), 0.0)
    mlp_token_grad = place_values(mlp_logit_grad, mlp_hot)
    normed_two_grad = normed_two_grad + mlp_token_grad[..., None] * routers[:, 2]
    router_mlp_grad = jnp.einsum("st,std->d", mlp_token_grad, normed_two, precision=TOP_PRECISION)
    gain_mlp_grad = jnp.sum(normed_two_grad * middle * factor_two, axis=(0, 1))
    middle_grad = upstream + norm_back(middle, factor_two, gains[:, 1], normed_two_grad)
    attn_low = middle_grad.astype(jnp.bfloat16)
    light_out_grad = jnp.einsum(
        "std,stc->dc", attn_low, light_blended_rows, preferred_element_type=jnp.float32
    )
    mix_grad = jnp.einsum(
        "std,dc->stc", attn_low, light_attention_output_weight, preferred_element_type=jnp.float32
    ).astype(jnp.bfloat16)
    mix_grad = mix_grad.reshape(seq_count, blocks, WIN, light_heads, LHD)
    probs_light = jnp.exp(light_scores - light_lse)
    light_prob_grad = jnp.einsum(
        "sbihd,sbjhd->sbhij", mix_grad, value_tiles, preferred_element_type=jnp.float32
    )
    light_delta = jnp.sum(probs_light * light_prob_grad, axis=-1, keepdims=True)
    light_score_grad = (probs_light * (light_prob_grad - light_delta)).astype(jnp.bfloat16)
    light_query_grad = (
        jnp.einsum(
            "sbhij,sbjhd->sbihd", light_score_grad, key_tiles, preferred_element_type=jnp.float32
        )
        * light_scale
    )
    light_query_grad = light_query_grad.reshape(seq_count, local_len, light_cols)
    light_key_win = (
        jnp.einsum(
            "sbhij,sbihd->sbjhd", light_score_grad, query_tiles, preferred_element_type=jnp.float32
        )
        * light_scale
    )
    light_value_win = jnp.einsum(
        "sbhij,sbihd->sbjhd",
        probs_light.astype(jnp.bfloat16),
        mix_grad,
        preferred_element_type=jnp.float32,
    )
    pair_win = jnp.stack(
        [
            light_key_win.reshape(seq_count, blocks, 3 * WIN, light_cols),
            light_value_win.reshape(seq_count, blocks, 3 * WIN, light_cols),
        ],
        axis=3,
    )
    pair_rows = unwindows(pair_win, WIN)
    rim_rows = jnp.concatenate([pair_rows[:, :WIN], pair_rows[:, local_len + WIN :]], axis=1)
    rim_back = padded(rim_rows.astype(jnp.bfloat16), (("seq", 1),), WIN).astype(rim_rows.dtype)
    pair_grad = pair_rows[:, WIN : WIN + local_len]
    pair_grad = pair_grad.at[:, :WIN].add(rim_back[:, :WIN])
    pair_grad = pair_grad.at[:, local_len - WIN :].add(rim_back[:, 3 * WIN :])
    light_grad = jnp.concatenate(
        [light_query_grad.astype(jnp.bfloat16)[:, :, None], pair_grad.astype(jnp.bfloat16)], axis=2
    )
    light_qkv_grad = jnp.einsum(
        "std,stjc->djc", normalized_lower_precision, light_grad, preferred_element_type=jnp.float32
    )
    input_low_grad = jnp.einsum(
        "stjc,djc->std",
        light_grad,
        light_query_key_value_weight,
        preferred_element_type=jnp.float32,
    )
    attn_upstream = pick_rows(attn_low, query_hot).astype(jnp.float32)
    slot_attn_grad = (query_weight[..., None] * attn_upstream).astype(jnp.bfloat16)
    query_gate_grad = jnp.sum(attn_upstream * heavy_rows, axis=-1)
    heavy_out_grad = jnp.einsum(
        "scd,sck->dk", slot_attn_grad, heavy_mix, preferred_element_type=jnp.float32
    )
    heavy_mix_grad = jnp.einsum(
        "scd,dk->sck", slot_attn_grad, heavy_out, preferred_element_type=jnp.float32
    ).astype(jnp.bfloat16)
    pair_grad_in = across(to_pairs([heavy_mix_grad]))
    pair_grad_in = jnp.pad(pair_grad_in, ((0, 0), (0, 0), (0, HHD)))
    pair_both_grad, pair_value_grad = heavy_backward(
        pair_both, pair_extra, pair_kept, pair_grad_in, heavy_scale
    )
    triple = back(
        jnp.concatenate([pair_both_grad, pair_value_grad[:, :, :HHD]], axis=-1)
    ).reshape(seq_count, heavy_heads, capacity, 3, HHD)
    triple = triple.transpose(3, 0, 2, 1, 4).reshape(3, seq_count, capacity, heavy_cols)
    query_grad, key_grad, value_grad = triple[0], triple[1], triple[2]
    key_grad_low = key_grad.astype(jnp.bfloat16)
    value_grad_low = value_grad.astype(jnp.bfloat16).astype(jnp.float32)
    raw_grad = (key_gate[..., None] * value_grad_low).astype(jnp.bfloat16)
    key_gate_grad = jnp.sum(value_grad_low * raw_value, axis=-1)
    key_pair_grad = jnp.stack([key_grad_low, raw_grad], axis=2)
    heavy_qkv_grad = jnp.concatenate(
        [
            jnp.einsum("scd,sck->dk", query_in, query_grad, preferred_element_type=jnp.float32)[
                :, None
            ],
            jnp.einsum("scd,scjk->djk", key_in, key_pair_grad, preferred_element_type=jnp.float32),
        ],
        axis=1,
    )
    input_low_grad = add_rows(
        input_low_grad,
        query_hot,
        jnp.einsum("sck,dk->scd", query_grad, heavy_qkv[:, 0], preferred_element_type=jnp.float32),
    )
    input_low_grad = add_rows(
        input_low_grad,
        key_hot,
        jnp.einsum(
            "scjk,djk->scd", key_pair_grad, heavy_qkv[:, 1:], preferred_element_type=jnp.float32
        ),
    )
    normed_grad, query_gate_sum, key_gate_sum = (
        core_sum(input_low_grad),
        core_sum(query_gate_grad),
        core_sum(key_gate_grad),
    )
    query_logit_grad = jnp.where(valid_query, query_gate_sum * query_gate * (1.0 - query_gate), 0.0)
    key_logit_grad = jnp.where(valid_key, key_gate_sum * key_gate * (1.0 - key_gate), 0.0)
    token_logit_grad = jnp.stack(
        [place_values(query_logit_grad, query_hot), place_values(key_logit_grad, key_hot)], axis=0
    )
    normed_grad = (
        normed_grad
        + token_logit_grad[0][..., None] * routers[:, 0]
        + token_logit_grad[1][..., None] * routers[:, 1]
    )
    router_attn_grad = jnp.einsum(
        "kst,std->dk", token_logit_grad, normed, precision=TOP_PRECISION
    )
    gain_attn_grad = jnp.sum(normed_grad * inputs * factor_one, axis=(0, 1))
    input_grad = middle_grad + norm_back(inputs, factor_one, gains[:, 0], normed_grad)
    small_grads = jnp.concatenate(
        [gain_attn_grad[:, None], gain_mlp_grad[:, None], router_attn_grad, router_mlp_grad[:, None]],
        axis=1,
    )

    def summed(parts):
        widths = [math.prod(p.shape[1:]) for p in parts]
        joined = jnp.concatenate(
            [p.reshape(model_width, -1).astype(jnp.bfloat16) for p in parts], axis=1
        )
        total = lax.psum(joined, "seq").astype(jnp.float32)
        marks = [sum(widths[:i]) for i in range(len(widths) + 1)]
        return [
            total[:, marks[i] : marks[i + 1]].reshape(p.shape) for i, p in enumerate(parts)
        ]

    sum_light_in, sum_light_down = summed([light_mlp_in_grad, light_mlp_out_grad])
    sum_light_qkv, sum_heavy_qkv, sum_light_out, sum_heavy_out, sum_small = summed(
        [light_qkv_grad, heavy_qkv_grad, light_out_grad, heavy_out_grad, small_grads]
    )
    if gather_heavy:
        sum_heavy_in, sum_heavy_down = heavy_mlp_in_grad, heavy_mlp_out_grad
    else:
        sum_heavy_in, sum_heavy_down = summed([heavy_mlp_in_grad, heavy_mlp_out_grad])
    return (
        result,
        input_grad,
        sum_light_qkv,
        sum_light_out,
        sum_heavy_qkv,
        sum_heavy_out,
        sum_light_in,
        sum_light_down,
        sum_heavy_in,
        sum_heavy_down,
        sum_small[:, :2],
        sum_small[:, 2:],
    )


def solution(mesh):
    placed = (
        P(None, "seq", None),
        P(None, "seq", None),
        P(),
        P(),
        P(None, None, "mp"),
        P(None, "mp"),
        P(None, None, "mp"),
        P(None, "mp"),
        P(None, None, "mp"),
        P(None, "mp"),
        P(None, None, "mp"),
        P(None, "mp"),
        P(None, "seq"),
        P(None, "seq"),
        P(None, "seq"),
        P(None, "seq", None),
    )
    return jax.shard_map(
        shards,
        mesh=mesh,
        in_specs=placed,
        out_specs=(
            P(None, "seq", None),
            P(None, "seq", None),
            P(None, None, "mp"),
            P(None, "mp"),
            P(None, None, "mp"),
            P(None, "mp"),
            P(None, None, "mp"),
            P(None, "mp"),
            P(None, None, "mp"),
            P(None, "mp"),
            P(),
            P(),
        ),
        check_vma=False,
    )
```

```python
import math

import jax
import jax.numpy as jnp
from jax import lax
from jax.experimental import pallas as pl
from jax.experimental.pallas import tpu as pltpu
from jax.sharding import PartitionSpec as P

LHD = 96
HHD = 64
WIN = 128
LANES = 128

EPSILON = 1e-06
MASKED = -1e30
EXACT = lax.Precision.HIGHEST
LOW = jnp.bfloat16
WIDE = jnp.float32

ROW_QUERY, ROW_KEY, ROW_MLP, OK_QUERY, OK_KEY, OK_MLP = range(6)


def lanes_of(shape):
    return lax.broadcasted_iota(jnp.int32, shape, len(shape) - 1)


def dot(a, b):
    return jnp.dot(a, b, preferred_element_type=WIDE)


def rows_dot(a, b):
    return lax.dot_general(a, b, (((1,), (1,)), ((), ())), preferred_element_type=WIDE)


def cols_dot(a, b):
    return lax.dot_general(a, b, (((0,), (0,)), ((), ())), preferred_element_type=WIDE)


def rms_of(values):
    return lax.rsqrt(jnp.mean(values * values, axis=-1, keepdims=True) + EPSILON)


def column(values, index):
    return values[:, index : index + 1]


def columns(shape, *parts):
    lane = lanes_of(shape)
    out = jnp.zeros(shape, WIDE)
    for index, part in enumerate(parts):
        out = jnp.where(lane == index, part, out)
    return out


def hot_rows(slots, index, length):
    rows = column(slots, index)
    return (lanes_of((rows.shape[0], length)) == rows).astype(WIDE)


def place_rows(hot, values):
    high = values.astype(LOW)
    rest = (values - high.astype(WIDE)).astype(LOW)
    return cols_dot(hot, high) + cols_dot(hot, rest)


def exact_place(hot, values):
    return lax.dot_general(
        hot, values, (((0,), (0,)), ((), ())), precision=EXACT, preferred_element_type=WIDE
    )


def exact_pick(hot, values):
    return jnp.dot(hot, values, precision=EXACT, preferred_element_type=WIDE)


def row_dots(values, vector):
    return jnp.sum(values * vector, axis=-1, keepdims=True)


def norm_back(values, factor, weighted):
    inner = jnp.mean(weighted * values, axis=-1, keepdims=True)
    return factor * weighted - values * (factor * factor * factor) * inner


def gelu_parts(gate, up, hidden_grad):
    root = math.sqrt(2.0 / math.pi)
    cube = 0.044715 * root
    square = gate * gate
    bend = jnp.tanh(gate * (root + cube * square))
    half = 0.5 + 0.5 * bend
    value = gate * half
    slope = half + gate * (1.0 - bend * bend) * (0.5 * root + (1.5 * cube) * square)
    return value * up, slope * up * hidden_grad, value * hidden_grad


def merge_heads(ref, offset, heads):
    tiles = []
    for head in range(0, heads, 2):
        first = ref[head, :, offset : offset + LANES].astype(WIDE)
        second = ref[head + 1, :, offset : offset + LANES].astype(WIDE)
        lane = lanes_of(first.shape)
        tiles.append(jnp.where(lane < HHD, first, pltpu.roll(second, HHD, 1)))
    return jnp.concatenate(tiles, axis=1)


def merge_upper(ref, heads):
    tiles = []
    for head in range(0, heads, 2):
        first = ref[head, :, :LANES].astype(WIDE)
        second = ref[head + 1, :, :LANES].astype(WIDE)
        lane = lanes_of(first.shape)
        tiles.append(jnp.where(lane < HHD, pltpu.roll(first, HHD, 1), second))
    return jnp.concatenate(tiles, axis=1)


def head_low(values, head):
    tile = values[:, head // 2 * LANES : (head // 2 + 1) * LANES]
    return tile if head % 2 == 0 else pltpu.roll(tile, HHD, 1)


def head_high(values, head):
    tile = values[:, head // 2 * LANES : (head // 2 + 1) * LANES]
    return tile if head % 2 == 1 else pltpu.roll(tile, HHD, 1)


def spread_matrix(heads):
    row = lax.broadcasted_iota(jnp.int32, (heads * LHD, heads * LANES), 0)
    lane = lanes_of((heads * LHD, heads * LANES))
    inner = lane & (LANES - 1)
    hit = (row == (lane >> 7) * LHD + inner) & (inner < LHD)
    return hit.astype(WIDE).astype(LOW)


def params(mib=56):
    return pltpu.CompilerParams(vmem_limit_bytes=mib * 2**20)


def whole(array):
    zeros = (0,) * array.ndim
    return pl.BlockSpec(array.shape, lambda *_: zeros, pipeline_mode=pl.Buffered(1))


def each(array):
    rest = (0,) * (array.ndim - 1)
    return pl.BlockSpec((1,) + array.shape[1:], lambda s: (s,) + rest)


def like(shape, kind):
    return jax.ShapeDtypeStruct(shape, kind)


def front_kernel(
    tokens_ref, gains_ref, routers_ref, slots_ref, light_ref, heavy_ref,
    low_ref, qkv_ref, pair_ref, raw_ref, gate_ref,
):
    inputs = tokens_ref[0].astype(WIDE)
    length = inputs.shape[0]
    normed = inputs * rms_of(inputs) * gains_ref[0:1, :]
    low = normed.astype(LOW)
    low_ref[0] = low
    slots = slots_ref[0]
    hot_query = hot_rows(slots, ROW_QUERY, length)
    hot_key = hot_rows(slots, ROW_KEY, length)
    logits = columns(
        (length, LANES),
        row_dots(normed, routers_ref[0:1, :]),
        row_dots(normed, routers_ref[1:2, :]),
    )
    query_gate = jax.nn.sigmoid(column(exact_pick(hot_query, logits), 0))
    key_gate = jax.nn.sigmoid(column(exact_pick(hot_key, logits), 1))
    gate_ref[0] = columns((slots.shape[0], LANES), query_gate, key_gate)
    query_in = dot(hot_query.astype(LOW), low).astype(LOW)
    key_in = dot(hot_key.astype(LOW), low).astype(LOW)
    query = dot(query_in, heavy_ref[0]).astype(LOW).astype(WIDE)
    key = dot(key_in, heavy_ref[1]).astype(LOW).astype(WIDE)
    raw = dot(key_in, heavy_ref[2])
    raw_ref[0] = raw
    value = (key_gate * raw).astype(LOW).astype(WIDE)
    bias = jnp.where(column(slots, OK_KEY) > 0, 0.0, MASKED)
    lane = lanes_of((slots.shape[0], LANES))
    for head in range(raw.shape[1] // HHD):
        both = jnp.where(lane < HHD, head_low(query, head), head_high(key, head))
        extra = jnp.where(lane < HHD, head_low(value, head), bias)
        pair_ref[head, :, :LANES] = both.astype(LOW)
        pair_ref[head, :, LANES:] = extra.astype(LOW)
    for kind in range(3):
        qkv_ref[0, kind] = dot(low, light_ref[kind]).astype(LOW)


def front(tokens, gains, routers, slots, light, heavy, seq_devices):
    seqs, length, width = tokens.shape
    cap = slots.shape[1]
    light_cols, heavy_cols = light.shape[2], heavy.shape[2]
    heads = heavy_cols // HHD
    shapes = [
        like(tokens.shape, LOW),
        like((seqs, 3, length, light_cols), LOW),
        like((seq_devices, cap, 2 * LANES), LOW),
        like((seqs, cap, heavy_cols), WIDE),
        like((seqs, cap, LANES), WIDE),
    ]
    specs = [each(s) for s in shapes]
    specs[2] = pl.BlockSpec((heads, cap, 2 * LANES), lambda s: (s, 0, 0))
    return pl.pallas_call(
        front_kernel,
        grid=(seqs,),
        in_specs=[each(tokens), whole(gains), whole(routers), each(slots), whole(light), whole(heavy)],
        out_specs=specs,
        out_shape=shapes,
        compiler_params=params(),
        name="front",
    )(tokens, gains, routers, slots, light, heavy)


def window_bias(block, length, base, total):
    row = lax.broadcasted_iota(jnp.int32, (WIN, 3 * WIN), 0)
    col = lanes_of((WIN, 3 * WIN))
    place = base + (block - 1) * WIN + col
    near = jnp.abs(col - WIN - row) < WIN
    return jnp.where(near & (place >= 0) & (place < total), 0.0, MASKED)


def light_forward_kernel(
    scale, place_ref, qkv_ref, before_ref, after_ref, gains_ref, weight_ref, out_ref,
    mix_ref, attn_ref, lse_ref, query_ref, window_ref, wide_ref,
):
    length, light_cols = qkv_ref.shape[2:]
    heads = light_cols // LHD
    spread = spread_matrix(heads)
    query_ref[0] = dot(qkv_ref[0, 0], spread).astype(LOW)
    edges = ((before_ref, slice(0, WIN)), (after_ref, slice(WIN + length, 2 * WIN + length)))
    for ref, rows in edges:
        inputs = ref[0].astype(WIDE)
        low = (inputs * rms_of(inputs) * gains_ref[0:1, :]).astype(LOW)
        for kind in range(2):
            edge = dot(low, weight_ref[1 + kind]).astype(LOW)
            window_ref[0, kind, rows, :] = dot(edge, spread).astype(LOW)
    for kind in range(2):
        window_ref[0, kind, WIN : WIN + length, :] = dot(qkv_ref[0, 1 + kind], spread).astype(LOW)
    for block in range(length // WIN):
        rows = slice(block * WIN, (block + 1) * WIN)
        near = slice(block * WIN, (block + 3) * WIN)
        bias = window_bias(block, length, place_ref[0, 0], place_ref[0, 1])
        kept = []
        for head in range(heads):
            lanes = slice(head * LANES, (head + 1) * LANES)
            scores = rows_dot(query_ref[0, rows, lanes], window_ref[0, 0, near, lanes]) * scale + bias
            top = jnp.max(scores, axis=-1, keepdims=True)
            expo = jnp.exp(scores - top)
            total = jnp.sum(expo, axis=-1, keepdims=True)
            mixed = dot(expo.astype(LOW), window_ref[0, 1, near, lanes]) / total
            wide_ref[rows, lanes] = mixed.astype(LOW)
            kept.append(top + jnp.log(total))
        lse_ref[0, rows, :] = columns((WIN, LANES), *kept)
    mix = rows_dot(wide_ref[...], spread).astype(LOW)
    mix_ref[0] = mix
    attn_ref[0] = rows_dot(mix, out_ref[...])


def light_forward(place, qkv, before, after, gains, weight, weight_out):
    seqs, _, length, light_cols = qkv.shape
    heads = light_cols // LHD
    shapes = [
        like((seqs, length, light_cols), LOW),
        like((seqs, length, weight_out.shape[0]), WIDE),
        like((seqs, length, LANES), WIDE),
        like((seqs, length, heads * LANES), LOW),
        like((seqs, 2, length + 2 * WIN, heads * LANES), LOW),
    ]
    return pl.pallas_call(
        lambda *refs: light_forward_kernel(1.0 / math.sqrt(LHD), *refs),
        grid=(seqs,),
        in_specs=[
            pl.BlockSpec(memory_space=pltpu.SMEM),
            each(qkv),
            each(before),
            each(after),
            whole(gains),
            whole(weight),
            whole(weight_out),
        ],
        out_specs=[each(s) for s in shapes],
        out_shape=shapes,
        scratch_shapes=[pltpu.VMEM((length, heads * LANES), LOW)],
        compiler_params=params(),
        name="light_forward",
    )(place, qkv, before, after, gains, weight, weight_out)


def light_backward_kernel(
    scale, place_ref, query_ref, window_ref, lse_ref, grad_ref, local_ref, early_ref, late_ref, *scratch
):
    wide_ref, dkey_ref, dvalue_ref = scratch
    length, light_cols = grad_ref.shape[1:]
    heads = light_cols // LHD
    spread = spread_matrix(heads)
    grad = dot(grad_ref[0], spread).astype(LOW)
    dkey_ref[...] = jnp.zeros_like(dkey_ref)
    dvalue_ref[...] = jnp.zeros_like(dvalue_ref)
    for block in range(length // WIN):
        rows = slice(block * WIN, (block + 1) * WIN)
        near = slice(block * WIN, (block + 3) * WIN)
        bias = window_bias(block, length, place_ref[0, 0], place_ref[0, 1])
        lse = lse_ref[0, rows, :]
        for head in range(heads):
            lanes = slice(head * LANES, (head + 1) * LANES)
            key = window_ref[0, 0, near, lanes]
            part = grad[rows, lanes]
            mine = query_ref[0, rows, lanes]
            probs = jnp.exp(rows_dot(mine, key) * scale + bias - column(lse, head))
            prob_grad = rows_dot(part, window_ref[0, 1, near, lanes])
            delta = jnp.sum(probs * prob_grad, axis=-1, keepdims=True)
            score_grad = (probs * (prob_grad - delta)).astype(LOW)
            wide_ref[rows, lanes] = (dot(score_grad, key) * scale).astype(LOW)
            dkey_ref[near, lanes] += cols_dot(score_grad, mine) * scale
            dvalue_ref[near, lanes] += cols_dot(probs.astype(LOW), part)
    local_ref[0, 0] = rows_dot(wide_ref[...], spread).astype(LOW)
    for kind, ref in ((1, dkey_ref), (2, dvalue_ref)):
        all_rows = rows_dot(ref[...].astype(LOW), spread).astype(LOW)
        early_ref[0, kind - 1] = all_rows[:WIN]
        local_ref[0, kind] = all_rows[WIN : WIN + length]
        late_ref[0, kind - 1] = all_rows[WIN + length :]


def light_backward(place, query, window, lse, grad):
    seqs, length, light_cols = grad.shape
    edge = like((seqs, 2, WIN, light_cols), LOW)
    shapes = [like((seqs, 3, length, light_cols), LOW), edge, edge]
    return pl.pallas_call(
        lambda *refs: light_backward_kernel(1.0 / math.sqrt(LHD), *refs),
        grid=(seqs,),
        in_specs=[
            pl.BlockSpec(memory_space=pltpu.SMEM),
            each(query),
            each(window),
            each(lse),
            each(grad),
        ],
        out_specs=[each(s) for s in shapes],
        out_shape=shapes,
        scratch_shapes=[
            pltpu.VMEM(query.shape[1:], LOW),
            pltpu.VMEM(window.shape[2:], WIDE),
            pltpu.VMEM(window.shape[2:], WIDE),
        ],
        compiler_params=params(),
        name="light_backward",
    )(place, query, window, lse, grad)


def key_operand(pair, extra):
    lane = lanes_of(pair.shape)
    moved = pltpu.roll(pair.astype(WIDE), HHD, 1)
    bias = column(extra, HHD).astype(WIDE)
    return jnp.where(lane < HHD, moved, jnp.where(lane == HHD, bias, 0.0)).astype(LOW)


def query_operand(pair, scale):
    lane = lanes_of(pair.shape)
    scaled = pair.astype(WIDE) * scale
    return jnp.where(lane < HHD, scaled, jnp.where(lane == HHD, 1.0, 0.0)).astype(LOW)


def heavy_forward_kernel(tile, scale, pair_ref, kept_ref, mix_ref, key_ref):
    @pl.when(pl.program_id(0) == 0)
    def _():
        key_ref[...] = key_operand(pair_ref[:, :LANES], pair_ref[:, LANES:])

    start = pl.multiple_of(pl.program_id(0) * tile, tile)
    query = query_operand(pair_ref[pl.ds(start, tile), :LANES], scale)
    scores = rows_dot(query, key_ref[...])
    top = jnp.max(scores, axis=-1, keepdims=True)
    expo = jnp.exp(scores - top)
    total = jnp.sum(expo, axis=-1, keepdims=True)
    mix = dot(expo.astype(LOW), pair_ref[:, LANES:]) / total
    lane = lanes_of(mix.shape)
    kept_ref[...] = jnp.where(lane < HHD, mix, top + jnp.log(total))
    mix_ref[...] = jnp.where(lane < HHD, mix, 0.0).astype(LOW)


def heavy_backward_kernel(
    tile, scale, pair_ref, kept_ref, grad_ref, both_ref, key_ref, dk_ref, dv_ref
):
    step = pl.program_id(0)

    @pl.when(step == 0)
    def _():
        key_ref[...] = key_operand(pair_ref[:, :LANES], pair_ref[:, LANES:])
        dk_ref[...] = jnp.zeros_like(dk_ref)
        dv_ref[...] = jnp.zeros_like(dv_ref)

    start = pl.multiple_of(step * tile, tile)
    query = query_operand(pair_ref[pl.ds(start, tile), :LANES], scale)
    lane = lanes_of(query.shape)
    kept = kept_ref[...]
    grad = grad_ref[...]
    lse = column(kept, HHD)
    delta = jnp.sum(
        jnp.where(lane < HHD, kept * grad.astype(WIDE), 0.0), axis=-1, keepdims=True
    )
    probs = jnp.exp(rows_dot(query, key_ref[...]) - lse)
    prob_grad = rows_dot(grad, pair_ref[:, LANES:])
    score_grad = (probs * (prob_grad - delta)).astype(LOW)
    query_grad = dot(score_grad, key_ref[...]) * scale
    both_ref[pl.ds(start, tile), :LANES] = jnp.where(lane < HHD, query_grad, 0.0).astype(LOW)
    dk_ref[...] += cols_dot(score_grad, query)
    dv_ref[...] += cols_dot(probs.astype(LOW), grad)

    @pl.when(step == pl.num_programs(0) - 1)
    def _():
        spot = lanes_of(dk_ref.shape)
        moved = pltpu.roll(dk_ref[...], HHD, 1)
        query_part = both_ref[:, :LANES].astype(WIDE)
        both_ref[:, :LANES] = jnp.where(spot < HHD, query_part, moved).astype(LOW)
        both_ref[:, LANES:] = dv_ref[...].astype(LOW)


def query_tile(length):
    return 256 if length % 256 == 0 else length


def heavy_forward(pair):
    length = pair.shape[0]
    tile = query_tile(length)
    rows = pl.BlockSpec((tile, LANES), lambda i: (i, 0))
    return pl.pallas_call(
        lambda *refs: heavy_forward_kernel(tile, 1.0 / math.sqrt(HHD), *refs),
        grid=(length // tile,),
        in_specs=[whole(pair)],
        out_specs=[rows, rows],
        out_shape=[like((length, LANES), WIDE), like((length, LANES), LOW)],
        scratch_shapes=[pltpu.VMEM((length, LANES), LOW)],
        compiler_params=params(60),
        name="heavy_forward",
    )(pair)


def heavy_backward(pair, kept, grad):
    length = pair.shape[0]
    tile = query_tile(length)
    rows = pl.BlockSpec((tile, LANES), lambda i: (i, 0))
    return pl.pallas_call(
        lambda *refs: heavy_backward_kernel(tile, 1.0 / math.sqrt(HHD), *refs),
        grid=(length // tile,),
        in_specs=[whole(pair), rows, rows],
        out_specs=whole(pair),
        out_shape=like(pair.shape, LOW),
        scratch_shapes=[
            pltpu.VMEM((length, LANES), LOW),
            pltpu.VMEM((length, LANES), WIDE),
            pltpu.VMEM((length, LANES), WIDE),
        ],
        compiler_params=params(60),
        name="heavy_backward",
    )(pair, kept, grad)


def combine_kernel(pairs_ref, attn_ref, out_ref, slots_ref, gate_ref, part_ref, mix_ref):
    slots = slots_ref[0]
    mix = merge_heads(pairs_ref, 0, pairs_ref.shape[0]).astype(LOW)
    mix_ref[0] = mix
    rows = rows_dot(mix, out_ref[...])
    weight = jnp.where(column(slots, OK_QUERY) > 0, column(gate_ref[0], 0), 0.0)
    hot = hot_rows(slots, ROW_QUERY, attn_ref.shape[1]).astype(LOW)
    part_ref[0] = (attn_ref[0] + place_rows(hot, weight * rows)).astype(LOW)


def pair_spec(pairs, heads):
    return pl.BlockSpec((heads,) + pairs.shape[1:], lambda s: (s, 0, 0))


def combine(pairs, attn, weight_out, slots, gate):
    seqs, cap = slots.shape[:2]
    heavy_cols = weight_out.shape[1]
    shapes = [like(attn.shape, LOW), like((seqs, cap, heavy_cols), LOW)]
    return pl.pallas_call(
        combine_kernel,
        grid=(seqs,),
        in_specs=[
            pair_spec(pairs, heavy_cols // HHD),
            each(attn),
            whole(weight_out),
            each(slots),
            each(gate),
        ],
        out_specs=[each(s) for s in shapes],
        out_shape=shapes,
        compiler_params=params(),
        name="combine",
    )(pairs, attn, weight_out, slots, gate)


def slots_kernel(
    core_ref, tokens_ref, own_ref, other_ref, up_ref, gains_ref, routers_ref, slots_ref,
    low_ref, rows_ref, slot_ref, ship_ref, gate_ref,
):
    middle = tokens_ref[0].astype(WIDE) + own_ref[0].astype(WIDE) + other_ref[0].astype(WIDE)
    length = middle.shape[0]
    normed = middle * rms_of(middle) * gains_ref[1:2, :]
    low = normed.astype(LOW)
    low_ref[0] = low
    slots = slots_ref[0]
    hot = hot_rows(slots, ROW_MLP, length)
    logits = columns((length, LANES), row_dots(normed, routers_ref[2:3, :]))
    gate = jax.nn.sigmoid(column(exact_pick(hot, logits), 0))
    weight = jnp.where(column(slots, OK_MLP) > 0, gate, 0.0)
    hot = hot.astype(LOW)
    rows = dot(hot, low)
    slot = weight * dot(hot, up_ref[0])
    rows_ref[0] = rows.astype(LOW)
    slot_ref[0] = slot.astype(LOW)
    ship_ref[0] = jnp.where(core_ref[0, 0] == 0, rows, slot).astype(LOW)
    gate_ref[0] = columns((slots.shape[0], LANES), gate, weight)


def mlp_slots(core, tokens, own, other, up, gains, routers, slots):
    seqs, length, width = tokens.shape
    cap = slots.shape[1]
    shapes = [like(tokens.shape, LOW)]
    shapes += [like((seqs, cap, width), LOW)] * 3 + [like((seqs, cap, LANES), WIDE)]
    return pl.pallas_call(
        slots_kernel,
        grid=(seqs,),
        in_specs=[
            pl.BlockSpec(memory_space=pltpu.SMEM),
            each(tokens), each(own), each(other), each(up), whole(gains), whole(routers), each(slots),
        ],
        out_specs=[each(s) for s in shapes],
        out_shape=shapes,
        compiler_params=params(),
        name="mlp_slots",
    )(core, tokens, own, other, up, gains, routers, slots)


def feed_kernel(
    low_ref, rows_ref, slot_ref, kept_ref, up_ref, slots_ref, in_ref, out_ref, heavy_in_ref,
    heavy_out_ref, part_ref, weights_ref, gate_ref, heavy_acc, back_acc, hidden_ref, dgate_ref, dup_ref,
):
    step = pl.program_id(0)
    seqs, length, width = up_ref.shape
    cap = slots_ref.shape[1]

    @pl.when(step == 0)
    def _():
        heavy_acc[...] = jnp.zeros_like(heavy_acc)
        back_acc[...] = jnp.zeros_like(back_acc)

    first, second, last = heavy_in_ref[0], heavy_in_ref[1], heavy_out_ref[...]
    rows = rows_ref[...]
    hidden, gate_grad, up_grad = gelu_parts(
        dot(rows, first), dot(rows, second), dot(slot_ref[...], last)
    )
    heavy_acc[...] += rows_dot(hidden.astype(LOW), last)
    back_acc[...] += rows_dot(gate_grad.astype(LOW), first) + rows_dot(up_grad.astype(LOW), second)

    @pl.when(step == pl.num_programs(0) - 1)
    def _():
        for s in range(seqs):
            here = slice(s * length, (s + 1) * length)
            mine = slice(s * cap, (s + 1) * cap)
            low = low_ref[s]
            hidden, gate_grad, up_grad = gelu_parts(
                dot(low, in_ref[0]), dot(low, in_ref[1]), dot(up_ref[s], out_ref[...])
            )
            hidden, gate_grad, up_grad = (
                hidden.astype(LOW),
                gate_grad.astype(LOW),
                up_grad.astype(LOW),
            )
            hidden_ref[here, :] = hidden
            dgate_ref[here, :] = gate_grad
            dup_ref[here, :] = up_grad
            hot = hot_rows(slots_ref[s], ROW_MLP, length).astype(LOW)
            kept = kept_ref[s]
            heavy_rows = heavy_acc[mine, :]
            part_ref[0, s] = (
                rows_dot(hidden, out_ref[...]) + place_rows(hot, column(kept, 1) * heavy_rows)
            ).astype(LOW)
            part_ref[1, s] = (
                rows_dot(gate_grad, in_ref[0])
                + rows_dot(up_grad, in_ref[1])
                + place_rows(hot, back_acc[mine, :])
            ).astype(LOW)
            gate_part = jnp.sum(dot(hot, up_ref[s]) * heavy_rows, axis=-1, keepdims=True)
            gate_ref[s] = columns((cap, LANES), column(kept, 0), gate_part)
        low = low_ref[...].reshape(seqs * length, width)
        up = up_ref[...].reshape(seqs * length, width)
        weights_ref[0] = cols_dot(low, dgate_ref[...]).astype(LOW)
        weights_ref[1] = cols_dot(low, dup_ref[...]).astype(LOW)
        weights_ref[2] = cols_dot(up, hidden_ref[...]).astype(LOW)


def feed(low, rows, slot, kept, up, slots, light_in, light_out, heavy_in, heavy_out):
    seqs, length, width = up.shape
    cap = slots.shape[1]
    hidden = light_out.shape[1]
    cols = 256
    rows, slot = rows.reshape(-1, width), slot.reshape(-1, width)
    shapes = [
        like((2, seqs, length, width), LOW),
        like((3, width, hidden), LOW),
        like((seqs, cap, LANES), WIDE),
    ]
    return pl.pallas_call(
        feed_kernel,
        grid=(heavy_out.shape[1] // cols,),
        in_specs=[
            whole(low),
            whole(rows),
            whole(slot),
            whole(kept),
            whole(up),
            whole(slots),
            whole(light_in),
            whole(light_out),
            pl.BlockSpec((2, width, cols), lambda i: (0, 0, i)),
            pl.BlockSpec((width, cols), lambda i: (0, i)),
        ],
        out_specs=[whole(s) for s in shapes],
        out_shape=shapes,
        scratch_shapes=[pltpu.VMEM((seqs * cap, width), WIDE)] * 2
        + [pltpu.VMEM((seqs * length, hidden), LOW)] * 3,
        compiler_params=params(),
        name="feed",
    )(low, rows, slot, kept, up, slots, light_in, light_out, heavy_in, heavy_out)


def middle_kernel(
    tokens_ref, own_ref, other_ref, part_ref, beyond_ref, up_ref, gains_ref, routers_ref, slots_ref,
    gate_ref, mlp_ref, mlp_other_ref, mix_ref, heavy_mix_ref, light_out_ref, heavy_out_ref,
    mixed_ref, middle_ref, grad_ref, pair_ref, weights_ref, small_ref, logit_ref, weights_acc,
):
    step = pl.program_id(0)

    @pl.when(step == 0)
    def _():
        weights_acc[...] = jnp.zeros_like(weights_acc)
        small_ref[...] = jnp.zeros_like(small_ref)

    slots = slots_ref[0]
    cap = slots.shape[0]
    middle = tokens_ref[0].astype(WIDE) + own_ref[0].astype(WIDE) + other_ref[0].astype(WIDE)
    length = middle.shape[0]
    factor = rms_of(middle)
    scaled = middle * factor
    normed = scaled * gains_ref[1:2, :]
    mixed = middle + (part_ref[0, 0].astype(WIDE) + beyond_ref[0, 0].astype(WIDE))
    mixed_ref[0] = mixed.astype(LOW)
    gate = column(mlp_ref[0], 0)
    gate_grad = column(mlp_ref[0], 1) + column(mlp_other_ref[0], 1)
    logit_grad = jnp.where(column(slots, OK_MLP) > 0, gate_grad * gate * (1.0 - gate), 0.0)
    token_grad = column(
        exact_place(hot_rows(slots, ROW_MLP, length), columns((cap, LANES), logit_grad)), 0
    )
    normed_grad = (
        part_ref[1, 0].astype(WIDE) + beyond_ref[1, 0].astype(WIDE)
    ) + token_grad * routers_ref[2:3, :]
    small_ref[0:1, :] += jnp.sum(normed_grad * scaled, axis=0, keepdims=True)
    small_ref[1:2, :] += jnp.sum(token_grad * normed, axis=0, keepdims=True)
    middle_grad = up_ref[0].astype(WIDE) + norm_back(middle, factor, normed_grad * gains_ref[1:2, :])
    middle_ref[0] = middle_grad
    low = middle_grad.astype(LOW)
    hot = hot_rows(slots, ROW_QUERY, length).astype(LOW)
    up_rows = dot(hot, low)
    weight = jnp.where(column(slots, OK_QUERY) > 0, column(gate_ref[0], 0), 0.0)
    slot = (weight * up_rows).astype(LOW)
    heavy_rows = rows_dot(heavy_mix_ref[0], heavy_out_ref[...])
    logit_ref[0] = columns(
        (cap, LANES), jnp.sum(up_rows * heavy_rows, axis=-1, keepdims=True)
    )
    mix_grad = dot(slot, heavy_out_ref[...]).astype(LOW).astype(WIDE)
    lane = lanes_of((cap, LANES))
    for head in range(mix_grad.shape[1] // HHD):
        pair_ref[head] = jnp.where(lane < HHD, head_low(mix_grad, head), 0.0).astype(LOW)
    grad_ref[0] = dot(low, light_out_ref[...]).astype(LOW)
    weights_acc[0] += cols_dot(low, mix_ref[0])
    weights_acc[1] += cols_dot(slot, heavy_mix_ref[0])

    @pl.when(step == pl.num_programs(0) - 1)
    def _():
        weights_ref[...] = weights_acc[...].astype(LOW)


def middle_back(
    tokens, own, other, part, beyond, up, gains, routers, slots, gate, mlp, mlp_other,
    mix, heavy_mix, light_out, heavy_out, seq_devices,
):
    seqs, length, width = tokens.shape
    cap = slots.shape[1]
    cols = light_out.shape[1]
    heads = heavy_out.shape[1] // HHD
    shapes = [
        like(tokens.shape, LOW),
        like(tokens.shape, WIDE),
        like((seqs, length, cols), LOW),
        like((seq_devices, cap, LANES), LOW),
        like((2, width, cols), LOW),
        like((8, width), WIDE),
        like((seqs, cap, LANES), WIDE),
    ]
    specs = [
        each(shapes[0]), each(shapes[1]), each(shapes[2]), pair_spec(shapes[3], heads),
        whole(shapes[4]), whole(shapes[5]), each(shapes[6]),
    ]
    both = pl.BlockSpec((2, 1, length, width), lambda s: (0, s, 0, 0))
    return pl.pallas_call(
        middle_kernel,
        grid=(seqs,),
        in_specs=[
            each(tokens), each(own), each(other), both, both, each(up), whole(gains),
            whole(routers), each(slots), each(gate), each(mlp), each(mlp_other), each(mix),
            each(heavy_mix), whole(light_out), whole(heavy_out),
        ],
        out_specs=specs,
        out_shape=shapes,
        scratch_shapes=[pltpu.VMEM((2, width, cols), WIDE)],
        compiler_params=params(),
        name="middle_back",
    )(
        tokens, own, other, part, beyond, up, gains, routers, slots, gate, mlp, mlp_other,
        mix, heavy_mix, light_out, heavy_out,
    )


def light_project_kernel(
    local_ref, lead_ref, tail_ref, low_ref, light_ref, grad_ref, part_ref, grad_acc
):
    step = pl.program_id(0)

    @pl.when(step == 0)
    def _():
        grad_acc[...] = jnp.zeros_like(grad_acc)

    low = low_ref[0]
    length = low.shape[0]
    part = jnp.zeros((length, low.shape[1]), WIDE)
    for kind in range(3):
        rows = local_ref[0, kind]
        if kind > 0:
            lead = rows[:WIN].astype(WIDE) + lead_ref[0, kind - 1].astype(WIDE)
            tail = rows[length - WIN :].astype(WIDE) + tail_ref[0, kind - 1].astype(WIDE)
            rows = jnp.concatenate(
                [lead.astype(LOW), rows[WIN : length - WIN], tail.astype(LOW)], axis=0
            )
        grad_acc[kind] += cols_dot(low, rows)
        part = part + rows_dot(rows, light_ref[kind])
    part_ref[0] = part

    @pl.when(step == pl.num_programs(0) - 1)
    def _():
        grad_ref[...] = grad_acc[...].astype(LOW)


def light_project(local, lead, tail, low, light):
    shapes = [like(light.shape, LOW), like(low.shape, WIDE)]
    return pl.pallas_call(
        light_project_kernel,
        grid=(low.shape[0],),
        in_specs=[each(local), each(lead), each(tail), each(low), whole(light)],
        out_specs=[whole(shapes[0]), each(shapes[1])],
        out_shape=shapes,
        scratch_shapes=[pltpu.VMEM(light.shape, WIDE)],
        compiler_params=params(),
        name="light_project",
    )(local, lead, tail, low, light)


def heavy_project_kernel(
    light_part_ref, low_ref, pairs_ref, heavy_ref, slots_ref, gate_ref, raw_ref, logit_ref,
    grad_ref, part_ref, both_logit_ref, grad_acc,
):
    step = pl.program_id(0)

    @pl.when(step == 0)
    def _():
        grad_acc[...] = jnp.zeros_like(grad_acc)

    low = low_ref[0]
    length = low.shape[0]
    slots = slots_ref[0]
    cap = slots.shape[0]
    heads = raw_ref.shape[2] // HHD
    key_gate = column(gate_ref[0], 1)
    query_grad = merge_heads(pairs_ref, 0, heads).astype(LOW)
    key_grad = merge_upper(pairs_ref, heads).astype(LOW)
    value_grad = merge_heads(pairs_ref, LANES, heads)
    raw_grad = (key_gate * value_grad).astype(LOW)
    key_logit = jnp.sum(value_grad * raw_ref[0], axis=-1, keepdims=True)
    both_logit_ref[0] = columns((cap, LANES), column(logit_ref[0], 0), key_logit)
    hot_query = hot_rows(slots, ROW_QUERY, length).astype(LOW)
    hot_key = hot_rows(slots, ROW_KEY, length).astype(LOW)
    query_in = dot(hot_query, low).astype(LOW)
    key_in = dot(hot_key, low).astype(LOW)
    grad_acc[0] += cols_dot(query_in, query_grad)
    grad_acc[1] += cols_dot(key_in, key_grad)
    grad_acc[2] += cols_dot(key_in, raw_grad)
    part = light_part_ref[0] + place_rows(hot_query, rows_dot(query_grad, heavy_ref[0]))
    part = part + place_rows(
        hot_key, rows_dot(key_grad, heavy_ref[1]) + rows_dot(raw_grad, heavy_ref[2])
    )
    part_ref[0] = part.astype(LOW)

    @pl.when(step == pl.num_programs(0) - 1)
    def _():
        grad_ref[...] = grad_acc[...].astype(LOW)


def heavy_project(light_part, low, pairs, heavy, slots, gate, raw, logit):
    heads = heavy.shape[2] // HHD
    shapes = [like(heavy.shape, LOW), like(low.shape, LOW), like(logit.shape, WIDE)]
    return pl.pallas_call(
        heavy_project_kernel,
        grid=(low.shape[0],),
        in_specs=[
            each(light_part), each(low), pair_spec(pairs, heads), whole(heavy), each(slots),
            each(gate), each(raw), each(logit),
        ],
        out_specs=[whole(shapes[0]), each(shapes[1]), each(shapes[2])],
        out_shape=shapes,
        scratch_shapes=[pltpu.VMEM(heavy.shape, WIDE)],
        compiler_params=params(),
        name="heavy_project",
    )(light_part, low, pairs, heavy, slots, gate, raw, logit)


def input_kernel(
    part_ref, other_ref, logit_ref, logit_other_ref, gate_ref, slots_ref, tokens_ref, gains_ref,
    routers_ref, middle_ref, small_in_ref, grad_ref, small_ref,
):
    @pl.when(pl.program_id(0) == 0)
    def _():
        small_ref[...] = small_in_ref[...]

    slots = slots_ref[0]
    cap = slots.shape[0]
    inputs = tokens_ref[0].astype(WIDE)
    length = inputs.shape[0]
    factor = rms_of(inputs)
    scaled = inputs * factor
    normed = scaled * gains_ref[0:1, :]
    gates = gate_ref[0]
    grads = (logit_ref[0] + logit_other_ref[0]) * gates * (1.0 - gates)
    query_logit = jnp.where(column(slots, OK_QUERY) > 0, column(grads, 0), 0.0)
    key_logit = jnp.where(column(slots, OK_KEY) > 0, column(grads, 1), 0.0)
    query_token = column(
        exact_place(hot_rows(slots, ROW_QUERY, length), columns((cap, LANES), query_logit)), 0
    )
    key_token = column(
        exact_place(hot_rows(slots, ROW_KEY, length), columns((cap, LANES), key_logit)), 0
    )
    normed_grad = (
        (part_ref[0].astype(WIDE) + other_ref[0].astype(WIDE))
        + query_token * routers_ref[0:1, :]
        + key_token * routers_ref[1:2, :]
    )
    small_ref[2:3, :] += jnp.sum(normed_grad * scaled, axis=0, keepdims=True)
    small_ref[3:4, :] += jnp.sum(query_token * normed, axis=0, keepdims=True)
    small_ref[4:5, :] += jnp.sum(key_token * normed, axis=0, keepdims=True)
    grad_ref[0] = middle_ref[0] + norm_back(inputs, factor, normed_grad * gains_ref[0:1, :])


def input_back(part, other, logit, logit_other, gate, slots, tokens, gains, routers, middle, small):
    shapes = [like(middle.shape, WIDE), like(small.shape, WIDE)]
    return pl.pallas_call(
        input_kernel,
        grid=(tokens.shape[0],),
        in_specs=[
            each(part), each(other), each(logit), each(logit_other), each(gate), each(slots),
            each(tokens), whole(gains), whole(routers), each(middle), whole(small),
        ],
        out_specs=[each(shapes[0]), whole(shapes[1])],
        out_shape=shapes,
        compiler_params=params(),
        name="input_back",
    )(part, other, logit, logit_other, gate, slots, tokens, gains, routers, middle, small)


def heavy_weights_kernel(tile, core_ref, here_ref, there_ref, in_ref, out_ref, *refs):
    din_ref, dout_ref, rows_ref, grad_ref, hidden_ref, gate_ref, up_ref, sems = refs[-8:]

    starts = range(0, rows_ref.shape[0], tile)
    first = pl.program_id(0) == 0

    def copies(rows_from, grad_from, index):
        part = pl.ds(index * tile, tile)
        return [
            pltpu.make_async_copy(rows_from.at[part, :], rows_ref.at[part, :], sems.at[0, index]),
            pltpu.make_async_copy(grad_from.at[part, :], grad_ref.at[part, :], sems.at[1, index]),
        ]

    def fetch(rows_from, grad_from):
        for index in range(len(starts)):
            for copy in copies(rows_from, grad_from, index):
                copy.start()

    @pl.when(first & (core_ref[0, 0] == 0))
    def _():
        fetch(here_ref, there_ref)

    @pl.when(first & (core_ref[0, 0] != 0))
    def _():
        fetch(there_ref, here_ref)

    for index, start in enumerate(starts):

        @pl.when(first)
        def _():
            for copy in copies(here_ref, there_ref, index):
                copy.wait()

        part = pl.ds(start, tile)
        rows = rows_ref[part, :]
        hidden, gate_grad, up_grad = gelu_parts(
            dot(rows, in_ref[0]), dot(rows, in_ref[1]), dot(grad_ref[part, :], out_ref[...])
        )
        hidden_ref[part, :] = hidden.astype(LOW)
        gate_ref[part, :] = gate_grad.astype(LOW)
        up_ref[part, :] = up_grad.astype(LOW)
    dout_ref[...] = cols_dot(grad_ref[...], hidden_ref[...])
    din_ref[:, 0, :] = cols_dot(rows_ref[...], gate_ref[...])
    din_ref[:, 1, :] = cols_dot(rows_ref[...], up_ref[...])


def heavy_weights(core, here, there, weight_in, weight_out, piece, pieces, done):
    count, width = here.shape
    hidden = weight_out.shape[1]
    cols = 256
    tile = 512 if count % 512 == 0 else count
    steps = hidden // cols // pieces
    out_block = pl.BlockSpec((width, cols), lambda i: (0, piece * steps + i))
    in_block = pl.BlockSpec((width, 2, cols), lambda i: (0, 0, piece * steps + i))
    return pl.pallas_call(
        lambda *refs: heavy_weights_kernel(tile, *refs),
        grid=(steps,),
        in_specs=[
            pl.BlockSpec(memory_space=pltpu.SMEM),
            pl.BlockSpec(memory_space=pl.ANY),
            pl.BlockSpec(memory_space=pl.ANY),
            pl.BlockSpec((2, width, cols), lambda i: (0, 0, piece * steps + i)),
            out_block,
        ]
        + [pl.BlockSpec(memory_space=pl.ANY)] * len(done),
        out_specs=[in_block, out_block],
        out_shape=[like((width, 2, hidden), WIDE), like((width, hidden), WIDE)],
        scratch_shapes=[pltpu.VMEM((count, width), LOW)] * 2
        + [pltpu.VMEM((count, cols), LOW)] * 3
        + [pltpu.SemaphoreType.DMA((2, count // tile))],
        input_output_aliases={5 + i: i for i in range(len(done))},
        compiler_params=params(60),
        cost_estimate=pl.CostEstimate(
            flops=12 * count * width * hidden // pieces, bytes_accessed=2**24, transcendentals=0
        ),
        name="heavy_weights",
    )(core, here, there, weight_in, weight_out, *done)


def bit_pairs(bit):
    return [(i, i ^ (1 << bit)) for i in range(lax.axis_size("seq"))]


def bit_here(bit):
    return (lax.axis_index("seq") >> bit) & 1


def scatter_stage(value, bit):
    halves = value.reshape(2, value.shape[0] // 2, value.shape[1])
    mine = bit_here(bit)
    sent = lax.dynamic_index_in_dim(halves, 1 - mine, 0, keepdims=False)
    kept = lax.dynamic_index_in_dim(halves, mine, 0, keepdims=False)
    got = lax.ppermute(sent, "seq", bit_pairs(bit))
    return (kept.astype(WIDE) + got.astype(WIDE)).astype(LOW)


def gather_stage(value, bit):
    got = lax.ppermute(value, "seq", bit_pairs(bit))
    return jnp.where(
        bit_here(bit) == 0,
        jnp.concatenate([value, got], axis=0),
        jnp.concatenate([got, value], axis=0),
    )


def stage_orders():
    bits = list(range((lax.axis_size("seq") - 1).bit_length()))
    return [
        bits,
        [bits[1], bits[0]] + bits[2:],
        [bits[2], bits[0], bits[1]] + bits[3:],
    ]


def scatter_all(parts, step):
    return [scatter_stage(p, order[step]) for p, order in zip(parts, stage_orders())]


def gather_all(parts, step):
    return [gather_stage(p, order[step]) for p, order in zip(parts, stage_orders())]


def after(value, *others):
    return lax.optimization_barrier((value,) + others)[0]


def widen_kernel(bit_ref, mine_ref, got_ref, out_ref):
    half = mine_ref.shape[0]

    @pl.when(bit_ref[0, 0] == 0)
    def _():
        out_ref[:half, :] = mine_ref[...].astype(WIDE)
        out_ref[half:, :] = got_ref[...].astype(WIDE)

    @pl.when(bit_ref[0, 0] != 0)
    def _():
        out_ref[:half, :] = got_ref[...].astype(WIDE)
        out_ref[half:, :] = mine_ref[...].astype(WIDE)


def widen(bit, mine, got):
    rows, cols = mine.shape
    half = pl.BlockSpec((rows, LANES), lambda i: (0, i))
    return pl.pallas_call(
        widen_kernel,
        grid=(cols // LANES,),
        in_specs=[pl.BlockSpec(memory_space=pltpu.SMEM), half, half],
        out_specs=pl.BlockSpec((2 * rows, LANES), lambda i: (0, i)),
        out_shape=like((2 * rows, cols), WIDE),
        compiler_params=params(24),
        name="widen",
    )(bit.astype(jnp.int32).reshape(1, 1), mine, got)


def split_kernel(sum_ref, in_ref, out_ref):
    width = out_ref.shape[0]
    in_ref[:, 0, :] = sum_ref[:width, :].astype(WIDE)
    in_ref[:, 1, :] = sum_ref[width : 2 * width, :].astype(WIDE)
    out_ref[...] = sum_ref[2 * width :, :].astype(WIDE)


def split_feed(total):
    rows, cols = total.shape
    width = rows // 3
    return pl.pallas_call(
        split_kernel,
        grid=(cols // LANES,),
        in_specs=[pl.BlockSpec((rows, LANES), lambda i: (0, i))],
        out_specs=[
            pl.BlockSpec((width, 2, LANES), lambda i: (0, 0, i)),
            pl.BlockSpec((width, LANES), lambda i: (0, i)),
        ],
        out_shape=[like((width, 2, cols), WIDE), like((width, cols), WIDE)],
        compiler_params=params(24),
        name="split_feed",
    )(total)


def other_core(value):
    return lax.ppermute(value, "mp", [(0, 1), (1, 0)])


def to_neighbours(first, last):
    peers = lax.axis_size("seq")
    up = [(i, i + 1) for i in range(peers - 1)]
    down = [(i + 1, i) for i in range(peers - 1)]
    return lax.ppermute(last, "seq", up), lax.ppermute(first, "seq", down)


def exchange(pairs):
    return lax.all_to_all(pairs, "seq", split_axis=0, concat_axis=0, tiled=True)


def by_kind(weights):
    return weights.transpose(1, 0, 2)


def shards(
    tokens,
    out_grad,
    gains,
    routers,
    light_query_key_value_weight,
    light_attention_output_weight,
    heavy_qkv,
    heavy_out,
    light_feedforward_input_weight,
    light_feedforward_output_weight,
    heavy_mlp_in,
    heavy_mlp_out,
    routed_queries,
    routed_keys,
    routed_mlp,
    block_counts,
):
    seq_count, local_len, width = tokens.shape
    seq_devices = lax.axis_size("seq")
    row_base = lax.axis_index("seq") * local_len
    capacity = routed_queries.shape[1]
    light_cols = light_query_key_value_weight.shape[2]
    gain_rows, router_rows = gains.T, routers.T
    slot_ids = jnp.arange(capacity, dtype=jnp.int32)[None, :, None]
    rows = jnp.stack([routed_queries, routed_keys, routed_mlp], axis=2) - row_base
    valid = (slot_ids < block_counts).astype(jnp.int32)
    slots = jnp.concatenate([rows, valid], axis=2)
    place = jnp.stack([row_base, jnp.int32(seq_devices * local_len)]).astype(jnp.int32)[None, :]
    core = lax.axis_index("mp").astype(jnp.int32).reshape(1, 1)
    light_weights = by_kind(light_query_key_value_weight)
    heavy_weights_qkv = by_kind(heavy_qkv)

    before, behind = to_neighbours(tokens[:, :WIN], tokens[:, local_len - WIN :])
    low, qkv, pairs, raw, gate = front(
        tokens, gain_rows, router_rows, slots, light_weights, heavy_weights_qkv, seq_devices
    )
    pair = exchange(after(pairs, before, behind)).reshape(seq_devices * capacity, -1)
    mix, attn, lse, query, window = light_forward(
        place, qkv, before, behind, gain_rows, light_weights, light_attention_output_weight
    )
    kept, pair_mix = heavy_forward(after(pair, attn))
    mix_pairs = exchange(pair_mix.reshape(seq_devices, capacity, LANES))
    light_in = by_kind(after(light_feedforward_input_weight, kept))
    heavy_in = by_kind(after(heavy_mlp_in, kept))
    own, heavy_mix = combine(after(mix_pairs, light_in, heavy_in), attn, heavy_out, slots, gate)
    other = other_core(own)
    low_two, rows, slot, ship, gate_two = mlp_slots(
        core, tokens, own, other, out_grad, gain_rows, router_rows, slots
    )
    all_slots = seq_count * capacity * seq_devices
    gather_heavy = 2 * all_slots * width < 4 * (heavy_mlp_in.size + heavy_mlp_out.size)
    here = lax.all_gather(ship, "seq", axis=1, tiled=True) if gather_heavy else ship
    part, feed_grads, mlp = feed(
        low_two, rows, slot, gate_two, out_grad, slots, light_in, light_feedforward_output_weight,
        heavy_in, heavy_mlp_out,
    )
    beyond, mlp_other = other_core(part), other_core(mlp)
    mixed, middle_grad, mix_grad, grad_pairs, out_grads, small, query_logit = middle_back(
        tokens, own, other, part, beyond, out_grad, gain_rows, router_rows, slots, gate, mlp,
        mlp_other, mix, heavy_mix, light_attention_output_weight, heavy_out, seq_devices,
    )
    feed_sum = lax.psum(feed_grads.reshape(3 * width, -1), "seq")
    pair_grad = exchange(grad_pairs).reshape(seq_devices * capacity, -1)
    local, early, late = light_backward(place, query, window, lse, mix_grad)
    lead, tail = to_neighbours(early, late)
    triple = heavy_backward(pair, kept, after(pair_grad, local))
    triple_pairs = exchange(after(triple, lead, tail).reshape(seq_devices, capacity, -1))
    light_grads, light_part = light_project(after(local, triple), lead, tail, low, light_weights)
    triple_pairs = after(triple_pairs, light_part)
    heavy_grads, low_part, logit = heavy_project(
        light_part, low, triple_pairs, heavy_weights_qkv, slots, gate, raw, query_logit
    )
    low_other, logit_other = other_core(low_part), other_core(logit)
    input_grad, small = input_back(
        low_part, low_other, logit, logit_other, gate, slots, tokens, gain_rows, router_rows,
        middle_grad, small,
    )
    small_rows = small.astype(LOW).reshape(-1, light_cols)
    small_rows = jnp.pad(small_rows, ((0, 256 - small_rows.shape[0]), (0, 0)))
    parts = [
        light_grads.reshape(-1, light_cols),
        heavy_grads.reshape(-1, light_cols),
        jnp.concatenate([out_grads.reshape(-1, light_cols), small_rows]),
    ]
    here = after(here, light_part)
    there = other_core(here).reshape(-1, width)
    here = here.reshape(-1, width)
    steps = len(stage_orders()[0])
    pieces = 4
    heavy_sums = []

    def heavy_piece(parts, piece):
        heavy_sums[:] = heavy_weights(
            core, after(here, *parts), there, heavy_in, heavy_mlp_out, piece, pieces, heavy_sums
        )

    def joined(parts):
        kept_all = lax.optimization_barrier(tuple(parts) + tuple(heavy_sums))
        heavy_sums[:] = kept_all[len(parts) :]
        return list(kept_all[: len(parts)])

    for step in range(steps):
        started = parts
        parts = scatter_all(parts, step)
        if step < 2:
            heavy_piece(started if step else [input_grad], step)
            parts = joined(parts)
    for step in reversed(range(1, steps)):
        started = parts
        parts = gather_all(parts, step)
        if step == 1:
            heavy_piece(started, 2)
            parts = joined(parts)
    halves = [
        (p, lax.ppermute(p, "seq", bit_pairs(order[0]))) for p, order in zip(parts, stage_orders())
    ]
    heavy_piece(parts, 3)
    halves = [tuple(joined(pair)) for pair in halves]
    heavy_in_grad, heavy_out_grad = heavy_sums
    if not gather_heavy:
        sums = [heavy_in_grad[:, 0], heavy_in_grad[:, 1], heavy_out_grad]
        sums = [p.astype(LOW) for p in sums]
        for step in range(steps):
            sums = scatter_all(sums, step)
        for step in reversed(range(steps)):
            sums = gather_all(sums, step)
        heavy_in_grad = jnp.stack(sums[:2], axis=1).astype(WIDE)
        heavy_out_grad = sums[2].astype(WIDE)
    light_sum, heavy_sum, rest = [
        widen(bit_here(order[0]), *pair) for pair, order in zip(halves, stage_orders())
    ]
    feed_in, feed_out = split_feed(after(feed_sum, light_sum, heavy_sum, rest))
    small_sum = rest[2 * width : 2 * width + 8 * width // light_cols].reshape(8, width)
    return (
        mixed,
        input_grad,
        light_sum.reshape(3, width, light_cols).transpose(1, 0, 2),
        rest[:width],
        heavy_sum.reshape(3, width, light_cols).transpose(1, 0, 2),
        rest[width : 2 * width],
        feed_in,
        feed_out,
        heavy_in_grad,
        heavy_out_grad,
        jnp.stack([small_sum[2], small_sum[0]], axis=1),
        jnp.stack([small_sum[3], small_sum[4], small_sum[1]], axis=1),
    )


def solution(mesh):
    rows = P(None, "seq", None)
    by_column = P(None, None, "mp")
    by_hidden = P(None, "mp")
    slots = P(None, "seq")
    weights = (by_column, by_hidden) * 4
    return jax.shard_map(
        shards,
        mesh=mesh,
        in_specs=(rows, rows, P(), P()) + weights + (slots, slots, slots, rows),
        out_specs=(rows, rows) + weights + (P(), P()),
        check_vma=False,
    )
```

```python
import math

import jax
import jax.numpy as jnp
from jax import lax
from jax.experimental import pallas as pl
from jax.experimental.pallas import tpu as pltpu
from jax.sharding import PartitionSpec as P

LHD = 96
HHD = 64
WIN = 128
LANES = 128

EPSILON = 1e-06
MASKED = -1e30
EXACT = lax.Precision.HIGHEST
LOW = jnp.bfloat16
WIDE = jnp.float32

ROW_QUERY, ROW_KEY, ROW_MLP, OK_QUERY, OK_KEY, OK_MLP = range(6)


def lanes_of(shape):
    return lax.broadcasted_iota(jnp.int32, shape, len(shape) - 1)


def dot(a, b):
    return jnp.dot(a, b, preferred_element_type=WIDE)


def rows_dot(a, b):
    return lax.dot_general(a, b, (((1,), (1,)), ((), ())), preferred_element_type=WIDE)


def cols_dot(a, b):
    return lax.dot_general(a, b, (((0,), (0,)), ((), ())), preferred_element_type=WIDE)


def rms_of(values):
    return lax.rsqrt(jnp.mean(values * values, axis=-1, keepdims=True) + EPSILON)


def column(values, index):
    return values[:, index : index + 1]


def columns(shape, *parts):
    lane = lanes_of(shape)
    out = jnp.zeros(shape, WIDE)
    for index, part in enumerate(parts):
        out = jnp.where(lane == index, part, out)
    return out


def hot_rows(slots, index, length):
    rows = column(slots, index)
    return (lanes_of((rows.shape[0], length)) == rows).astype(WIDE)


def place_rows(hot, values):
    high = values.astype(LOW)
    rest = (values - high.astype(WIDE)).astype(LOW)
    return cols_dot(hot, high) + cols_dot(hot, rest)


def exact_place(hot, values):
    return lax.dot_general(
        hot, values, (((0,), (0,)), ((), ())), precision=EXACT, preferred_element_type=WIDE
    )


def exact_pick(hot, values):
    return jnp.dot(hot, values, precision=EXACT, preferred_element_type=WIDE)


def row_dots(values, vector):
    return jnp.sum(values * vector, axis=-1, keepdims=True)


def norm_back(values, factor, weighted):
    inner = jnp.mean(weighted * values, axis=-1, keepdims=True)
    return factor * weighted - values * (factor * factor * factor) * inner


def gelu_parts(gate, up, hidden_grad):
    root = math.sqrt(2.0 / math.pi)
    cube = 0.044715 * root
    square = gate * gate
    bend = jnp.tanh(gate * (root + cube * square))
    half = 0.5 + 0.5 * bend
    value = gate * half
    slope = half + gate * (1.0 - bend * bend) * (0.5 * root + (1.5 * cube) * square)
    return value * up, slope * up * hidden_grad, value * hidden_grad


def merge_heads(ref, offset, heads):
    tiles = []
    for head in range(0, heads, 2):
        first = ref[head, :, offset : offset + LANES].astype(WIDE)
        second = ref[head + 1, :, offset : offset + LANES].astype(WIDE)
        lane = lanes_of(first.shape)
        tiles.append(jnp.where(lane < HHD, first, pltpu.roll(second, HHD, 1)))
    return jnp.concatenate(tiles, axis=1)


def merge_upper(ref, heads):
    tiles = []
    for head in range(0, heads, 2):
        first = ref[head, :, :LANES].astype(WIDE)
        second = ref[head + 1, :, :LANES].astype(WIDE)
        lane = lanes_of(first.shape)
        tiles.append(jnp.where(lane < HHD, pltpu.roll(first, HHD, 1), second))
    return jnp.concatenate(tiles, axis=1)


def head_low(values, head):
    tile = values[:, head // 2 * LANES : (head // 2 + 1) * LANES]
    return tile if head % 2 == 0 else pltpu.roll(tile, HHD, 1)


def head_high(values, head):
    tile = values[:, head // 2 * LANES : (head // 2 + 1) * LANES]
    return tile if head % 2 == 1 else pltpu.roll(tile, HHD, 1)


def spread_matrix(heads):
    row = lax.broadcasted_iota(jnp.int32, (heads * LHD, heads * LANES), 0)
    lane = lanes_of((heads * LHD, heads * LANES))
    inner = lane & (LANES - 1)
    hit = (row == (lane >> 7) * LHD + inner) & (inner < LHD)
    return hit.astype(WIDE).astype(LOW)


def params(mib=56):
    return pltpu.CompilerParams(vmem_limit_bytes=mib * 2**20)


def cost(microseconds):
    return pl.CostEstimate(
        flops=int(microseconds * 2e7), bytes_accessed=2**10, transcendentals=0
    )


def whole(array):
    zeros = (0,) * array.ndim
    return pl.BlockSpec(array.shape, lambda *_: zeros, pipeline_mode=pl.Buffered(1))


def each(array):
    rest = (0,) * (array.ndim - 1)
    return pl.BlockSpec((1,) + array.shape[1:], lambda s: (s,) + rest)


def like(shape, kind):
    return jax.ShapeDtypeStruct(shape, kind)


def front_kernel(
    tokens_ref, gains_ref, routers_ref, slots_ref, light_ref, heavy_ref,
    low_ref, qkv_ref, pair_ref, raw_ref, gate_ref,
):
    inputs = tokens_ref[0].astype(WIDE)
    length = inputs.shape[0]
    normed = inputs * rms_of(inputs) * gains_ref[0:1, :]
    low = normed.astype(LOW)
    low_ref[0] = low
    slots = slots_ref[0]
    hot_query = hot_rows(slots, ROW_QUERY, length)
    hot_key = hot_rows(slots, ROW_KEY, length)
    logits = columns(
        (length, LANES),
        row_dots(normed, routers_ref[0:1, :]),
        row_dots(normed, routers_ref[1:2, :]),
    )
    query_gate = jax.nn.sigmoid(column(exact_pick(hot_query, logits), 0))
    key_gate = jax.nn.sigmoid(column(exact_pick(hot_key, logits), 1))
    gate_ref[0] = columns((slots.shape[0], LANES), query_gate, key_gate)
    query_in = dot(hot_query.astype(LOW), low).astype(LOW)
    key_in = dot(hot_key.astype(LOW), low).astype(LOW)
    query = dot(query_in, heavy_ref[0]).astype(LOW).astype(WIDE)
    key = dot(key_in, heavy_ref[1]).astype(LOW).astype(WIDE)
    raw = dot(key_in, heavy_ref[2])
    raw_ref[0] = raw
    value = (key_gate * raw).astype(LOW).astype(WIDE)
    bias = jnp.where(column(slots, OK_KEY) > 0, 0.0, MASKED)
    lane = lanes_of((slots.shape[0], LANES))
    for head in range(raw.shape[1] // HHD):
        both = jnp.where(lane < HHD, head_low(query, head), head_high(key, head))
        extra = jnp.where(lane < HHD, head_low(value, head), bias)
        pair_ref[head, :, :LANES] = both.astype(LOW)
        pair_ref[head, :, LANES:] = extra.astype(LOW)
    for kind in range(3):
        qkv_ref[0, kind] = dot(low, light_ref[kind]).astype(LOW)


def front(tokens, gains, routers, slots, light, heavy, seq_devices):
    seqs, length, width = tokens.shape
    cap = slots.shape[1]
    light_cols, heavy_cols = light.shape[2], heavy.shape[2]
    heads = heavy_cols // HHD
    shapes = [
        like(tokens.shape, LOW),
        like((seqs, 3, length, light_cols), LOW),
        like((seq_devices, cap, 2 * LANES), LOW),
        like((seqs, cap, heavy_cols), WIDE),
        like((seqs, cap, LANES), WIDE),
    ]
    specs = [each(s) for s in shapes]
    specs[2] = pl.BlockSpec((heads, cap, 2 * LANES), lambda s: (s, 0, 0))
    return pl.pallas_call(
        front_kernel,
        grid=(seqs,),
        in_specs=[each(tokens), whole(gains), whole(routers), each(slots), whole(light), whole(heavy)],
        out_specs=specs,
        out_shape=shapes,
        compiler_params=params(),
        cost_estimate=cost(8),
        name="front",
    )(tokens, gains, routers, slots, light, heavy)


def window_bias(block, length, base, total):
    row = lax.broadcasted_iota(jnp.int32, (WIN, 3 * WIN), 0)
    col = lanes_of((WIN, 3 * WIN))
    place = base + (block - 1) * WIN + col
    near = jnp.abs(col - WIN - row) < WIN
    return jnp.where(near & (place >= 0) & (place < total), 0.0, MASKED)


def light_forward_kernel(
    scale, place_ref, qkv_ref, before_ref, after_ref, gains_ref, weight_ref, out_ref,
    mix_ref, attn_ref, lse_ref, query_ref, window_ref, wide_ref,
):
    length, light_cols = qkv_ref.shape[2:]
    heads = light_cols // LHD
    spread = spread_matrix(heads)
    query_ref[0] = dot(qkv_ref[0, 0], spread).astype(LOW)
    edges = ((before_ref, slice(0, WIN)), (after_ref, slice(WIN + length, 2 * WIN + length)))
    for ref, rows in edges:
        inputs = ref[0].astype(WIDE)
        low = (inputs * rms_of(inputs) * gains_ref[0:1, :]).astype(LOW)
        for kind in range(2):
            edge = dot(low, weight_ref[1 + kind]).astype(LOW)
            window_ref[0, kind, rows, :] = dot(edge, spread).astype(LOW)
    for kind in range(2):
        window_ref[0, kind, WIN : WIN + length, :] = dot(qkv_ref[0, 1 + kind], spread).astype(LOW)
    for block in range(length // WIN):
        rows = slice(block * WIN, (block + 1) * WIN)
        near = slice(block * WIN, (block + 3) * WIN)
        bias = window_bias(block, length, place_ref[0, 0], place_ref[0, 1])
        kept = []
        for head in range(heads):
            lanes = slice(head * LANES, (head + 1) * LANES)
            scores = rows_dot(query_ref[0, rows, lanes], window_ref[0, 0, near, lanes]) * scale + bias
            top = jnp.max(scores, axis=-1, keepdims=True)
            expo = jnp.exp(scores - top)
            total = jnp.sum(expo, axis=-1, keepdims=True)
            mixed = dot(expo.astype(LOW), window_ref[0, 1, near, lanes]) / total
            wide_ref[rows, lanes] = mixed.astype(LOW)
            kept.append(top + jnp.log(total))
        lse_ref[0, rows, :] = columns((WIN, LANES), *kept)
    mix = rows_dot(wide_ref[...], spread).astype(LOW)
    mix_ref[0] = mix
    attn_ref[0] = rows_dot(mix, out_ref[...])


def light_forward(place, qkv, before, after, gains, weight, weight_out):
    seqs, _, length, light_cols = qkv.shape
    heads = light_cols // LHD
    shapes = [
        like((seqs, length, light_cols), LOW),
        like((seqs, length, weight_out.shape[0]), WIDE),
        like((seqs, length, LANES), WIDE),
        like((seqs, length, heads * LANES), LOW),
        like((seqs, 2, length + 2 * WIN, heads * LANES), LOW),
    ]
    return pl.pallas_call(
        lambda *refs: light_forward_kernel(1.0 / math.sqrt(LHD), *refs),
        grid=(seqs,),
        in_specs=[
            pl.BlockSpec(memory_space=pltpu.SMEM),
            each(qkv),
            each(before),
            each(after),
            whole(gains),
            whole(weight),
            whole(weight_out),
        ],
        out_specs=[each(s) for s in shapes],
        out_shape=shapes,
        scratch_shapes=[pltpu.VMEM((length, heads * LANES), LOW)],
        compiler_params=params(),
        cost_estimate=cost(15),
        name="light_forward",
    )(place, qkv, before, after, gains, weight, weight_out)


def light_backward_kernel(
    scale, place_ref, query_ref, window_ref, lse_ref, grad_ref, local_ref, early_ref, late_ref, *scratch
):
    wide_ref, dkey_ref, dvalue_ref = scratch
    length, light_cols = grad_ref.shape[1:]
    heads = light_cols // LHD
    spread = spread_matrix(heads)
    grad = dot(grad_ref[0], spread).astype(LOW)
    dkey_ref[...] = jnp.zeros_like(dkey_ref)
    dvalue_ref[...] = jnp.zeros_like(dvalue_ref)
    for block in range(length // WIN):
        rows = slice(block * WIN, (block + 1) * WIN)
        near = slice(block * WIN, (block + 3) * WIN)
        bias = window_bias(block, length, place_ref[0, 0], place_ref[0, 1])
        lse = lse_ref[0, rows, :]
        for head in range(heads):
            lanes = slice(head * LANES, (head + 1) * LANES)
            key = window_ref[0, 0, near, lanes]
            part = grad[rows, lanes]
            mine = query_ref[0, rows, lanes]
            probs = jnp.exp(rows_dot(mine, key) * scale + bias - column(lse, head))
            prob_grad = rows_dot(part, window_ref[0, 1, near, lanes])
            delta = jnp.sum(probs * prob_grad, axis=-1, keepdims=True)
            score_grad = (probs * (prob_grad - delta)).astype(LOW)
            wide_ref[rows, lanes] = (dot(score_grad, key) * scale).astype(LOW)
            dkey_ref[near, lanes] += cols_dot(score_grad, mine) * scale
            dvalue_ref[near, lanes] += cols_dot(probs.astype(LOW), part)
    local_ref[0, 0] = rows_dot(wide_ref[...], spread).astype(LOW)
    for kind, ref in ((1, dkey_ref), (2, dvalue_ref)):
        all_rows = rows_dot(ref[...].astype(LOW), spread).astype(LOW)
        early_ref[0, kind - 1] = all_rows[:WIN]
        local_ref[0, kind] = all_rows[WIN : WIN + length]
        late_ref[0, kind - 1] = all_rows[WIN + length :]


def light_backward(place, query, window, lse, grad):
    seqs, length, light_cols = grad.shape
    edge = like((seqs, 2, WIN, light_cols), LOW)
    shapes = [like((seqs, 3, length, light_cols), LOW), edge, edge]
    return pl.pallas_call(
        lambda *refs: light_backward_kernel(1.0 / math.sqrt(LHD), *refs),
        grid=(seqs,),
        in_specs=[
            pl.BlockSpec(memory_space=pltpu.SMEM),
            each(query),
            each(window),
            each(lse),
            each(grad),
        ],
        out_specs=[each(s) for s in shapes],
        out_shape=shapes,
        scratch_shapes=[
            pltpu.VMEM(query.shape[1:], LOW),
            pltpu.VMEM(window.shape[2:], WIDE),
            pltpu.VMEM(window.shape[2:], WIDE),
        ],
        compiler_params=params(),
        cost_estimate=cost(14),
        name="light_backward",
    )(place, query, window, lse, grad)


def key_operand(pair, extra):
    lane = lanes_of(pair.shape)
    moved = pltpu.roll(pair.astype(WIDE), HHD, 1)
    bias = column(extra, HHD).astype(WIDE)
    return jnp.where(lane < HHD, moved, jnp.where(lane == HHD, bias, 0.0)).astype(LOW)


def query_operand(pair, scale):
    lane = lanes_of(pair.shape)
    scaled = pair.astype(WIDE) * scale
    return jnp.where(lane < HHD, scaled, jnp.where(lane == HHD, 1.0, 0.0)).astype(LOW)


def heavy_forward_kernel(tile, scale, pair_ref, kept_ref, mix_ref, key_ref):
    @pl.when(pl.program_id(0) == 0)
    def _():
        key_ref[...] = key_operand(pair_ref[:, :LANES], pair_ref[:, LANES:])

    start = pl.multiple_of(pl.program_id(0) * tile, tile)
    query = query_operand(pair_ref[pl.ds(start, tile), :LANES], scale)
    scores = rows_dot(query, key_ref[...])
    top = jnp.max(scores, axis=-1, keepdims=True)
    expo = jnp.exp(scores - top)
    total = jnp.sum(expo, axis=-1, keepdims=True)
    mix = dot(expo.astype(LOW), pair_ref[:, LANES:]) / total
    lane = lanes_of(mix.shape)
    kept_ref[...] = jnp.where(lane < HHD, mix, top + jnp.log(total))
    mix_ref[...] = jnp.where(lane < HHD, mix, 0.0).astype(LOW)


def heavy_backward_kernel(
    tile, scale, pair_ref, kept_ref, grad_ref, both_ref, key_ref, dk_ref, dv_ref
):
    step = pl.program_id(0)

    @pl.when(step == 0)
    def _():
        key_ref[...] = key_operand(pair_ref[:, :LANES], pair_ref[:, LANES:])
        dk_ref[...] = jnp.zeros_like(dk_ref)
        dv_ref[...] = jnp.zeros_like(dv_ref)

    start = pl.multiple_of(step * tile, tile)
    query = query_operand(pair_ref[pl.ds(start, tile), :LANES], scale)
    lane = lanes_of(query.shape)
    kept = kept_ref[...]
    grad = grad_ref[...]
    lse = column(kept, HHD)
    delta = jnp.sum(
        jnp.where(lane < HHD, kept * grad.astype(WIDE), 0.0), axis=-1, keepdims=True
    )
    probs = jnp.exp(rows_dot(query, key_ref[...]) - lse)
    prob_grad = rows_dot(grad, pair_ref[:, LANES:])
    score_grad = (probs * (prob_grad - delta)).astype(LOW)
    query_grad = dot(score_grad, key_ref[...]) * scale
    both_ref[pl.ds(start, tile), :LANES] = jnp.where(lane < HHD, query_grad, 0.0).astype(LOW)
    dk_ref[...] += cols_dot(score_grad, query)
    dv_ref[...] += cols_dot(probs.astype(LOW), grad)

    @pl.when(step == pl.num_programs(0) - 1)
    def _():
        spot = lanes_of(dk_ref.shape)
        moved = pltpu.roll(dk_ref[...], HHD, 1)
        query_part = both_ref[:, :LANES].astype(WIDE)
        both_ref[:, :LANES] = jnp.where(spot < HHD, query_part, moved).astype(LOW)
        both_ref[:, LANES:] = dv_ref[...].astype(LOW)


def query_tile(length):
    return 256 if length % 256 == 0 else length


def heavy_forward(pair):
    length = pair.shape[0]
    tile = query_tile(length)
    rows = pl.BlockSpec((tile, LANES), lambda i: (i, 0))
    return pl.pallas_call(
        lambda *refs: heavy_forward_kernel(tile, 1.0 / math.sqrt(HHD), *refs),
        grid=(length // tile,),
        in_specs=[whole(pair)],
        out_specs=[rows, rows],
        out_shape=[like((length, LANES), WIDE), like((length, LANES), LOW)],
        scratch_shapes=[pltpu.VMEM((length, LANES), LOW)],
        compiler_params=params(60),
        cost_estimate=cost(7),
        name="heavy_forward",
    )(pair)


def heavy_backward(pair, kept, grad):
    length = pair.shape[0]
    tile = query_tile(length)
    rows = pl.BlockSpec((tile, LANES), lambda i: (i, 0))
    return pl.pallas_call(
        lambda *refs: heavy_backward_kernel(tile, 1.0 / math.sqrt(HHD), *refs),
        grid=(length // tile,),
        in_specs=[whole(pair), rows, rows],
        out_specs=whole(pair),
        out_shape=like(pair.shape, LOW),
        scratch_shapes=[
            pltpu.VMEM((length, LANES), LOW),
            pltpu.VMEM((length, LANES), WIDE),
            pltpu.VMEM((length, LANES), WIDE),
        ],
        compiler_params=params(60),
        cost_estimate=cost(10),
        name="heavy_backward",
    )(pair, kept, grad)


def combine_kernel(pairs_ref, attn_ref, out_ref, slots_ref, gate_ref, part_ref, mix_ref):
    slots = slots_ref[0]
    mix = merge_heads(pairs_ref, 0, pairs_ref.shape[0]).astype(LOW)
    mix_ref[0] = mix
    rows = rows_dot(mix, out_ref[...])
    weight = jnp.where(column(slots, OK_QUERY) > 0, column(gate_ref[0], 0), 0.0)
    hot = hot_rows(slots, ROW_QUERY, attn_ref.shape[1]).astype(LOW)
    part_ref[0] = (attn_ref[0] + place_rows(hot, weight * rows)).astype(LOW)


def pair_spec(pairs, heads):
    return pl.BlockSpec((heads,) + pairs.shape[1:], lambda s: (s, 0, 0))


def combine(pairs, attn, weight_out, slots, gate):
    seqs, cap = slots.shape[:2]
    heavy_cols = weight_out.shape[1]
    shapes = [like(attn.shape, LOW), like((seqs, cap, heavy_cols), LOW)]
    return pl.pallas_call(
        combine_kernel,
        grid=(seqs,),
        in_specs=[
            pair_spec(pairs, heavy_cols // HHD),
            each(attn),
            whole(weight_out),
            each(slots),
            each(gate),
        ],
        out_specs=[each(s) for s in shapes],
        out_shape=shapes,
        compiler_params=params(),
        cost_estimate=cost(4),
        name="combine",
    )(pairs, attn, weight_out, slots, gate)


def slots_kernel(
    core_ref, tokens_ref, own_ref, other_ref, up_ref, gains_ref, routers_ref, slots_ref,
    low_ref, rows_ref, slot_ref, ship_ref, gate_ref,
):
    middle = tokens_ref[0].astype(WIDE) + own_ref[0].astype(WIDE) + other_ref[0].astype(WIDE)
    length = middle.shape[0]
    normed = middle * rms_of(middle) * gains_ref[1:2, :]
    low = normed.astype(LOW)
    low_ref[0] = low
    slots = slots_ref[0]
    hot = hot_rows(slots, ROW_MLP, length)
    logits = columns((length, LANES), row_dots(normed, routers_ref[2:3, :]))
    gate = jax.nn.sigmoid(column(exact_pick(hot, logits), 0))
    weight = jnp.where(column(slots, OK_MLP) > 0, gate, 0.0)
    hot = hot.astype(LOW)
    rows = dot(hot, low)
    slot = weight * dot(hot, up_ref[0])
    rows_ref[0] = rows.astype(LOW)
    slot_ref[0] = slot.astype(LOW)
    ship_ref[0] = jnp.where(core_ref[0, 0] == 0, rows, slot).astype(LOW)
    gate_ref[0] = columns((slots.shape[0], LANES), gate, weight)


def mlp_slots(core, tokens, own, other, up, gains, routers, slots):
    seqs, length, width = tokens.shape
    cap = slots.shape[1]
    shapes = [like(tokens.shape, LOW)]
    shapes += [like((seqs, cap, width), LOW)] * 3 + [like((seqs, cap, LANES), WIDE)]
    return pl.pallas_call(
        slots_kernel,
        grid=(seqs,),
        in_specs=[
            pl.BlockSpec(memory_space=pltpu.SMEM),
            each(tokens), each(own), each(other), each(up), whole(gains), whole(routers), each(slots),
        ],
        out_specs=[each(s) for s in shapes],
        out_shape=shapes,
        compiler_params=params(),
        cost_estimate=cost(5),
        name="mlp_slots",
    )(core, tokens, own, other, up, gains, routers, slots)


def pack_wide(ref, value):
    value = value.astype(LOW)
    rows, cols = value.shape[0], ref.shape[1]
    extra = value.shape[1] - cols
    group = rows * extra // cols
    ref[:rows, :] = value[:, :cols]
    for index in range(cols // extra):
        ref[rows:, index * extra : (index + 1) * extra] = value[
            index * group : (index + 1) * group, cols:
        ]


def unpack_wide(store, ref, start, rows, extra):
    cols = ref.shape[1]
    group = rows * extra // cols
    store(slice(0, rows), slice(0, cols), ref[start : start + rows, :])
    for index in range(cols // extra):
        store(
            slice(index * group, (index + 1) * group),
            slice(cols, cols + extra),
            ref[start + rows : start + rows + group, index * extra : (index + 1) * extra],
        )


def feed_kernel(
    low_ref, rows_ref, slot_ref, kept_ref, up_ref, slots_ref, in_ref, out_ref, heavy_in_ref,
    heavy_out_ref, part_ref, weights_ref, gate_ref, heavy_acc, back_acc, hidden_ref, dgate_ref, dup_ref,
):
    step = pl.program_id(0)
    seqs, length, width = up_ref.shape
    cap = slots_ref.shape[1]

    @pl.when(step == 0)
    def _():
        heavy_acc[...] = jnp.zeros_like(heavy_acc)
        back_acc[...] = jnp.zeros_like(back_acc)

    first, second, last = heavy_in_ref[0], heavy_in_ref[1], heavy_out_ref[...]
    rows = rows_ref[...]
    hidden, gate_grad, up_grad = gelu_parts(
        dot(rows, first), dot(rows, second), dot(slot_ref[...], last)
    )
    heavy_acc[...] += rows_dot(hidden.astype(LOW), last)
    back_acc[...] += rows_dot(gate_grad.astype(LOW), first) + rows_dot(up_grad.astype(LOW), second)

    @pl.when(step == pl.num_programs(0) - 1)
    def _():
        for s in range(seqs):
            here = slice(s * length, (s + 1) * length)
            mine = slice(s * cap, (s + 1) * cap)
            low = low_ref[s]
            hidden, gate_grad, up_grad = gelu_parts(
                dot(low, in_ref[0]), dot(low, in_ref[1]), dot(up_ref[s], out_ref[...])
            )
            hidden, gate_grad, up_grad = (
                hidden.astype(LOW),
                gate_grad.astype(LOW),
                up_grad.astype(LOW),
            )
            hidden_ref[here, :] = hidden
            dgate_ref[here, :] = gate_grad
            dup_ref[here, :] = up_grad
            hot = hot_rows(slots_ref[s], ROW_MLP, length).astype(LOW)
            kept = kept_ref[s]
            heavy_rows = heavy_acc[mine, :]
            part_ref[0, s] = (
                rows_dot(hidden, out_ref[...]) + place_rows(hot, column(kept, 1) * heavy_rows)
            ).astype(LOW)
            part_ref[1, s] = (
                rows_dot(gate_grad, in_ref[0])
                + rows_dot(up_grad, in_ref[1])
                + place_rows(hot, back_acc[mine, :])
            ).astype(LOW)
            gate_part = jnp.sum(dot(hot, up_ref[s]) * heavy_rows, axis=-1, keepdims=True)
            gate_ref[s] = columns((cap, LANES), column(kept, 0), gate_part)
        low = low_ref[...].reshape(seqs * length, width)
        up = up_ref[...].reshape(seqs * length, width)
        pack_wide(weights_ref.at[0], cols_dot(low, dgate_ref[...]))
        pack_wide(weights_ref.at[1], cols_dot(low, dup_ref[...]))
        pack_wide(weights_ref.at[2], cols_dot(up, hidden_ref[...]))


def feed(low, rows, slot, kept, up, slots, light_in, light_out, heavy_in, heavy_out, packed_cols):
    seqs, length, width = up.shape
    cap = slots.shape[1]
    hidden = light_out.shape[1]
    cols = 256
    rows, slot = rows.reshape(-1, width), slot.reshape(-1, width)
    shapes = [
        like((2, seqs, length, width), LOW),
        like((3, width * hidden // packed_cols, packed_cols), LOW),
        like((seqs, cap, LANES), WIDE),
    ]
    return pl.pallas_call(
        feed_kernel,
        grid=(heavy_out.shape[1] // cols,),
        in_specs=[
            whole(low),
            whole(rows),
            whole(slot),
            whole(kept),
            whole(up),
            whole(slots),
            whole(light_in),
            whole(light_out),
            pl.BlockSpec((2, width, cols), lambda i: (0, 0, i)),
            pl.BlockSpec((width, cols), lambda i: (0, i)),
        ],
        out_specs=[whole(s) for s in shapes],
        out_shape=shapes,
        scratch_shapes=[pltpu.VMEM((seqs * cap, width), WIDE)] * 2
        + [pltpu.VMEM((seqs * length, hidden), LOW)] * 3,
        compiler_params=params(),
        cost_estimate=cost(20),
        name="feed",
    )(low, rows, slot, kept, up, slots, light_in, light_out, heavy_in, heavy_out)


def middle_kernel(
    tokens_ref, own_ref, other_ref, part_ref, beyond_ref, up_ref, gains_ref, routers_ref, slots_ref,
    gate_ref, mlp_ref, mlp_other_ref, mix_ref, heavy_mix_ref, light_out_ref, heavy_out_ref, down_ref,
    mixed_ref, middle_ref, grad_ref, pair_ref, weights_ref, small_ref, logit_ref, weights_acc,
):
    step = pl.program_id(0)

    @pl.when(step == 0)
    def _():
        weights_acc[...] = jnp.zeros_like(weights_acc)
        small_ref[...] = jnp.zeros_like(small_ref)

    slots = slots_ref[0]
    cap = slots.shape[0]
    middle = tokens_ref[0].astype(WIDE) + own_ref[0].astype(WIDE) + other_ref[0].astype(WIDE)
    length = middle.shape[0]
    factor = rms_of(middle)
    scaled = middle * factor
    normed = scaled * gains_ref[1:2, :]
    mixed = middle + (part_ref[0, 0].astype(WIDE) + beyond_ref[0, 0].astype(WIDE))
    mixed_ref[0] = mixed.astype(LOW)
    gate = column(mlp_ref[0], 0)
    gate_grad = column(mlp_ref[0], 1) + column(mlp_other_ref[0], 1)
    logit_grad = jnp.where(column(slots, OK_MLP) > 0, gate_grad * gate * (1.0 - gate), 0.0)
    token_grad = column(
        exact_place(hot_rows(slots, ROW_MLP, length), columns((cap, LANES), logit_grad)), 0
    )
    normed_grad = (
        part_ref[1, 0].astype(WIDE) + beyond_ref[1, 0].astype(WIDE)
    ) + token_grad * routers_ref[2:3, :]
    small_ref[0:1, :] += jnp.sum(normed_grad * scaled, axis=0, keepdims=True)
    small_ref[1:2, :] += jnp.sum(token_grad * normed, axis=0, keepdims=True)
    middle_grad = up_ref[0].astype(WIDE) + norm_back(middle, factor, normed_grad * gains_ref[1:2, :])
    middle_ref[0] = middle_grad
    low = middle_grad.astype(LOW)
    hot = hot_rows(slots, ROW_QUERY, length).astype(LOW)
    up_rows = dot(hot, low)
    weight = jnp.where(column(slots, OK_QUERY) > 0, column(gate_ref[0], 0), 0.0)
    slot = (weight * up_rows).astype(LOW)
    heavy_rows = rows_dot(heavy_mix_ref[0], heavy_out_ref[...])
    logit_ref[0] = columns(
        (cap, LANES), jnp.sum(up_rows * heavy_rows, axis=-1, keepdims=True)
    )
    mix_grad = dot(slot, heavy_out_ref[...]).astype(LOW).astype(WIDE)
    lane = lanes_of((cap, LANES))
    for head in range(mix_grad.shape[1] // HHD):
        pair_ref[head] = jnp.where(lane < HHD, head_low(mix_grad, head), 0.0).astype(LOW)
    grad_ref[0] = dot(low, light_out_ref[...]).astype(LOW)
    weights_acc[0] += cols_dot(low, mix_ref[0])
    weights_acc[1] += cols_dot(slot, heavy_mix_ref[0])

    @pl.when(step == pl.num_programs(0) - 1)
    def _():
        start, rows = down_ref.shape[0], weights_acc.shape[1]
        weights_ref[:start, :] = down_ref[...]
        for kind in range(2):
            weights_ref[start + kind * rows : start + (kind + 1) * rows, :] = weights_acc[kind].astype(LOW)


def middle_back(
    tokens, own, other, part, beyond, up, gains, routers, slots, gate, mlp, mlp_other,
    mix, heavy_mix, light_out, heavy_out, down, seq_devices,
):
    seqs, length, width = tokens.shape
    cap = slots.shape[1]
    cols = light_out.shape[1]
    heads = heavy_out.shape[1] // HHD
    shapes = [
        like(tokens.shape, LOW),
        like(tokens.shape, WIDE),
        like((seqs, length, cols), LOW),
        like((seq_devices, cap, LANES), LOW),
        like((down.shape[0] + 2 * width, cols), LOW),
        like((8, width), WIDE),
        like((seqs, cap, LANES), WIDE),
    ]
    specs = [
        each(shapes[0]), each(shapes[1]), each(shapes[2]), pair_spec(shapes[3], heads),
        whole(shapes[4]), whole(shapes[5]), each(shapes[6]),
    ]
    both = pl.BlockSpec((2, 1, length, width), lambda s: (0, s, 0, 0))
    return pl.pallas_call(
        middle_kernel,
        grid=(seqs,),
        in_specs=[
            each(tokens), each(own), each(other), both, both, each(up), whole(gains),
            whole(routers), each(slots), each(gate), each(mlp), each(mlp_other), each(mix),
            each(heavy_mix), whole(light_out), whole(heavy_out), whole(down),
        ],
        out_specs=specs,
        out_shape=shapes,
        scratch_shapes=[pltpu.VMEM((2, width, cols), WIDE)],
        compiler_params=params(),
        cost_estimate=cost(11),
        name="middle_back",
    )(
        tokens, own, other, part, beyond, up, gains, routers, slots, gate, mlp, mlp_other,
        mix, heavy_mix, light_out, heavy_out, down,
    )


def light_project_kernel(local_ref, low_ref, light_ref, grad_ref, part_ref):
    @pl.when(pl.program_id(0) == 0)
    def _():
        grad_ref[...] = jnp.zeros_like(grad_ref)

    low = low_ref[0]
    part = None
    for kind in range(3):
        rows = local_ref[0, kind]
        grad_ref[kind] += cols_dot(low, rows)
        more = rows_dot(rows, light_ref[kind])
        part = more if part is None else part + more
    part_ref[0] = part


def light_project(local, low, light):
    shapes = [like(light.shape, WIDE), like(low.shape, WIDE)]
    return pl.pallas_call(
        light_project_kernel,
        grid=(low.shape[0],),
        in_specs=[each(local), each(low), whole(light)],
        out_specs=[whole(shapes[0]), each(shapes[1])],
        out_shape=shapes,
        compiler_params=params(),
        cost_estimate=cost(9),
        name="light_project",
    )(local, low, light)


def heavy_project_kernel(
    light_part_ref, low_ref, pairs_ref, heavy_ref, slots_ref, gate_ref, raw_ref, logit_ref,
    lead_ref, tail_ref, light_ref, light_sum_ref,
    grad_ref, light_grad_ref, part_ref, both_logit_ref, grad_acc, light_acc,
):
    step = pl.program_id(0)

    @pl.when(step == 0)
    def _():
        grad_acc[...] = jnp.zeros_like(grad_acc)
        light_acc[...] = light_sum_ref[1:]

    low = low_ref[0]
    length = low.shape[0]
    slots = slots_ref[0]
    cap = slots.shape[0]
    heads = raw_ref.shape[2] // HHD
    key_gate = column(gate_ref[0], 1)
    query_grad = merge_heads(pairs_ref, 0, heads).astype(LOW)
    key_grad = merge_upper(pairs_ref, heads).astype(LOW)
    value_grad = merge_heads(pairs_ref, LANES, heads)
    raw_grad = (key_gate * value_grad).astype(LOW)
    key_logit = jnp.sum(value_grad * raw_ref[0], axis=-1, keepdims=True)
    both_logit_ref[0] = columns((cap, LANES), column(logit_ref[0], 0), key_logit)
    hot_query = hot_rows(slots, ROW_QUERY, length).astype(LOW)
    hot_key = hot_rows(slots, ROW_KEY, length).astype(LOW)
    query_in = dot(hot_query, low).astype(LOW)
    key_in = dot(hot_key, low).astype(LOW)
    grad_acc[0] += cols_dot(query_in, query_grad)
    grad_acc[1] += cols_dot(key_in, key_grad)
    grad_acc[2] += cols_dot(key_in, raw_grad)
    part = light_part_ref[0] + place_rows(hot_query, rows_dot(query_grad, heavy_ref[0]))
    part = part + place_rows(
        hot_key, rows_dot(key_grad, heavy_ref[1]) + rows_dot(raw_grad, heavy_ref[2])
    )
    edges = []
    for ref, rows in ((lead_ref, slice(0, WIN)), (tail_ref, slice(length - WIN, length))):
        for kind in range(2):
            light_acc[kind] += cols_dot(low[rows], ref[0, kind])
        edges.append(rows_dot(ref[0, 0], light_ref[1]) + rows_dot(ref[0, 1], light_ref[2]))
    part_ref[0, :WIN] = (part[:WIN] + edges[0]).astype(LOW)
    part_ref[0, WIN : length - WIN] = part[WIN : length - WIN].astype(LOW)
    part_ref[0, length - WIN :] = (part[length - WIN :] + edges[1]).astype(LOW)

    @pl.when(step == pl.num_programs(0) - 1)
    def _():
        grad_ref[...] = grad_acc[...].astype(LOW)
        light_grad_ref[0] = light_sum_ref[0].astype(LOW)
        light_grad_ref[1:] = light_acc[...].astype(LOW)


def heavy_project(
    light_part, low, pairs, heavy, slots, gate, raw, logit, lead, tail, light, light_sum
):
    heads = heavy.shape[2] // HHD
    shapes = [
        like(heavy.shape, LOW),
        like(light.shape, LOW),
        like(low.shape, LOW),
        like(logit.shape, WIDE),
    ]
    return pl.pallas_call(
        heavy_project_kernel,
        grid=(low.shape[0],),
        in_specs=[
            each(light_part), each(low), pair_spec(pairs, heads), whole(heavy), each(slots),
            each(gate), each(raw), each(logit), each(lead), each(tail), whole(light),
            whole(light_sum),
        ],
        out_specs=[whole(shapes[0]), whole(shapes[1]), each(shapes[2]), each(shapes[3])],
        out_shape=shapes,
        scratch_shapes=[
            pltpu.VMEM(heavy.shape, WIDE),
            pltpu.VMEM((2,) + light.shape[1:], WIDE),
        ],
        compiler_params=params(),
        cost_estimate=cost(11),
        name="heavy_project",
    )(light_part, low, pairs, heavy, slots, gate, raw, logit, lead, tail, light, light_sum)


def input_kernel(
    part_ref, other_ref, logit_ref, logit_other_ref, gate_ref, slots_ref, tokens_ref, gains_ref,
    routers_ref, middle_ref, small_in_ref, grad_ref, small_ref,
):
    @pl.when(pl.program_id(0) == 0)
    def _():
        small_ref[...] = small_in_ref[...]

    slots = slots_ref[0]
    cap = slots.shape[0]
    inputs = tokens_ref[0].astype(WIDE)
    length = inputs.shape[0]
    factor = rms_of(inputs)
    scaled = inputs * factor
    normed = scaled * gains_ref[0:1, :]
    gates = gate_ref[0]
    grads = (logit_ref[0] + logit_other_ref[0]) * gates * (1.0 - gates)
    query_logit = jnp.where(column(slots, OK_QUERY) > 0, column(grads, 0), 0.0)
    key_logit = jnp.where(column(slots, OK_KEY) > 0, column(grads, 1), 0.0)
    query_token = column(
        exact_place(hot_rows(slots, ROW_QUERY, length), columns((cap, LANES), query_logit)), 0
    )
    key_token = column(
        exact_place(hot_rows(slots, ROW_KEY, length), columns((cap, LANES), key_logit)), 0
    )
    normed_grad = (
        (part_ref[0].astype(WIDE) + other_ref[0].astype(WIDE))
        + query_token * routers_ref[0:1, :]
        + key_token * routers_ref[1:2, :]
    )
    small_ref[2:3, :] += jnp.sum(normed_grad * scaled, axis=0, keepdims=True)
    small_ref[3:4, :] += jnp.sum(query_token * normed, axis=0, keepdims=True)
    small_ref[4:5, :] += jnp.sum(key_token * normed, axis=0, keepdims=True)
    grad_ref[0] = middle_ref[0] + norm_back(inputs, factor, normed_grad * gains_ref[0:1, :])


def input_back(part, other, logit, logit_other, gate, slots, tokens, gains, routers, middle, small):
    shapes = [like(middle.shape, WIDE), like(small.shape, WIDE)]
    return pl.pallas_call(
        input_kernel,
        grid=(tokens.shape[0],),
        in_specs=[
            each(part), each(other), each(logit), each(logit_other), each(gate), each(slots),
            each(tokens), whole(gains), whole(routers), each(middle), whole(small),
        ],
        out_specs=[each(shapes[0]), whole(shapes[1])],
        out_shape=shapes,
        compiler_params=params(),
        cost_estimate=cost(6),
        name="input_back",
    )(part, other, logit, logit_other, gate, slots, tokens, gains, routers, middle, small)


def heavy_weights_kernel(tile, core_ref, here_ref, there_ref, in_ref, out_ref, *refs):
    din_ref, dout_ref, rows_ref, grad_ref, hidden_ref, gate_ref, up_ref, sems = refs[-8:]

    starts = range(0, rows_ref.shape[0], tile)
    first = pl.program_id(0) == 0

    def copies(rows_from, grad_from, index):
        part = pl.ds(index * tile, tile)
        return [
            pltpu.make_async_copy(rows_from.at[part, :], rows_ref.at[part, :], sems.at[0, index]),
            pltpu.make_async_copy(grad_from.at[part, :], grad_ref.at[part, :], sems.at[1, index]),
        ]

    def fetch(rows_from, grad_from):
        for index in range(len(starts)):
            for copy in copies(rows_from, grad_from, index):
                copy.start()

    @pl.when(first & (core_ref[0, 0] == 0))
    def _():
        fetch(here_ref, there_ref)

    @pl.when(first & (core_ref[0, 0] != 0))
    def _():
        fetch(there_ref, here_ref)

    def every_tile(waits):
        for index, start in enumerate(starts):
            if waits:
                for copy in copies(here_ref, there_ref, index):
                    copy.wait()
            part = pl.ds(start, tile)
            rows = rows_ref[part, :]
            hidden, gate_grad, up_grad = gelu_parts(
                dot(rows, in_ref[0]), dot(rows, in_ref[1]), dot(grad_ref[part, :], out_ref[...])
            )
            hidden_ref[part, :] = hidden.astype(LOW)
            gate_ref[part, :] = gate_grad.astype(LOW)
            up_ref[part, :] = up_grad.astype(LOW)

    pl.when(first)(lambda: every_tile(True))
    pl.when(jnp.logical_not(first))(lambda: every_tile(False))
    dout_ref[...] = cols_dot(grad_ref[...], hidden_ref[...])
    din_ref[:, 0, :] = cols_dot(rows_ref[...], gate_ref[...])
    din_ref[:, 1, :] = cols_dot(rows_ref[...], up_ref[...])


def heavy_weights(core, here, there, weight_in, weight_out, first_block, count_blocks, done):
    count, width = here.shape
    hidden = weight_out.shape[1]
    cols = 256
    tile = 512 if count % 512 == 0 else count
    out_block = pl.BlockSpec((width, cols), lambda i: (0, first_block + i))
    in_block = pl.BlockSpec((width, 2, cols), lambda i: (0, 0, first_block + i))
    return pl.pallas_call(
        lambda *refs: heavy_weights_kernel(tile, *refs),
        grid=(count_blocks,),
        in_specs=[
            pl.BlockSpec(memory_space=pltpu.SMEM),
            pl.BlockSpec(memory_space=pl.ANY),
            pl.BlockSpec(memory_space=pl.ANY),
            pl.BlockSpec((2, width, cols), lambda i: (0, 0, first_block + i)),
            out_block,
        ]
        + [pl.BlockSpec(memory_space=pl.ANY)] * len(done),
        out_specs=[in_block, out_block],
        out_shape=[like((width, 2, hidden), WIDE), like((width, hidden), WIDE)],
        scratch_shapes=[pltpu.VMEM((count, width), LOW)] * 2
        + [pltpu.VMEM((count, cols), LOW)] * 3
        + [pltpu.SemaphoreType.DMA((2, count // tile))],
        input_output_aliases={5 + i: i for i in range(len(done))},
        compiler_params=params(60),
        cost_estimate=cost(4 + 9 * count_blocks * count / 3072),
        name="heavy_weights",
    )(core, here, there, weight_in, weight_out, *done)


def bit_pairs(bit):
    return [(i, i ^ (1 << bit)) for i in range(lax.axis_size("seq"))]


def bit_here(bit):
    return (lax.axis_index("seq") >> bit) & 1


def after(value, *others):
    return lax.optimization_barrier((value,) + others)[0]


def scatter_start(value, bit):
    halves = value.reshape(2, value.shape[0] // 2, value.shape[1])
    mine = bit_here(bit)
    sent = lax.dynamic_index_in_dim(halves, 1 - mine, 0, keepdims=False)
    kept = lax.dynamic_index_in_dim(halves, mine, 0, keepdims=False)
    return kept, lax.ppermute(sent, "seq", bit_pairs(bit))


def scatter_end(started, *others):
    kept, got = started
    got = after(got, *others)
    return (kept.astype(WIDE) + got.astype(WIDE)).astype(LOW)


def gather_start(value, bit):
    return value, lax.ppermute(value, "seq", bit_pairs(bit)), bit_here(bit)


def gather_end(started, *others):
    value, got, mine = started
    got = after(got, *others)
    return jnp.where(
        mine == 0,
        jnp.concatenate([value, got], axis=0),
        jnp.concatenate([got, value], axis=0),
    )


def interleave(parts, blocks):
    cut = [p.reshape(blocks, -1, p.shape[1]) for p in parts]
    return jnp.concatenate(cut, axis=1).reshape(-1, parts[0].shape[1])


def apart(value, blocks, rows):
    cut = value.reshape(blocks, -1, value.shape[1])
    marks = [sum(rows[:i]) // blocks for i in range(len(rows) + 1)]
    return [
        cut[:, marks[i] : marks[i + 1]].reshape(-1, value.shape[1]) for i in range(len(rows))
    ]


def in_order(bit_ref, mine_ref, got_ref, body):
    pl.when(bit_ref[0, 0] == 0)(lambda: body(mine_ref, got_ref))
    pl.when(bit_ref[0, 0] != 0)(lambda: body(got_ref, mine_ref))


def finish_call(kernel, bit, mine, got, shapes, name):
    shapes = [like(shape, WIDE) for shape in shapes]
    return pl.pallas_call(
        kernel,
        in_specs=[
            pl.BlockSpec(memory_space=pltpu.SMEM),
            pl.BlockSpec(memory_space=pltpu.VMEM),
            pl.BlockSpec(memory_space=pltpu.VMEM),
        ],
        out_shape=shapes,
        compiler_params=params(),
        name=name,
    )(bit_here(bit).astype(jnp.int32).reshape(1, 1), mine, got)


def feed_in_kernel(bit_ref, mine_ref, got_ref, in_ref):
    width, _, hidden = in_ref.shape

    def body(*halves):
        for kind, ref in enumerate(halves):

            def store(rows, cols, value, kind=kind):
                in_ref[rows, kind, cols] = value.astype(WIDE)

            unpack_wide(store, ref, 0, width, hidden - ref.shape[1])

    in_order(bit_ref, mine_ref, got_ref, body)


def outs_kernel(bit_ref, mine_ref, got_ref, feed_ref, light_ref, heavy_ref):
    width, hidden = feed_ref.shape

    def body(first_ref, second_ref):
        half, cols = first_ref.shape

        def store(rows, lanes, value):
            feed_ref[rows, lanes] = value.astype(WIDE)

        unpack_wide(store, first_ref, 0, width, hidden - cols)
        start = width * hidden // cols
        light_ref[: half - start, :] = first_ref[start:, :].astype(WIDE)
        rest = width - (half - start)
        light_ref[half - start :, :] = second_ref[:rest, :].astype(WIDE)
        heavy_ref[...] = second_ref[rest:, :].astype(WIDE)

    in_order(bit_ref, mine_ref, got_ref, body)


def kinds_kernel(bit_ref, mine_ref, got_ref, wide_ref):
    def body(first_ref, second_ref):
        half = first_ref.shape[0]
        wide_ref[:half, :] = first_ref[...].astype(WIDE)
        wide_ref[half:, :] = second_ref[...].astype(WIDE)

    in_order(bit_ref, mine_ref, got_ref, body)


def other_core(value):
    return lax.ppermute(value, "mp", [(0, 1), (1, 0)])


def to_neighbours(first, last):
    peers = lax.axis_size("seq")
    up = [(i, i + 1) for i in range(peers - 1)]
    down = [(i + 1, i) for i in range(peers - 1)]
    return lax.ppermute(last, "seq", up), lax.ppermute(first, "seq", down)


def exchange(pairs):
    return lax.all_to_all(pairs, "seq", split_axis=0, concat_axis=0, tiled=True)


def by_kind(weights):
    return weights.transpose(1, 0, 2)


def shards(
    tokens,
    out_grad,
    gains,
    routers,
    light_query_key_value_weight,
    light_attention_output_weight,
    heavy_qkv,
    heavy_out,
    light_feedforward_input_weight,
    light_feedforward_output_weight,
    heavy_mlp_in,
    heavy_mlp_out,
    routed_queries,
    routed_keys,
    routed_mlp,
    block_counts,
):
    seq_count, local_len, width = tokens.shape
    seq_devices = lax.axis_size("seq")
    row_base = lax.axis_index("seq") * local_len
    capacity = routed_queries.shape[1]
    light_cols = light_query_key_value_weight.shape[2]
    gain_rows, router_rows = gains.T, routers.T
    slot_ids = jnp.arange(capacity, dtype=jnp.int32)[None, :, None]
    rows = jnp.stack([routed_queries, routed_keys, routed_mlp], axis=2) - row_base
    valid = (slot_ids < block_counts).astype(jnp.int32)
    slots = jnp.concatenate([rows, valid], axis=2)
    place = jnp.stack([row_base, jnp.int32(seq_devices * local_len)]).astype(jnp.int32)[None, :]
    core = lax.axis_index("mp").astype(jnp.int32).reshape(1, 1)
    light_weights = by_kind(light_query_key_value_weight)
    heavy_weights_qkv = by_kind(heavy_qkv)

    before, behind = to_neighbours(tokens[:, :WIN], tokens[:, local_len - WIN :])
    low, qkv, pairs, raw, gate = front(
        tokens, gain_rows, router_rows, slots, light_weights, heavy_weights_qkv, seq_devices
    )
    pair = exchange(after(pairs, before, behind)).reshape(seq_devices * capacity, -1)
    mix, attn, lse, query, window = light_forward(
        place, qkv, before, behind, gain_rows, light_weights, light_attention_output_weight
    )
    kept, pair_mix = heavy_forward(after(pair, attn))
    mix_pairs = exchange(pair_mix.reshape(seq_devices, capacity, LANES))
    light_in = by_kind(after(light_feedforward_input_weight, kept))
    heavy_in = by_kind(after(heavy_mlp_in, kept))
    own, heavy_mix = combine(after(mix_pairs, light_in, heavy_in), attn, heavy_out, slots, gate)
    other = other_core(own)
    low_two, rows, slot, ship, gate_two = mlp_slots(
        core, tokens, own, other, out_grad, gain_rows, router_rows, slots
    )
    all_slots = seq_count * capacity * seq_devices
    gather_heavy = 2 * all_slots * width < 4 * (heavy_mlp_in.size + heavy_mlp_out.size)
    here = lax.all_gather(ship, "seq", axis=1, tiled=True) if gather_heavy else ship
    part, feed_grads, mlp = feed(
        low_two, rows, slot, gate_two, out_grad, slots, light_in, light_feedforward_output_weight,
        heavy_in, heavy_mlp_out, light_cols,
    )
    beyond, mlp_other = other_core(part), other_core(mlp)
    bits = (seq_devices - 1).bit_length()
    blocks = 1 << (bits - 2)
    first_going = scatter_start(feed_grads[:2].reshape(-1, light_cols), 0)
    mixed, middle_grad, mix_grad, grad_pairs, out_grads, small, query_logit = middle_back(
        tokens, own, other, part, beyond, out_grad, gain_rows, router_rows, slots, gate, mlp,
        mlp_other, mix, heavy_mix, light_attention_output_weight, heavy_out, feed_grads[2], seq_devices,
    )
    pair_grad = exchange(grad_pairs).reshape(seq_devices * capacity, -1)
    local, early, late = light_backward(place, query, window, lse, mix_grad)
    first_wave = scatter_end(first_going, local)
    lead, tail = to_neighbours(early, late)
    triple = heavy_backward(pair, kept, after(pair_grad, local, first_wave))
    triple_pairs = exchange(triple.reshape(seq_devices, capacity, -1))
    second_going = scatter_start(after(out_grads, triple), 1)
    light_sums, light_part = light_project(after(local, triple), low, light_weights)
    second_wave = scatter_end(second_going, light_part)
    heavy_grads, light_grads, low_part, logit = heavy_project(
        light_part, low, after(triple_pairs, second_wave), heavy_weights_qkv, slots, gate, raw,
        query_logit, lead, tail, light_weights, light_sums,
    )
    heavy_going = scatter_start(heavy_grads.reshape(-1, light_cols), 1)
    light_going = scatter_start(light_grads.reshape(-1, light_cols), 0)
    second_going = scatter_start(after(second_wave, low_part), 0)
    first_going = scatter_start(after(first_wave, low_part), 1)
    low_other, logit_other = other_core(low_part), other_core(logit)
    here = after(here, low_part)
    there = other_core(here).reshape(-1, width)
    here = here.reshape(-1, width)
    blocks_done = [0]
    heavy_sums = []

    def heavy_piece(count, *others):
        heavy_sums[:] = heavy_weights(
            core, after(here, *others), there, heavy_in, heavy_mlp_out, blocks_done[0], count, heavy_sums
        )
        blocks_done[0] += count
        return heavy_sums[1]

    input_grad, small = input_back(
        low_part, low_other, logit, logit_other, gate, slots, tokens, gain_rows,
        router_rows, middle_grad, small,
    )
    small_rows = small.astype(LOW).reshape(-1, light_cols)
    small_rows = jnp.pad(small_rows, ((0, 16 * blocks - small_rows.shape[0]), (0, 0)))
    small_got = lax.ppermute(small_rows, "seq", bit_pairs(1))
    second_wave = scatter_end(second_going, input_grad)
    first_wave = scatter_end(first_going, input_grad)
    early_sizes = [first_wave.shape[0], second_wave.shape[0]]
    wave = interleave([first_wave, second_wave], blocks)
    going = scatter_start(wave, 2)
    mark = heavy_piece(2, input_grad, wave)
    wave = scatter_end(going, mark)
    heavy_wave = scatter_end(heavy_going, mark)
    light_wave = scatter_end(light_going, mark)
    light_going = scatter_start(light_wave, 1)
    small_rows = scatter_end((small_rows, small_got), mark)
    for bit in range(3, bits - 1):
        wave = scatter_end(scatter_start(wave, bit))
    going = scatter_start(wave, bits - 1)
    heavy_going = scatter_start(heavy_wave, 0)
    small_got = lax.ppermute(small_rows, "seq", bit_pairs(0))
    mark = heavy_piece(1, wave, heavy_wave, light_wave, small_rows)
    wave = scatter_end(going, mark)
    heavy_wave = scatter_end(heavy_going, mark)
    light_wave = scatter_end(light_going, mark)
    small_rows = scatter_end((small_rows, small_got), mark)
    for bit in reversed(range(4, bits)):
        wave = gather_end(gather_start(wave, bit))
    going = gather_start(wave, 3)
    late_wave = [light_wave, heavy_wave, small_rows]
    late_sizes = [p.shape[0] for p in late_wave]
    late_wave = interleave(late_wave, blocks)
    late_going = scatter_start(late_wave, 2)
    mark = heavy_piece(1, late_wave, wave)
    wave = gather_end(going, mark)
    late_wave = scatter_end(late_going, mark)
    for bit in range(3, bits - 1):
        late_wave = scatter_end(scatter_start(late_wave, bit))
    going = gather_start(wave, 2)
    late_going = scatter_start(late_wave, bits - 1)
    mark = heavy_piece(1, late_wave, wave)
    wave = apart(gather_end(going, mark), blocks, early_sizes)
    going = [gather_start(p, bit) for p, bit in zip(wave, (1, 0))]
    late_wave = scatter_end(late_going, mark)
    for bit in reversed(range(4, bits)):
        late_wave = gather_end(gather_start(late_wave, bit))
    late_going = gather_start(late_wave, 3)
    mark = heavy_piece(1, late_wave, *wave)
    wave = [gather_end(p, mark) for p in going]
    early_halves = [(p, lax.ppermute(p, "seq", bit_pairs(bit))) for p, bit in zip(wave, (0, 1))]
    late_wave = gather_end(late_going, mark)
    late_going = gather_start(late_wave, 2)
    mark = heavy_piece(1, late_wave, *wave)
    late_wave = apart(gather_end(late_going, mark), blocks, late_sizes)
    small_sum = late_wave.pop().astype(WIDE)
    late_going = [gather_start(p, bit) for p, bit in zip(late_wave, (1, 0))]
    early_halves = [(after(p, *late_wave), after(got, mark)) for p, got in early_halves]
    hidden = light_feedforward_output_weight.shape[1]
    square, kinds = (width, light_cols), [(3 * width, light_cols)]
    (feed_in,) = finish_call(feed_in_kernel, 0, *early_halves[0], [(width, 2, hidden)], "feed_in")
    feed_out, light_out_sum, heavy_out_sum = finish_call(
        outs_kernel, 1, *early_halves[1], [(width, hidden), square, square], "outs"
    )
    late_wave = [gather_end(p, feed_in, feed_out) for p in late_going]
    late_halves = [
        (p, lax.ppermute(p, "seq", bit_pairs(bit))) for p, bit in zip(late_wave, (0, 1))
    ]
    mark = heavy_piece(1, *late_wave)
    late_halves = [(p, after(got, mark)) for p, got in late_halves]
    heavy_in_grad, heavy_out_grad = heavy_sums
    if not gather_heavy:
        sums = [heavy_in_grad[:, 0], heavy_in_grad[:, 1], heavy_out_grad]
        sums = [p.astype(LOW) for p in sums]
        for bit in range(bits):
            sums = [scatter_end(scatter_start(p, bit)) for p in sums]
        for bit in reversed(range(bits)):
            sums = [gather_end(gather_start(p, bit)) for p in sums]
        heavy_in_grad = jnp.stack(sums[:2], axis=1).astype(WIDE)
        heavy_out_grad = sums[2].astype(WIDE)
    (light_sum,) = finish_call(kinds_kernel, 0, *late_halves[0], kinds, "light_sum")
    (heavy_sum,) = finish_call(kinds_kernel, 1, *late_halves[1], kinds, "heavy_sum")
    small_sum = small_sum[: 8 * width // light_cols].reshape(8, width)
    return (
        mixed,
        input_grad,
        light_sum.reshape(3, width, light_cols).transpose(1, 0, 2),
        light_out_sum,
        heavy_sum.reshape(3, width, light_cols).transpose(1, 0, 2),
        heavy_out_sum,
        feed_in,
        feed_out,
        heavy_in_grad,
        heavy_out_grad,
        jnp.stack([small_sum[2], small_sum[0]], axis=1),
        jnp.stack([small_sum[3], small_sum[4], small_sum[1]], axis=1),
    )


def solution(mesh):
    rows = P(None, "seq", None)
    by_column = P(None, None, "mp")
    by_hidden = P(None, "mp")
    slots = P(None, "seq")
    weights = (by_column, by_hidden) * 4
    return jax.shard_map(
        shards,
        mesh=mesh,
        in_specs=(rows, rows, P(), P()) + weights + (slots, slots, slots, rows),
        out_specs=(rows, rows) + weights + (P(), P()),
        check_vma=False,
    )
```

```python
import math

import jax
import jax.numpy as jnp
from jax import lax
from jax.experimental import pallas as pl
from jax.experimental.pallas import tpu as pltpu
from jax.sharding import PartitionSpec as P

LHD = 96
HHD = 64
WIN = 128
LANES = 128

EPSILON = 1e-06
MASKED = -1e30
MARK = 1e30
EXACT = lax.Precision.HIGHEST
LOW = jnp.bfloat16
WIDE = jnp.float32

ROW_QUERY, ROW_KEY, ROW_MLP, OK_QUERY, OK_KEY, OK_MLP = range(6)


def lanes_of(shape):
    return lax.broadcasted_iota(jnp.int32, shape, len(shape) - 1)


def dot(a, b):
    return jnp.dot(a, b, preferred_element_type=WIDE)


def rows_dot(a, b):
    return lax.dot_general(a, b, (((1,), (1,)), ((), ())), preferred_element_type=WIDE)


def cols_dot(a, b):
    return lax.dot_general(a, b, (((0,), (0,)), ((), ())), preferred_element_type=WIDE)


def rms_of(values):
    return lax.rsqrt(jnp.mean(values * values, axis=-1, keepdims=True) + EPSILON)


def column(values, index):
    return values[:, index : index + 1]


def columns(shape, *parts):
    lane = lanes_of(shape)
    out = jnp.zeros(shape, WIDE)
    for index, part in enumerate(parts):
        out = jnp.where(lane == index, part, out)
    return out


def hot_rows(slots, index, length):
    rows = column(slots, index)
    return (lanes_of((rows.shape[0], length)) == rows).astype(WIDE)


def place_rows(hot, values):
    high = values.astype(LOW)
    rest = (values - high.astype(WIDE)).astype(LOW)
    return cols_dot(hot, high) + cols_dot(hot, rest)


def exact_place(hot, values):
    return lax.dot_general(
        hot, values, (((0,), (0,)), ((), ())), precision=EXACT, preferred_element_type=WIDE
    )


def exact_pick(hot, values):
    return jnp.dot(hot, values, precision=EXACT, preferred_element_type=WIDE)


def row_dots(values, vector):
    return jnp.sum(values * vector, axis=-1, keepdims=True)


def norm_back(values, factor, weighted):
    inner = jnp.mean(weighted * values, axis=-1, keepdims=True)
    return factor * weighted - values * (factor * factor * factor) * inner


def gelu_parts(gate, up, hidden_grad):
    root = math.sqrt(2.0 / math.pi)
    cube = 0.044715 * root
    square = gate * gate
    bend = jnp.tanh(gate * (root + cube * square))
    half = 0.5 + 0.5 * bend
    value = gate * half
    slope = half + gate * (1.0 - bend * bend) * (0.5 * root + (1.5 * cube) * square)
    return value * up, slope * up * hidden_grad, value * hidden_grad


def merge_heads(ref, rows, heads):
    tiles = []
    for head in range(0, heads, 2):
        first = ref[head, :rows, :].astype(WIDE)
        second = ref[head + 1, :rows, :].astype(WIDE)
        lane = lanes_of(first.shape)
        tiles.append(jnp.where(lane < HHD, first, pltpu.roll(second, HHD, 1)))
    return jnp.concatenate(tiles, axis=1)


def merge_upper(ref, rows, heads):
    tiles = []
    for head in range(0, heads, 2):
        first = ref[head, :rows, :].astype(WIDE)
        second = ref[head + 1, :rows, :].astype(WIDE)
        lane = lanes_of(first.shape)
        tiles.append(jnp.where(lane < HHD, pltpu.roll(first, HHD, 1), second))
    return jnp.concatenate(tiles, axis=1)


def head_low(values, head):
    tile = values[:, head // 2 * LANES : (head // 2 + 1) * LANES]
    return tile if head % 2 == 0 else pltpu.roll(tile, HHD, 1)


def head_high(values, head):
    tile = values[:, head // 2 * LANES : (head // 2 + 1) * LANES]
    return tile if head % 2 == 1 else pltpu.roll(tile, HHD, 1)


def fold(values):
    half = values.shape[0] // 2
    lane = lanes_of((half, LANES))
    return jnp.where(lane < HHD, values[:half], pltpu.roll(values[half:], HHD, 1))


def unfold(folded):
    lane = lanes_of(folded.shape)
    return jnp.concatenate(
        [
            jnp.where(lane < HHD, folded, 0.0),
            jnp.where(lane < HHD, pltpu.roll(folded, HHD, 1), 0.0),
        ],
        axis=0,
    )


def merge_folded(ref, start, heads):
    tiles = []
    for head in range(0, heads, 2):
        first = ref[head, start:, :].astype(WIDE)
        second = ref[head + 1, start:, :].astype(WIDE)
        lane = lanes_of(first.shape)
        upper = jnp.where(lane < HHD, first, pltpu.roll(second, HHD, 1))
        lower = jnp.where(lane < HHD, pltpu.roll(first, HHD, 1), second)
        tiles.append(jnp.concatenate([upper, lower], axis=0))
    return jnp.concatenate(tiles, axis=1)


def spread_matrix(heads):
    row = lax.broadcasted_iota(jnp.int32, (heads * LHD, heads * LANES), 0)
    lane = lanes_of((heads * LHD, heads * LANES))
    inner = lane & (LANES - 1)
    hit = (row == (lane >> 7) * LHD + inner) & (inner < LHD)
    return hit.astype(WIDE).astype(LOW)


def params(mib=56):
    return pltpu.CompilerParams(vmem_limit_bytes=mib * 2**20)


def cost(microseconds):
    return pl.CostEstimate(
        flops=int(microseconds * 2e7), bytes_accessed=2**10, transcendentals=0
    )


def whole(array):
    zeros = (0,) * array.ndim
    return pl.BlockSpec(array.shape, lambda *_: zeros, pipeline_mode=pl.Buffered(1))


def each(array):
    rest = (0,) * (array.ndim - 1)
    return pl.BlockSpec((1,) + array.shape[1:], lambda s: (s,) + rest)


def like(shape, kind):
    return jax.ShapeDtypeStruct(shape, kind)


def front_kernel(
    tokens_ref, gains_ref, routers_ref, slots_ref, heavy_ref, low_ref, pair_ref, raw_ref, gate_ref,
):
    inputs = tokens_ref[0].astype(WIDE)
    length = inputs.shape[0]
    normed = inputs * rms_of(inputs) * gains_ref[0:1, :]
    low = normed.astype(LOW)
    low_ref[0] = low
    slots = slots_ref[0]
    hot_query = hot_rows(slots, ROW_QUERY, length)
    hot_key = hot_rows(slots, ROW_KEY, length)
    logits = columns(
        (length, LANES),
        row_dots(normed, routers_ref[0:1, :]),
        row_dots(normed, routers_ref[1:2, :]),
    )
    query_gate = jax.nn.sigmoid(column(exact_pick(hot_query, logits), 0))
    key_gate = jax.nn.sigmoid(column(exact_pick(hot_key, logits), 1))
    gate_ref[0] = columns((slots.shape[0], LANES), query_gate, key_gate)
    query_in = dot(hot_query.astype(LOW), low).astype(LOW)
    key_in = dot(hot_key.astype(LOW), low).astype(LOW)
    query = dot(query_in, heavy_ref[0]).astype(LOW).astype(WIDE)
    key = dot(key_in, heavy_ref[1]).astype(LOW).astype(WIDE)
    raw = dot(key_in, heavy_ref[2])
    raw_ref[0] = raw
    value = (key_gate * raw).astype(LOW).astype(WIDE)
    value = jnp.where(column(slots, OK_KEY) > 0, value, MARK)
    cap = slots.shape[0]
    lane = lanes_of((cap, LANES))
    for head in range(raw.shape[1] // HHD):
        both = jnp.where(lane < HHD, head_low(query, head), head_high(key, head))
        pair_ref[head, :cap, :] = both.astype(LOW)
        pair_ref[head, cap:, :] = fold(head_low(value, head)).astype(LOW)


def front(tokens, gains, routers, slots, heavy, seq_devices):
    seqs, length, width = tokens.shape
    cap = slots.shape[1]
    heavy_cols = heavy.shape[2]
    heads = heavy_cols // HHD
    shapes = [
        like(tokens.shape, LOW),
        like((seq_devices, 3 * cap // 2, LANES), LOW),
        like((seqs, cap, heavy_cols), WIDE),
        like((seqs, cap, LANES), WIDE),
    ]
    specs = [each(s) for s in shapes]
    specs[1] = pl.BlockSpec((heads, 3 * cap // 2, LANES), lambda s: (s, 0, 0))
    return pl.pallas_call(
        front_kernel,
        grid=(seqs,),
        in_specs=[each(tokens), whole(gains), whole(routers), each(slots), whole(heavy)],
        out_specs=specs,
        out_shape=shapes,
        compiler_params=params(),
        cost_estimate=cost(8),
        name="front",
    )(tokens, gains, routers, slots, heavy)


def window_bias(block, length, base, total):
    row = lax.broadcasted_iota(jnp.int32, (WIN, 3 * WIN), 0)
    col = lanes_of((WIN, 3 * WIN))
    place = base + (block - 1) * WIN + col
    near = jnp.abs(col - WIN - row) < WIN
    return jnp.where(near & (place >= 0) & (place < total), 0.0, MASKED)


def light_forward_kernel(
    scale, place_ref, low_ref, before_ref, after_ref, gains_ref, weight_ref, out_ref,
    mix_ref, attn_ref, lse_ref, query_ref, window_ref, wide_ref,
):
    length, heads = low_ref.shape[1], weight_ref.shape[2] // LHD
    spread = spread_matrix(heads)

    def heads_of(rows, kind):
        projected = dot(rows, weight_ref[kind]).astype(LOW)
        return dot(projected, spread).astype(LOW)

    query_ref[0] = heads_of(low_ref[0], 0)
    edges = ((before_ref, slice(0, WIN)), (after_ref, slice(WIN + length, 2 * WIN + length)))
    for ref, rows in edges:
        inputs = ref[0].astype(WIDE)
        low = (inputs * rms_of(inputs) * gains_ref[0:1, :]).astype(LOW)
        for kind in range(2):
            window_ref[0, kind, rows, :] = heads_of(low, 1 + kind)
    for kind in range(2):
        window_ref[0, kind, WIN : WIN + length, :] = heads_of(low_ref[0], 1 + kind)
    for block in range(length // WIN):
        rows = slice(block * WIN, (block + 1) * WIN)
        near = slice(block * WIN, (block + 3) * WIN)
        bias = window_bias(block, length, place_ref[0, 0], place_ref[0, 1])
        lanes = [slice(head * LANES, (head + 1) * LANES) for head in range(heads)]
        scores = jnp.concatenate(
            [
                rows_dot(query_ref[0, rows, at], window_ref[0, 0, near, at]) * scale + bias
                for at in lanes
            ],
            axis=0,
        )
        top = jnp.max(scores, axis=-1, keepdims=True)
        expo = jnp.exp(scores - top)
        total = jnp.sum(expo, axis=-1, keepdims=True)
        lse = top + jnp.log(total)
        share = 1.0 / total
        expo = expo.astype(LOW)
        kept = []
        for head, at in enumerate(lanes):
            mine = slice(head * WIN, (head + 1) * WIN)
            mixed = dot(expo[mine], window_ref[0, 1, near, at]) * share[mine]
            wide_ref[rows, at] = mixed.astype(LOW)
            kept.append(lse[mine])
        lse_ref[0, rows, :] = columns((WIN, LANES), *kept)
    mix = rows_dot(wide_ref[...], spread).astype(LOW)
    mix_ref[0] = mix
    attn_ref[0] = rows_dot(mix, out_ref[...])


def light_forward(place, low, before, after, gains, weight, weight_out):
    seqs, length, _ = low.shape
    light_cols = weight.shape[2]
    heads = light_cols // LHD
    shapes = [
        like((seqs, length, light_cols), LOW),
        like((seqs, length, weight_out.shape[0]), WIDE),
        like((seqs, length, LANES), WIDE),
        like((seqs, length, heads * LANES), LOW),
        like((seqs, 2, length + 2 * WIN, heads * LANES), LOW),
    ]
    return pl.pallas_call(
        lambda *refs: light_forward_kernel(1.0 / math.sqrt(LHD), *refs),
        grid=(seqs,),
        in_specs=[
            pl.BlockSpec(memory_space=pltpu.SMEM),
            each(low),
            each(before),
            each(after),
            whole(gains),
            whole(weight),
            whole(weight_out),
        ],
        out_specs=[each(s) for s in shapes],
        out_shape=shapes,
        scratch_shapes=[pltpu.VMEM((length, heads * LANES), LOW)],
        compiler_params=params(),
        cost_estimate=cost(15),
        name="light_forward",
    )(place, low, before, after, gains, weight, weight_out)


def light_backward_kernel(
    scale, place_ref, query_ref, window_ref, lse_ref, grad_ref, local_ref, early_ref, late_ref, *scratch
):
    wide_ref, dkey_ref, dvalue_ref = scratch
    length, light_cols = grad_ref.shape[1:]
    heads = light_cols // LHD
    spread = spread_matrix(heads)
    grad = dot(grad_ref[0], spread).astype(LOW)
    dkey_ref[...] = jnp.zeros_like(dkey_ref)
    dvalue_ref[...] = jnp.zeros_like(dvalue_ref)
    for block in range(length // WIN):
        rows = slice(block * WIN, (block + 1) * WIN)
        near = slice(block * WIN, (block + 3) * WIN)
        bias = window_bias(block, length, place_ref[0, 0], place_ref[0, 1])
        lse = lse_ref[0, rows, :]
        lanes = [slice(head * LANES, (head + 1) * LANES) for head in range(heads)]
        scores = jnp.concatenate(
            [
                rows_dot(query_ref[0, rows, at], window_ref[0, 0, near, at]) * scale
                + (bias - column(lse, head))
                for head, at in enumerate(lanes)
            ],
            axis=0,
        )
        prob_grad = jnp.concatenate(
            [rows_dot(grad[rows, at], window_ref[0, 1, near, at]) for at in lanes], axis=0
        )
        probs = jnp.exp(scores)
        delta = jnp.sum(probs * prob_grad, axis=-1, keepdims=True)
        score_grad = (probs * (prob_grad - delta)).astype(LOW)
        probs = probs.astype(LOW)
        for head, at in enumerate(lanes):
            mine = slice(head * WIN, (head + 1) * WIN)
            part = score_grad[mine]
            wide_ref[rows, at] = (dot(part, window_ref[0, 0, near, at]) * scale).astype(LOW)
            dkey_ref[near, at] += cols_dot(part, query_ref[0, rows, at]) * scale
            dvalue_ref[near, at] += cols_dot(probs[mine], grad[rows, at])
    local_ref[0, 0] = rows_dot(wide_ref[...], spread).astype(LOW)
    for kind, ref in ((1, dkey_ref), (2, dvalue_ref)):
        all_rows = rows_dot(ref[...].astype(LOW), spread).astype(LOW)
        early_ref[0, kind - 1] = all_rows[:WIN]
        local_ref[0, kind] = all_rows[WIN : WIN + length]
        late_ref[0, kind - 1] = all_rows[WIN + length :]


def light_backward(place, query, window, lse, grad):
    seqs, length, light_cols = grad.shape
    edge = like((seqs, 2, WIN, light_cols), LOW)
    shapes = [like((seqs, 3, length, light_cols), LOW), edge, edge]
    return pl.pallas_call(
        lambda *refs: light_backward_kernel(1.0 / math.sqrt(LHD), *refs),
        grid=(seqs,),
        in_specs=[
            pl.BlockSpec(memory_space=pltpu.SMEM),
            each(query),
            each(window),
            each(lse),
            each(grad),
        ],
        out_specs=[each(s) for s in shapes],
        out_shape=shapes,
        scratch_shapes=[
            pltpu.VMEM(query.shape[1:], LOW),
            pltpu.VMEM(window.shape[2:], WIDE),
            pltpu.VMEM(window.shape[2:], WIDE),
        ],
        compiler_params=params(),
        cost_estimate=cost(14),
        name="light_backward",
    )(place, query, window, lse, grad)


def heavy_forward_kernel(scale, pair_ref, query_ref, key_ref, value_ref, kept_ref, mix_ref):
    devices, rows, _ = pair_ref.shape
    cap = 2 * rows // 3
    tile = kept_ref.shape[0]

    @pl.when(pl.program_id(0) == 0)
    def _():
        def unpack(index, carry):
            lane = lanes_of((cap, LANES))
            at = pl.ds(pl.multiple_of(index * cap, 16), cap)
            both = pair_ref[index, :cap, :].astype(WIDE)
            value = unfold(pair_ref[index, cap:, :].astype(WIDE))
            unused = column(value, 0) > 0.5 * MARK
            bias = jnp.where(unused, MASKED, 0.0)
            query = jnp.where(lane < HHD, both * scale, jnp.where(lane == HHD, 1.0, 0.0))
            key = jnp.where(
                lane < HHD, pltpu.roll(both, HHD, 1), jnp.where(lane == HHD, bias, 0.0)
            )
            query_ref[at, :] = query.astype(LOW)
            key_ref[at, :] = key.astype(LOW)
            value_ref[at, :] = jnp.where(unused, 0.0, value).astype(LOW)
            return carry

        lax.fori_loop(0, devices, unpack, 0, unroll=devices <= 16)

    start = pl.multiple_of(pl.program_id(0) * tile, 16)
    scores = rows_dot(query_ref[pl.ds(start, tile), :], key_ref[...])
    top = jnp.max(scores, axis=-1, keepdims=True)
    expo = jnp.exp(scores - top)
    total = jnp.sum(expo, axis=-1, keepdims=True)
    mix = dot(expo.astype(LOW), value_ref[...]) / total
    lane = lanes_of(mix.shape)
    kept_ref[...] = jnp.where(lane < HHD, mix, top + jnp.log(total))
    for index in range(tile // cap):
        mix_ref[index] = fold(mix[index * cap : (index + 1) * cap]).astype(LOW)


def heavy_backward_kernel(
    scale, query_ref, key_ref, value_ref, kept_ref, grad_ref, triple_ref, dq_ref, dk_ref, dv_ref
):
    step = pl.program_id(0)
    devices, rows, _ = triple_ref.shape
    cap = 2 * rows // 3
    tile = kept_ref.shape[0]

    @pl.when(step == 0)
    def _():
        dk_ref[...] = jnp.zeros_like(dk_ref)
        dv_ref[...] = jnp.zeros_like(dv_ref)

    start = pl.multiple_of(step * tile, 16)
    query = query_ref[pl.ds(start, tile), :]
    grad = jnp.concatenate(
        [unfold(grad_ref[index].astype(WIDE)) for index in range(tile // cap)], axis=0
    )
    kept = kept_ref[...]
    lse = column(kept, HHD)
    delta = jnp.sum(kept * grad, axis=-1, keepdims=True)
    grad = grad.astype(LOW)
    probs = jnp.exp(rows_dot(query, key_ref[...]) - lse)
    prob_grad = rows_dot(grad, value_ref[...])
    score_grad = (probs * (prob_grad - delta)).astype(LOW)
    dq_ref[pl.ds(start, tile), :] = dot(score_grad, key_ref[...]) * scale
    dk_ref[...] += cols_dot(score_grad, query)
    dv_ref[...] += cols_dot(probs.astype(LOW), grad)

    @pl.when(step == pl.num_programs(0) - 1)
    def _():
        def pack(index, carry):
            lane = lanes_of((cap, LANES))
            at = pl.ds(pl.multiple_of(index * cap, 16), cap)
            moved = pltpu.roll(dk_ref[at, :], HHD, 1)
            triple_ref[index, :cap, :] = jnp.where(lane < HHD, dq_ref[at, :], moved).astype(LOW)
            triple_ref[index, cap:, :] = fold(dv_ref[at, :]).astype(LOW)
            return carry

        lax.fori_loop(0, devices, pack, 0, unroll=devices <= 16)


def query_tile(devices, cap):
    return 4 * cap if devices <= 32 else cap


def heavy_forward(pair):
    devices, rows, _ = pair.shape
    cap = 2 * rows // 3
    length, tile = devices * cap, query_tile(devices, cap)
    operand = like((length, LANES), LOW)
    shapes = [operand] * 3 + [
        like((length, LANES), WIDE),
        like((devices, cap // 2, LANES), LOW),
    ]
    return pl.pallas_call(
        lambda *refs: heavy_forward_kernel(1.0 / math.sqrt(HHD), *refs),
        grid=(length // tile,),
        in_specs=[whole(pair)],
        out_specs=[whole(operand)] * 3
        + [
            pl.BlockSpec((tile, LANES), lambda i: (i, 0)),
            pl.BlockSpec((tile // cap, cap // 2, LANES), lambda i: (i, 0, 0)),
        ],
        out_shape=shapes,
        compiler_params=params(60),
        cost_estimate=cost(7),
        name="heavy_forward",
    )(pair)


def heavy_backward(query, key, value, kept, grad):
    devices, half, _ = grad.shape
    cap = 2 * half
    length, tile = devices * cap, query_tile(devices, cap)
    triple = like((devices, cap + half, LANES), LOW)
    return pl.pallas_call(
        lambda *refs: heavy_backward_kernel(1.0 / math.sqrt(HHD), *refs),
        grid=(length // tile,),
        in_specs=[
            whole(query),
            whole(key),
            whole(value),
            pl.BlockSpec((tile, LANES), lambda i: (i, 0)),
            pl.BlockSpec((tile // cap, half, LANES), lambda i: (i, 0, 0)),
        ],
        out_specs=whole(triple),
        out_shape=triple,
        scratch_shapes=[pltpu.VMEM((length, LANES), WIDE)] * 3,
        compiler_params=params(60),
        cost_estimate=cost(10),
        name="heavy_backward",
    )(query, key, value, kept, grad)


def combine_kernel(pairs_ref, attn_ref, out_ref, slots_ref, gate_ref, part_ref, mix_ref):
    slots = slots_ref[0]
    mix = merge_folded(pairs_ref, 0, pairs_ref.shape[0]).astype(LOW)
    mix_ref[0] = mix
    rows = rows_dot(mix, out_ref[...])
    weight = jnp.where(column(slots, OK_QUERY) > 0, column(gate_ref[0], 0), 0.0)
    hot = hot_rows(slots, ROW_QUERY, attn_ref.shape[1]).astype(LOW)
    part_ref[0] = (attn_ref[0] + place_rows(hot, weight * rows)).astype(LOW)


def pair_spec(pairs, heads):
    return pl.BlockSpec((heads,) + pairs.shape[1:], lambda s: (s, 0, 0))


def combine(pairs, attn, weight_out, slots, gate):
    seqs, cap = slots.shape[:2]
    heavy_cols = weight_out.shape[1]
    shapes = [like(attn.shape, LOW), like((seqs, cap, heavy_cols), LOW)]
    return pl.pallas_call(
        combine_kernel,
        grid=(seqs,),
        in_specs=[
            pair_spec(pairs, heavy_cols // HHD),
            each(attn),
            whole(weight_out),
            each(slots),
            each(gate),
        ],
        out_specs=[each(s) for s in shapes],
        out_shape=shapes,
        compiler_params=params(),
        cost_estimate=cost(4),
        name="combine",
    )(pairs, attn, weight_out, slots, gate)


def slots_kernel(
    core_ref, tokens_ref, own_ref, other_ref, up_ref, gains_ref, routers_ref, slots_ref,
    low_ref, rows_ref, slot_ref, ship_ref, gate_ref,
):
    middle = tokens_ref[0].astype(WIDE) + own_ref[0].astype(WIDE) + other_ref[0].astype(WIDE)
    length = middle.shape[0]
    normed = middle * rms_of(middle) * gains_ref[1:2, :]
    low = normed.astype(LOW)
    low_ref[0] = low
    slots = slots_ref[0]
    hot = hot_rows(slots, ROW_MLP, length)
    logits = columns((length, LANES), row_dots(normed, routers_ref[2:3, :]))
    gate = jax.nn.sigmoid(column(exact_pick(hot, logits), 0))
    weight = jnp.where(column(slots, OK_MLP) > 0, gate, 0.0)
    hot = hot.astype(LOW)
    rows = dot(hot, low)
    slot = weight * dot(hot, up_ref[0])
    rows_ref[0] = rows.astype(LOW)
    slot_ref[0] = slot.astype(LOW)
    ship_ref[0] = jnp.where(core_ref[0, 0] == 0, rows, slot).astype(LOW)
    gate_ref[0] = columns((slots.shape[0], LANES), gate, weight)


def mlp_slots(core, tokens, own, other, up, gains, routers, slots):
    seqs, length, width = tokens.shape
    cap = slots.shape[1]
    shapes = [like(tokens.shape, LOW)]
    shapes += [like((seqs, cap, width), LOW)] * 3 + [like((seqs, cap, LANES), WIDE)]
    return pl.pallas_call(
        slots_kernel,
        grid=(seqs,),
        in_specs=[
            pl.BlockSpec(memory_space=pltpu.SMEM),
            each(tokens), each(own), each(other), each(up), whole(gains), whole(routers), each(slots),
        ],
        out_specs=[each(s) for s in shapes],
        out_shape=shapes,
        compiler_params=params(),
        cost_estimate=cost(5),
        name="mlp_slots",
    )(core, tokens, own, other, up, gains, routers, slots)


def pack_wide(ref, value):
    value = value.astype(LOW)
    rows, cols = value.shape[0], ref.shape[1]
    extra = value.shape[1] - cols
    group = rows * extra // cols
    ref[:rows, :] = value[:, :cols]
    for index in range(cols // extra):
        ref[rows:, index * extra : (index + 1) * extra] = value[
            index * group : (index + 1) * group, cols:
        ]


def unpack_wide(store, ref, start, rows, extra):
    cols = ref.shape[1]
    group = rows * extra // cols
    store(slice(0, rows), slice(0, cols), ref[start : start + rows, :])
    for index in range(cols // extra):
        store(
            slice(index * group, (index + 1) * group),
            slice(cols, cols + extra),
            ref[start + rows : start + rows + group, index * extra : (index + 1) * extra],
        )


def feed_kernel(
    low_ref, rows_ref, slot_ref, kept_ref, up_ref, slots_ref, in_ref, out_ref, heavy_in_ref,
    heavy_out_ref, part_ref, weights_ref, gate_ref, heavy_acc, back_acc, hidden_ref, dgate_ref, dup_ref,
):
    step = pl.program_id(0)
    seqs, length, width = up_ref.shape
    cap = slots_ref.shape[1]

    @pl.when(step == 0)
    def _():
        heavy_acc[...] = jnp.zeros_like(heavy_acc)
        back_acc[...] = jnp.zeros_like(back_acc)

    first, second, last = heavy_in_ref[0], heavy_in_ref[1], heavy_out_ref[...]
    rows = rows_ref[...]
    hidden, gate_grad, up_grad = gelu_parts(
        dot(rows, first), dot(rows, second), dot(slot_ref[...], last)
    )
    heavy_acc[...] += rows_dot(hidden.astype(LOW), last)
    back_acc[...] += rows_dot(gate_grad.astype(LOW), first) + rows_dot(up_grad.astype(LOW), second)

    @pl.when(step == pl.num_programs(0) - 1)
    def _():
        for s in range(seqs):
            here = slice(s * length, (s + 1) * length)
            mine = slice(s * cap, (s + 1) * cap)
            low = low_ref[s]
            hidden, gate_grad, up_grad = gelu_parts(
                dot(low, in_ref[0]), dot(low, in_ref[1]), dot(up_ref[s], out_ref[...])
            )
            hidden, gate_grad, up_grad = (
                hidden.astype(LOW),
                gate_grad.astype(LOW),
                up_grad.astype(LOW),
            )
            hidden_ref[here, :] = hidden
            dgate_ref[here, :] = gate_grad
            dup_ref[here, :] = up_grad
            hot = hot_rows(slots_ref[s], ROW_MLP, length).astype(LOW)
            kept = kept_ref[s]
            heavy_rows = heavy_acc[mine, :]
            part_ref[0, s] = (
                rows_dot(hidden, out_ref[...]) + place_rows(hot, column(kept, 1) * heavy_rows)
            ).astype(LOW)
            part_ref[1, s] = (
                rows_dot(gate_grad, in_ref[0])
                + rows_dot(up_grad, in_ref[1])
                + place_rows(hot, back_acc[mine, :])
            ).astype(LOW)
            gate_part = jnp.sum(dot(hot, up_ref[s]) * heavy_rows, axis=-1, keepdims=True)
            gate_ref[s] = columns((cap, LANES), column(kept, 0), gate_part)
        low = low_ref[...].reshape(seqs * length, width)
        up = up_ref[...].reshape(seqs * length, width)
        pack_wide(weights_ref.at[0], cols_dot(low, dgate_ref[...]))
        pack_wide(weights_ref.at[1], cols_dot(low, dup_ref[...]))
        pack_wide(weights_ref.at[2], cols_dot(up, hidden_ref[...]))


def feed(low, rows, slot, kept, up, slots, light_in, light_out, heavy_in, heavy_out, packed_cols):
    seqs, length, width = up.shape
    cap = slots.shape[1]
    hidden = light_out.shape[1]
    cols = 256
    rows, slot = rows.reshape(-1, width), slot.reshape(-1, width)
    shapes = [
        like((2, seqs, length, width), LOW),
        like((3, width * hidden // packed_cols, packed_cols), LOW),
        like((seqs, cap, LANES), WIDE),
    ]
    return pl.pallas_call(
        feed_kernel,
        grid=(heavy_out.shape[1] // cols,),
        in_specs=[
            whole(low),
            whole(rows),
            whole(slot),
            whole(kept),
            whole(up),
            whole(slots),
            whole(light_in),
            whole(light_out),
            pl.BlockSpec((2, width, cols), lambda i: (0, 0, i)),
            pl.BlockSpec((width, cols), lambda i: (0, i)),
        ],
        out_specs=[whole(s) for s in shapes],
        out_shape=shapes,
        scratch_shapes=[pltpu.VMEM((seqs * cap, width), WIDE)] * 2
        + [pltpu.VMEM((seqs * length, hidden), LOW)] * 3,
        compiler_params=params(),
        cost_estimate=cost(20),
        name="feed",
    )(low, rows, slot, kept, up, slots, light_in, light_out, heavy_in, heavy_out)


def middle_kernel(
    tokens_ref, own_ref, other_ref, part_ref, beyond_ref, up_ref, gains_ref, routers_ref, slots_ref,
    gate_ref, mlp_ref, mlp_other_ref, mix_ref, heavy_mix_ref, light_out_ref, heavy_out_ref, down_ref,
    mixed_ref, middle_ref, grad_ref, pair_ref, weights_ref, small_ref, logit_ref, weights_acc,
):
    step = pl.program_id(0)

    @pl.when(step == 0)
    def _():
        weights_acc[...] = jnp.zeros_like(weights_acc)
        small_ref[...] = jnp.zeros_like(small_ref)

    slots = slots_ref[0]
    cap = slots.shape[0]
    middle = tokens_ref[0].astype(WIDE) + own_ref[0].astype(WIDE) + other_ref[0].astype(WIDE)
    length = middle.shape[0]
    factor = rms_of(middle)
    scaled = middle * factor
    normed = scaled * gains_ref[1:2, :]
    mixed = middle + (part_ref[0, 0].astype(WIDE) + beyond_ref[0, 0].astype(WIDE))
    mixed_ref[0] = mixed.astype(LOW)
    gate = column(mlp_ref[0], 0)
    gate_grad = column(mlp_ref[0], 1) + column(mlp_other_ref[0], 1)
    logit_grad = jnp.where(column(slots, OK_MLP) > 0, gate_grad * gate * (1.0 - gate), 0.0)
    token_grad = column(
        exact_place(hot_rows(slots, ROW_MLP, length), columns((cap, LANES), logit_grad)), 0
    )
    normed_grad = (
        part_ref[1, 0].astype(WIDE) + beyond_ref[1, 0].astype(WIDE)
    ) + token_grad * routers_ref[2:3, :]
    small_ref[0:1, :] += jnp.sum(normed_grad * scaled, axis=0, keepdims=True)
    small_ref[1:2, :] += jnp.sum(token_grad * normed, axis=0, keepdims=True)
    middle_grad = up_ref[0].astype(WIDE) + norm_back(middle, factor, normed_grad * gains_ref[1:2, :])
    middle_ref[0] = middle_grad
    low = middle_grad.astype(LOW)
    hot = hot_rows(slots, ROW_QUERY, length).astype(LOW)
    up_rows = dot(hot, low)
    weight = jnp.where(column(slots, OK_QUERY) > 0, column(gate_ref[0], 0), 0.0)
    slot = (weight * up_rows).astype(LOW)
    heavy_rows = rows_dot(heavy_mix_ref[0], heavy_out_ref[...])
    logit_ref[0] = columns(
        (cap, LANES), jnp.sum(up_rows * heavy_rows, axis=-1, keepdims=True)
    )
    mix_grad = dot(slot, heavy_out_ref[...]).astype(LOW).astype(WIDE)
    for head in range(mix_grad.shape[1] // HHD):
        pair_ref[head] = fold(head_low(mix_grad, head)).astype(LOW)
    grad_ref[0] = dot(low, light_out_ref[...]).astype(LOW)
    weights_acc[0] += cols_dot(low, mix_ref[0])
    weights_acc[1] += cols_dot(slot, heavy_mix_ref[0])

    @pl.when(step == pl.num_programs(0) - 1)
    def _():
        start, rows = down_ref.shape[0], weights_acc.shape[1]
        weights_ref[:start, :] = down_ref[...]
        for kind in range(2):
            weights_ref[start + kind * rows : start + (kind + 1) * rows, :] = weights_acc[kind].astype(LOW)


def middle_back(
    tokens, own, other, part, beyond, up, gains, routers, slots, gate, mlp, mlp_other,
    mix, heavy_mix, light_out, heavy_out, down, seq_devices,
):
    seqs, length, width = tokens.shape
    cap = slots.shape[1]
    cols = light_out.shape[1]
    heads = heavy_out.shape[1] // HHD
    shapes = [
        like(tokens.shape, LOW),
        like(tokens.shape, WIDE),
        like((seqs, length, cols), LOW),
        like((seq_devices, cap // 2, LANES), LOW),
        like((down.shape[0] + 2 * width, cols), LOW),
        like((8, width), WIDE),
        like((seqs, cap, LANES), WIDE),
    ]
    specs = [
        each(shapes[0]), each(shapes[1]), each(shapes[2]), pair_spec(shapes[3], heads),
        whole(shapes[4]), whole(shapes[5]), each(shapes[6]),
    ]
    both = pl.BlockSpec((2, 1, length, width), lambda s: (0, s, 0, 0))
    return pl.pallas_call(
        middle_kernel,
        grid=(seqs,),
        in_specs=[
            each(tokens), each(own), each(other), both, both, each(up), whole(gains),
            whole(routers), each(slots), each(gate), each(mlp), each(mlp_other), each(mix),
            each(heavy_mix), whole(light_out), whole(heavy_out), whole(down),
        ],
        out_specs=specs,
        out_shape=shapes,
        scratch_shapes=[pltpu.VMEM((2, width, cols), WIDE)],
        compiler_params=params(),
        cost_estimate=cost(11),
        name="middle_back",
    )(
        tokens, own, other, part, beyond, up, gains, routers, slots, gate, mlp, mlp_other,
        mix, heavy_mix, light_out, heavy_out, down,
    )


def light_project_kernel(local_ref, low_ref, light_ref, grad_ref, part_ref):
    @pl.when(pl.program_id(0) == 0)
    def _():
        grad_ref[...] = jnp.zeros_like(grad_ref)

    low = low_ref[0]
    part = None
    for kind in range(3):
        rows = local_ref[0, kind]
        grad_ref[kind] += cols_dot(low, rows)
        more = rows_dot(rows, light_ref[kind])
        part = more if part is None else part + more
    part_ref[0] = part


def light_project(local, low, light):
    shapes = [like(light.shape, WIDE), like(low.shape, WIDE)]
    return pl.pallas_call(
        light_project_kernel,
        grid=(low.shape[0],),
        in_specs=[each(local), each(low), whole(light)],
        out_specs=[whole(shapes[0]), each(shapes[1])],
        out_shape=shapes,
        compiler_params=params(),
        cost_estimate=cost(9),
        name="light_project",
    )(local, low, light)


def heavy_project_kernel(
    light_part_ref, low_ref, pairs_ref, heavy_ref, slots_ref, gate_ref, raw_ref, logit_ref,
    lead_ref, tail_ref, light_ref, light_sum_ref,
    grad_ref, light_grad_ref, part_ref, both_logit_ref, grad_acc, light_acc,
):
    step = pl.program_id(0)

    @pl.when(step == 0)
    def _():
        grad_acc[...] = jnp.zeros_like(grad_acc)
        light_acc[...] = light_sum_ref[1:]

    low = low_ref[0]
    length = low.shape[0]
    slots = slots_ref[0]
    cap = slots.shape[0]
    heads = raw_ref.shape[2] // HHD
    key_gate = column(gate_ref[0], 1)
    query_grad = merge_heads(pairs_ref, cap, heads).astype(LOW)
    key_grad = merge_upper(pairs_ref, cap, heads).astype(LOW)
    value_grad = merge_folded(pairs_ref, cap, heads)
    raw_grad = (key_gate * value_grad).astype(LOW)
    key_logit = jnp.sum(value_grad * raw_ref[0], axis=-1, keepdims=True)
    both_logit_ref[0] = columns((cap, LANES), column(logit_ref[0], 0), key_logit)
    hot_query = hot_rows(slots, ROW_QUERY, length).astype(LOW)
    hot_key = hot_rows(slots, ROW_KEY, length).astype(LOW)
    query_in = dot(hot_query, low).astype(LOW)
    key_in = dot(hot_key, low).astype(LOW)
    grad_acc[0] += cols_dot(query_in, query_grad)
    grad_acc[1] += cols_dot(key_in, key_grad)
    grad_acc[2] += cols_dot(key_in, raw_grad)
    part = light_part_ref[0] + place_rows(hot_query, rows_dot(query_grad, heavy_ref[0]))
    part = part + place_rows(
        hot_key, rows_dot(key_grad, heavy_ref[1]) + rows_dot(raw_grad, heavy_ref[2])
    )
    edges = []
    for ref, rows in ((lead_ref, slice(0, WIN)), (tail_ref, slice(length - WIN, length))):
        for kind in range(2):
            light_acc[kind] += cols_dot(low[rows], ref[0, kind])
        edges.append(rows_dot(ref[0, 0], light_ref[1]) + rows_dot(ref[0, 1], light_ref[2]))
    part_ref[0, :WIN] = (part[:WIN] + edges[0]).astype(LOW)
    part_ref[0, WIN : length - WIN] = part[WIN : length - WIN].astype(LOW)
    part_ref[0, length - WIN :] = (part[length - WIN :] + edges[1]).astype(LOW)

    @pl.when(step == pl.num_programs(0) - 1)
    def _():
        grad_ref[...] = grad_acc[...].astype(LOW)
        light_grad_ref[0] = light_sum_ref[0].astype(LOW)
        light_grad_ref[1:] = light_acc[...].astype(LOW)


def heavy_project(
    light_part, low, pairs, heavy, slots, gate, raw, logit, lead, tail, light, light_sum
):
    heads = heavy.shape[2] // HHD
    shapes = [
        like(heavy.shape, LOW),
        like(light.shape, LOW),
        like(low.shape, LOW),
        like(logit.shape, WIDE),
    ]
    return pl.pallas_call(
        heavy_project_kernel,
        grid=(low.shape[0],),
        in_specs=[
            each(light_part), each(low), pair_spec(pairs, heads), whole(heavy), each(slots),
            each(gate), each(raw), each(logit), each(lead), each(tail), whole(light),
            whole(light_sum),
        ],
        out_specs=[whole(shapes[0]), whole(shapes[1]), each(shapes[2]), each(shapes[3])],
        out_shape=shapes,
        scratch_shapes=[
            pltpu.VMEM(heavy.shape, WIDE),
            pltpu.VMEM((2,) + light.shape[1:], WIDE),
        ],
        compiler_params=params(),
        cost_estimate=cost(11),
        name="heavy_project",
    )(light_part, low, pairs, heavy, slots, gate, raw, logit, lead, tail, light, light_sum)


def input_kernel(
    part_ref, other_ref, logit_ref, logit_other_ref, gate_ref, slots_ref, tokens_ref, gains_ref,
    routers_ref, middle_ref, small_in_ref, grad_ref, small_ref,
):
    @pl.when(pl.program_id(0) == 0)
    def _():
        small_ref[...] = small_in_ref[...]

    slots = slots_ref[0]
    cap = slots.shape[0]
    inputs = tokens_ref[0].astype(WIDE)
    length = inputs.shape[0]
    factor = rms_of(inputs)
    scaled = inputs * factor
    normed = scaled * gains_ref[0:1, :]
    gates = gate_ref[0]
    grads = (logit_ref[0] + logit_other_ref[0]) * gates * (1.0 - gates)
    query_logit = jnp.where(column(slots, OK_QUERY) > 0, column(grads, 0), 0.0)
    key_logit = jnp.where(column(slots, OK_KEY) > 0, column(grads, 1), 0.0)
    query_token = column(
        exact_place(hot_rows(slots, ROW_QUERY, length), columns((cap, LANES), query_logit)), 0
    )
    key_token = column(
        exact_place(hot_rows(slots, ROW_KEY, length), columns((cap, LANES), key_logit)), 0
    )
    normed_grad = (
        (part_ref[0].astype(WIDE) + other_ref[0].astype(WIDE))
        + query_token * routers_ref[0:1, :]
        + key_token * routers_ref[1:2, :]
    )
    small_ref[2:3, :] += jnp.sum(normed_grad * scaled, axis=0, keepdims=True)
    small_ref[3:4, :] += jnp.sum(query_token * normed, axis=0, keepdims=True)
    small_ref[4:5, :] += jnp.sum(key_token * normed, axis=0, keepdims=True)
    grad_ref[0] = middle_ref[0] + norm_back(inputs, factor, normed_grad * gains_ref[0:1, :])


def input_back(part, other, logit, logit_other, gate, slots, tokens, gains, routers, middle, small):
    shapes = [like(middle.shape, WIDE), like(small.shape, WIDE)]
    return pl.pallas_call(
        input_kernel,
        grid=(tokens.shape[0],),
        in_specs=[
            each(part), each(other), each(logit), each(logit_other), each(gate), each(slots),
            each(tokens), whole(gains), whole(routers), each(middle), whole(small),
        ],
        out_specs=[each(shapes[0]), whole(shapes[1])],
        out_shape=shapes,
        compiler_params=params(),
        cost_estimate=cost(6),
        name="input_back",
    )(part, other, logit, logit_other, gate, slots, tokens, gains, routers, middle, small)


def heavy_weights_kernel(tile, core_ref, here_ref, there_ref, in_ref, out_ref, *refs):
    din_ref, dout_ref, rows_ref, grad_ref, hidden_ref, gate_ref, up_ref, sems = refs[-8:]

    starts = range(0, rows_ref.shape[0], tile)
    first = pl.program_id(0) == 0

    def copies(rows_from, grad_from, index):
        part = pl.ds(index * tile, tile)
        return [
            pltpu.make_async_copy(rows_from.at[part, :], rows_ref.at[part, :], sems.at[0, index]),
            pltpu.make_async_copy(grad_from.at[part, :], grad_ref.at[part, :], sems.at[1, index]),
        ]

    def fetch(rows_from, grad_from):
        for index in range(len(starts)):
            for copy in copies(rows_from, grad_from, index):
                copy.start()

    @pl.when(first & (core_ref[0, 0] == 0))
    def _():
        fetch(here_ref, there_ref)

    @pl.when(first & (core_ref[0, 0] != 0))
    def _():
        fetch(there_ref, here_ref)

    def every_tile(waits):
        for index, start in enumerate(starts):
            if waits:
                for copy in copies(here_ref, there_ref, index):
                    copy.wait()
            part = pl.ds(start, tile)
            rows = rows_ref[part, :]
            hidden, gate_grad, up_grad = gelu_parts(
                dot(rows, in_ref[0]), dot(rows, in_ref[1]), dot(grad_ref[part, :], out_ref[...])
            )
            hidden_ref[part, :] = hidden.astype(LOW)
            gate_ref[part, :] = gate_grad.astype(LOW)
            up_ref[part, :] = up_grad.astype(LOW)

    pl.when(first)(lambda: every_tile(True))
    pl.when(jnp.logical_not(first))(lambda: every_tile(False))
    dout_ref[...] = cols_dot(grad_ref[...], hidden_ref[...])
    din_ref[:, 0, :] = cols_dot(rows_ref[...], gate_ref[...])
    din_ref[:, 1, :] = cols_dot(rows_ref[...], up_ref[...])


def heavy_weights(core, here, there, weight_in, weight_out, first_block, count_blocks, done):
    count, width = here.shape
    hidden = weight_out.shape[1]
    cols = 256
    tile = 512 if count % 512 == 0 else count
    out_block = pl.BlockSpec((width, cols), lambda i: (0, first_block + i))
    in_block = pl.BlockSpec((width, 2, cols), lambda i: (0, 0, first_block + i))
    return pl.pallas_call(
        lambda *refs: heavy_weights_kernel(tile, *refs),
        grid=(count_blocks,),
        in_specs=[
            pl.BlockSpec(memory_space=pltpu.SMEM),
            pl.BlockSpec(memory_space=pl.ANY),
            pl.BlockSpec(memory_space=pl.ANY),
            pl.BlockSpec((2, width, cols), lambda i: (0, 0, first_block + i)),
            out_block,
        ]
        + [pl.BlockSpec(memory_space=pl.ANY)] * len(done),
        out_specs=[in_block, out_block],
        out_shape=[like((width, 2, hidden), WIDE), like((width, hidden), WIDE)],
        scratch_shapes=[pltpu.VMEM((count, width), LOW)] * 2
        + [pltpu.VMEM((count, cols), LOW)] * 3
        + [pltpu.SemaphoreType.DMA((2, count // tile))],
        input_output_aliases={5 + i: i for i in range(len(done))},
        compiler_params=params(60),
        cost_estimate=cost(4 + 9 * count_blocks * count / 3072),
        name="heavy_weights",
    )(core, here, there, weight_in, weight_out, *done)


def bit_pairs(bit):
    return [(i, i ^ (1 << bit)) for i in range(lax.axis_size("seq"))]


def bit_here(bit):
    return (lax.axis_index("seq") >> bit) & 1


def after(value, *others):
    return lax.optimization_barrier((value,) + others)[0]


def scatter_start(value, bit):
    halves = value.reshape(2, value.shape[0] // 2, value.shape[1])
    mine = bit_here(bit)
    sent = lax.dynamic_index_in_dim(halves, 1 - mine, 0, keepdims=False)
    kept = lax.dynamic_index_in_dim(halves, mine, 0, keepdims=False)
    return kept, lax.ppermute(sent, "seq", bit_pairs(bit))


def scatter_end(started, *others):
    kept, got = started
    got = after(got, *others)
    return (kept.astype(WIDE) + got.astype(WIDE)).astype(LOW)


def gather_start(value, bit):
    return value, lax.ppermute(value, "seq", bit_pairs(bit)), bit_here(bit)


def gather_end(started, *others):
    value, got, mine = started
    got = after(got, *others)
    return jnp.where(
        mine == 0,
        jnp.concatenate([value, got], axis=0),
        jnp.concatenate([got, value], axis=0),
    )


def interleave(parts, blocks):
    cut = [p.reshape(blocks, -1, p.shape[1]) for p in parts]
    return jnp.concatenate(cut, axis=1).reshape(-1, parts[0].shape[1])


def apart(value, blocks, rows):
    cut = value.reshape(blocks, -1, value.shape[1])
    marks = [sum(rows[:i]) // blocks for i in range(len(rows) + 1)]
    return [
        cut[:, marks[i] : marks[i + 1]].reshape(-1, value.shape[1]) for i in range(len(rows))
    ]


def in_order(bit_ref, mine_ref, got_ref, body):
    pl.when(bit_ref[0, 0] == 0)(lambda: body(mine_ref, got_ref))
    pl.when(bit_ref[0, 0] != 0)(lambda: body(got_ref, mine_ref))


def finish_call(kernel, bit, mine, got, shapes, name):
    shapes = [like(shape, WIDE) for shape in shapes]
    return pl.pallas_call(
        kernel,
        in_specs=[
            pl.BlockSpec(memory_space=pltpu.SMEM),
            pl.BlockSpec(memory_space=pltpu.VMEM),
            pl.BlockSpec(memory_space=pltpu.VMEM),
        ],
        out_shape=shapes,
        compiler_params=params(),
        name=name,
    )(bit_here(bit).astype(jnp.int32).reshape(1, 1), mine, got)


def feed_in_kernel(bit_ref, mine_ref, got_ref, in_ref):
    width, _, hidden = in_ref.shape

    def body(*halves):
        for kind, ref in enumerate(halves):

            def store(rows, cols, value, kind=kind):
                in_ref[rows, kind, cols] = value.astype(WIDE)

            unpack_wide(store, ref, 0, width, hidden - ref.shape[1])

    in_order(bit_ref, mine_ref, got_ref, body)


def outs_kernel(bit_ref, mine_ref, got_ref, feed_ref, light_ref, heavy_ref):
    width, hidden = feed_ref.shape

    def body(first_ref, second_ref):
        half, cols = first_ref.shape

        def store(rows, lanes, value):
            feed_ref[rows, lanes] = value.astype(WIDE)

        unpack_wide(store, first_ref, 0, width, hidden - cols)
        start = width * hidden // cols
        light_ref[: half - start, :] = first_ref[start:, :].astype(WIDE)
        rest = width - (half - start)
        light_ref[half - start :, :] = second_ref[:rest, :].astype(WIDE)
        heavy_ref[...] = second_ref[rest:, :].astype(WIDE)

    in_order(bit_ref, mine_ref, got_ref, body)


def kinds_kernel(bit_ref, mine_ref, got_ref, wide_ref):
    def body(first_ref, second_ref):
        half = first_ref.shape[0]
        wide_ref[:half, :] = first_ref[...].astype(WIDE)
        wide_ref[half:, :] = second_ref[...].astype(WIDE)

    in_order(bit_ref, mine_ref, got_ref, body)


def other_core(value):
    return lax.ppermute(value, "mp", [(0, 1), (1, 0)])


def to_neighbours(first, last):
    peers = lax.axis_size("seq")
    up = [(i, i + 1) for i in range(peers - 1)]
    down = [(i + 1, i) for i in range(peers - 1)]
    return lax.ppermute(last, "seq", up), lax.ppermute(first, "seq", down)


def exchange(pairs):
    return lax.all_to_all(pairs, "seq", split_axis=0, concat_axis=0, tiled=True)


def by_kind(weights):
    return weights.transpose(1, 0, 2)


def shards(
    tokens,
    out_grad,
    gains,
    routers,
    light_query_key_value_weight,
    light_attention_output_weight,
    heavy_qkv,
    heavy_out,
    light_feedforward_input_weight,
    light_feedforward_output_weight,
    heavy_mlp_in,
    heavy_mlp_out,
    routed_queries,
    routed_keys,
    routed_mlp,
    block_counts,
):
    seq_count, local_len, width = tokens.shape
    seq_devices = lax.axis_size("seq")
    row_base = lax.axis_index("seq") * local_len
    capacity = routed_queries.shape[1]
    light_cols = light_query_key_value_weight.shape[2]
    gain_rows, router_rows = gains.T, routers.T
    slot_ids = jnp.arange(capacity, dtype=jnp.int32)[None, :, None]
    rows = jnp.stack([routed_queries, routed_keys, routed_mlp], axis=2) - row_base
    valid = (slot_ids < block_counts).astype(jnp.int32)
    slots = jnp.concatenate([rows, valid], axis=2)
    place = jnp.stack([row_base, jnp.int32(seq_devices * local_len)]).astype(jnp.int32)[None, :]
    core = lax.axis_index("mp").astype(jnp.int32).reshape(1, 1)
    light_weights = by_kind(light_query_key_value_weight)
    heavy_weights_qkv = by_kind(heavy_qkv)

    own_tokens = lax.dynamic_index_in_dim(tokens, lax.axis_index("mp"), 0, keepdims=False)
    edges = to_neighbours(own_tokens[:WIN], own_tokens[local_len - WIN :])
    low, pairs, raw, gate = front(
        tokens, gain_rows, router_rows, slots, heavy_weights_qkv, seq_devices
    )
    edges = [after(edge, low) for edge in edges]
    first_core = lax.axis_index("mp") == 0
    before, behind = [
        jnp.where(first_core, jnp.stack([mine, more]), jnp.stack([more, mine]))
        for mine, more in zip(edges, [other_core(edge) for edge in edges])
    ]
    pair = exchange(after(pairs, before, behind))
    mix, attn, lse, query, window = light_forward(
        place, low, before, behind, gain_rows, light_weights, light_attention_output_weight
    )
    pair_query, pair_key, pair_value, kept, pair_mix = heavy_forward(after(pair, attn))
    mix_pairs = exchange(pair_mix)
    light_in = by_kind(after(light_feedforward_input_weight, kept))
    heavy_in = by_kind(after(heavy_mlp_in, kept))
    own, heavy_mix = combine(after(mix_pairs, light_in, heavy_in), attn, heavy_out, slots, gate)
    other = other_core(own)
    low_two, rows, slot, ship, gate_two = mlp_slots(
        core, tokens, own, other, out_grad, gain_rows, router_rows, slots
    )
    all_slots = seq_count * capacity * seq_devices
    gather_heavy = 2 * all_slots * width < 4 * (heavy_mlp_in.size + heavy_mlp_out.size)
    here = lax.all_gather(ship, "seq", axis=1, tiled=True) if gather_heavy else ship
    part, feed_grads, mlp = feed(
        low_two, rows, slot, gate_two, out_grad, slots, light_in, light_feedforward_output_weight,
        heavy_in, heavy_mlp_out, light_cols,
    )
    beyond, mlp_other = other_core(part), other_core(mlp)
    bits = (seq_devices - 1).bit_length()
    blocks = 1 << (bits - 2)
    first_going = scatter_start(feed_grads[:2].reshape(-1, light_cols), 0)
    mixed, middle_grad, mix_grad, grad_pairs, out_grads, small, query_logit = middle_back(
        tokens, own, other, part, beyond, out_grad, gain_rows, router_rows, slots, gate, mlp,
        mlp_other, mix, heavy_mix, light_attention_output_weight, heavy_out, feed_grads[2], seq_devices,
    )
    pair_grad = exchange(grad_pairs)
    local, early, late = light_backward(place, query, window, lse, mix_grad)
    first_wave = scatter_end(first_going, local)
    lead, tail = to_neighbours(early, late)
    triple = heavy_backward(
        pair_query, pair_key, pair_value, kept, after(pair_grad, local, first_wave)
    )
    triple_pairs = exchange(triple)
    second_going = scatter_start(after(out_grads, triple), 1)
    light_sums, light_part = light_project(after(local, triple), low, light_weights)
    second_wave = scatter_end(second_going, light_part)
    heavy_grads, light_grads, low_part, logit = heavy_project(
        light_part, low, after(triple_pairs, second_wave), heavy_weights_qkv, slots, gate, raw,
        query_logit, lead, tail, light_weights, light_sums,
    )
    heavy_going = scatter_start(heavy_grads.reshape(-1, light_cols), 1)
    light_going = scatter_start(light_grads.reshape(-1, light_cols), 0)
    second_going = scatter_start(after(second_wave, low_part), 0)
    first_going = scatter_start(after(first_wave, low_part), 1)
    low_other, logit_other = other_core(low_part), other_core(logit)
    here = after(here, low_part)
    there = other_core(here).reshape(-1, width)
    here = here.reshape(-1, width)
    blocks_done = [0]
    heavy_sums = []

    def heavy_piece(count, *others):
        heavy_sums[:] = heavy_weights(
            core, after(here, *others), there, heavy_in, heavy_mlp_out, blocks_done[0], count, heavy_sums
        )
        blocks_done[0] += count
        return heavy_sums[1]

    input_grad, small = input_back(
        low_part, low_other, logit, logit_other, gate, slots, tokens, gain_rows,
        router_rows, middle_grad, small,
    )
    small_rows = small.astype(LOW).reshape(-1, light_cols)
    small_rows = jnp.pad(small_rows, ((0, 16 * blocks - small_rows.shape[0]), (0, 0)))
    small_got = lax.ppermute(small_rows, "seq", bit_pairs(1))
    second_wave = scatter_end(second_going, input_grad)
    first_wave = scatter_end(first_going, input_grad)
    early_sizes = [first_wave.shape[0], second_wave.shape[0]]
    wave = interleave([first_wave, second_wave], blocks)
    going = scatter_start(wave, 2)
    mark = heavy_piece(2, input_grad, wave)
    wave = scatter_end(going, mark)
    heavy_wave = scatter_end(heavy_going, mark)
    light_wave = scatter_end(light_going, mark)
    light_going = scatter_start(light_wave, 1)
    small_rows = scatter_end((small_rows, small_got), mark)
    for bit in range(3, bits - 1):
        wave = scatter_end(scatter_start(wave, bit))
    going = scatter_start(wave, bits - 1)
    heavy_going = scatter_start(heavy_wave, 0)
    small_got = lax.ppermute(small_rows, "seq", bit_pairs(0))
    mark = heavy_piece(1, wave, heavy_wave, light_wave, small_rows)
    wave = scatter_end(going, mark)
    heavy_wave = scatter_end(heavy_going, mark)
    light_wave = scatter_end(light_going, mark)
    small_rows = scatter_end((small_rows, small_got), mark)
    for bit in reversed(range(4, bits)):
        wave = gather_end(gather_start(wave, bit))
    going = gather_start(wave, 3)
    late_wave = [light_wave, heavy_wave, small_rows]
    late_sizes = [p.shape[0] for p in late_wave]
    late_wave = interleave(late_wave, blocks)
    late_going = scatter_start(late_wave, 2)
    mark = heavy_piece(1, late_wave, wave)
    wave = gather_end(going, mark)
    late_wave = scatter_end(late_going, mark)
    for bit in range(3, bits - 1):
        late_wave = scatter_end(scatter_start(late_wave, bit))
    going = gather_start(wave, 2)
    late_going = scatter_start(late_wave, bits - 1)
    mark = heavy_piece(1, late_wave, wave)
    wave = apart(gather_end(going, mark), blocks, early_sizes)
    going = [gather_start(p, bit) for p, bit in zip(wave, (1, 0))]
    late_wave = scatter_end(late_going, mark)
    for bit in reversed(range(4, bits)):
        late_wave = gather_end(gather_start(late_wave, bit))
    late_going = gather_start(late_wave, 3)
    mark = heavy_piece(1, late_wave, *wave)
    wave = [gather_end(p, mark) for p in going]
    early_halves = [(p, lax.ppermute(p, "seq", bit_pairs(bit))) for p, bit in zip(wave, (0, 1))]
    late_wave = gather_end(late_going, mark)
    late_going = gather_start(late_wave, 2)
    mark = heavy_piece(1, late_wave, *wave)
    late_wave = apart(gather_end(late_going, mark), blocks, late_sizes)
    small_sum = late_wave.pop().astype(WIDE)
    late_going = [gather_start(p, bit) for p, bit in zip(late_wave, (1, 0))]
    early_halves = [(after(p, *late_wave), after(got, mark)) for p, got in early_halves]
    hidden = light_feedforward_output_weight.shape[1]
    square, kinds = (width, light_cols), [(3 * width, light_cols)]
    (feed_in,) = finish_call(feed_in_kernel, 0, *early_halves[0], [(width, 2, hidden)], "feed_in")
    feed_out, light_out_sum, heavy_out_sum = finish_call(
        outs_kernel, 1, *early_halves[1], [(width, hidden), square, square], "outs"
    )
    late_wave = [gather_end(p, feed_in, feed_out) for p in late_going]
    late_halves = [
        (p, lax.ppermute(p, "seq", bit_pairs(bit))) for p, bit in zip(late_wave, (0, 1))
    ]
    mark = heavy_piece(1, *late_wave)
    late_halves = [(p, after(got, mark)) for p, got in late_halves]
    heavy_in_grad, heavy_out_grad = heavy_sums
    if not gather_heavy:
        sums = [heavy_in_grad[:, 0], heavy_in_grad[:, 1], heavy_out_grad]
        sums = [p.astype(LOW) for p in sums]
        for bit in range(bits):
            sums = [scatter_end(scatter_start(p, bit)) for p in sums]
        for bit in reversed(range(bits)):
            sums = [gather_end(gather_start(p, bit)) for p in sums]
        heavy_in_grad = jnp.stack(sums[:2], axis=1).astype(WIDE)
        heavy_out_grad = sums[2].astype(WIDE)
    (light_sum,) = finish_call(kinds_kernel, 0, *late_halves[0], kinds, "light_sum")
    (heavy_sum,) = finish_call(kinds_kernel, 1, *late_halves[1], kinds, "heavy_sum")
    small_sum = small_sum[: 8 * width // light_cols].reshape(8, width)
    return (
        mixed,
        input_grad,
        light_sum.reshape(3, width, light_cols).transpose(1, 0, 2),
        light_out_sum,
        heavy_sum.reshape(3, width, light_cols).transpose(1, 0, 2),
        heavy_out_sum,
        feed_in,
        feed_out,
        heavy_in_grad,
        heavy_out_grad,
        jnp.stack([small_sum[2], small_sum[0]], axis=1),
        jnp.stack([small_sum[3], small_sum[4], small_sum[1]], axis=1),
    )


def solution(mesh):
    rows = P(None, "seq", None)
    by_column = P(None, None, "mp")
    by_hidden = P(None, "mp")
    slots = P(None, "seq")
    weights = (by_column, by_hidden) * 4
    return jax.shard_map(
        shards,
        mesh=mesh,
        in_specs=(rows, rows, P(), P()) + weights + (slots, slots, slots, rows),
        out_specs=(rows, rows) + weights + (P(), P()),
        check_vma=False,
    )
```

```python
import math

import jax
import jax.numpy as jnp
from jax import lax
from jax.experimental import pallas as pl
from jax.experimental.pallas import tpu as pltpu
from jax.sharding import PartitionSpec as P

LHD = 96
HHD = 64
WIN = 128
LANES = 128

EPSILON = 1e-06
MASKED = -1e30
MARK = 1e30
EXACT = lax.Precision.HIGHEST
LOW = jnp.bfloat16
WIDE = jnp.float32

ROW_QUERY, ROW_KEY, ROW_MLP, OK_QUERY, OK_KEY, OK_MLP = range(6)


def lanes_of(shape):
    return lax.broadcasted_iota(jnp.int32, shape, len(shape) - 1)


def dot(a, b):
    return jnp.dot(a, b, preferred_element_type=WIDE)


def rows_dot(a, b):
    return lax.dot_general(a, b, (((1,), (1,)), ((), ())), preferred_element_type=WIDE)


def cols_dot(a, b):
    return lax.dot_general(a, b, (((0,), (0,)), ((), ())), preferred_element_type=WIDE)


def rms_of(values):
    return lax.rsqrt(jnp.mean(values * values, axis=-1, keepdims=True) + EPSILON)


def column(values, index):
    return values[:, index : index + 1]


def columns(shape, *parts):
    lane = lanes_of(shape)
    out = jnp.zeros(shape, WIDE)
    for index, part in enumerate(parts):
        out = jnp.where(lane == index, part, out)
    return out


def hot_rows(slots, index, length):
    rows = column(slots, index)
    return (lanes_of((rows.shape[0], length)) == rows).astype(WIDE)


def place_rows(hot, values):
    high = values.astype(LOW)
    rest = (values - high.astype(WIDE)).astype(LOW)
    return cols_dot(hot, high) + cols_dot(hot, rest)


def exact_place(hot, values):
    return lax.dot_general(
        hot, values, (((0,), (0,)), ((), ())), precision=EXACT, preferred_element_type=WIDE
    )


def exact_pick(hot, values):
    return jnp.dot(hot, values, precision=EXACT, preferred_element_type=WIDE)


def row_dots(values, vector):
    return jnp.sum(values * vector, axis=-1, keepdims=True)


def norm_back(values, factor, weighted):
    inner = jnp.mean(weighted * values, axis=-1, keepdims=True)
    return factor * weighted - values * (factor * factor * factor) * inner


def gelu_parts(gate, up, hidden_grad):
    root = math.sqrt(2.0 / math.pi)
    cube = 0.044715 * root
    square = gate * gate
    bend = jnp.tanh(gate * (root + cube * square))
    half = 0.5 + 0.5 * bend
    value = gate * half
    slope = half + gate * (1.0 - bend * bend) * (0.5 * root + (1.5 * cube) * square)
    return value * up, slope * up * hidden_grad, value * hidden_grad


def merge_heads(ref, rows, heads):
    tiles = []
    for head in range(0, heads, 2):
        first = ref[head, :rows, :].astype(WIDE)
        second = ref[head + 1, :rows, :].astype(WIDE)
        lane = lanes_of(first.shape)
        tiles.append(jnp.where(lane < HHD, first, pltpu.roll(second, HHD, 1)))
    return jnp.concatenate(tiles, axis=1)


def merge_upper(ref, rows, heads):
    tiles = []
    for head in range(0, heads, 2):
        first = ref[head, :rows, :].astype(WIDE)
        second = ref[head + 1, :rows, :].astype(WIDE)
        lane = lanes_of(first.shape)
        tiles.append(jnp.where(lane < HHD, pltpu.roll(first, HHD, 1), second))
    return jnp.concatenate(tiles, axis=1)


def head_low(values, head):
    tile = values[:, head // 2 * LANES : (head // 2 + 1) * LANES]
    return tile if head % 2 == 0 else pltpu.roll(tile, HHD, 1)


def head_high(values, head):
    tile = values[:, head // 2 * LANES : (head // 2 + 1) * LANES]
    return tile if head % 2 == 1 else pltpu.roll(tile, HHD, 1)


def fold(values):
    half = values.shape[0] // 2
    lane = lanes_of((half, LANES))
    return jnp.where(lane < HHD, values[:half], pltpu.roll(values[half:], HHD, 1))


def unfold(folded):
    lane = lanes_of(folded.shape)
    return jnp.concatenate(
        [
            jnp.where(lane < HHD, folded, 0.0),
            jnp.where(lane < HHD, pltpu.roll(folded, HHD, 1), 0.0),
        ],
        axis=0,
    )


def merge_folded(ref, start, heads):
    tiles = []
    for head in range(0, heads, 2):
        first = ref[head, start:, :].astype(WIDE)
        second = ref[head + 1, start:, :].astype(WIDE)
        lane = lanes_of(first.shape)
        upper = jnp.where(lane < HHD, first, pltpu.roll(second, HHD, 1))
        lower = jnp.where(lane < HHD, pltpu.roll(first, HHD, 1), second)
        tiles.append(jnp.concatenate([upper, lower], axis=0))
    return jnp.concatenate(tiles, axis=1)


def spread_matrix(heads):
    row = lax.broadcasted_iota(jnp.int32, (heads * LHD, heads * LANES), 0)
    lane = lanes_of((heads * LHD, heads * LANES))
    inner = lane & (LANES - 1)
    hit = (row == (lane >> 7) * LHD + inner) & (inner < LHD)
    return hit.astype(WIDE).astype(LOW)


def params(mib=56):
    return pltpu.CompilerParams(vmem_limit_bytes=mib * 2**20)


def cost(microseconds):
    return pl.CostEstimate(
        flops=int(microseconds * 2e7), bytes_accessed=2**10, transcendentals=0
    )


def whole(array):
    zeros = (0,) * array.ndim
    return pl.BlockSpec(array.shape, lambda *_: zeros, pipeline_mode=pl.Buffered(1))


def each(array):
    rest = (0,) * (array.ndim - 1)
    return pl.BlockSpec((1,) + array.shape[1:], lambda s: (s,) + rest)


def like(shape, kind):
    return jax.ShapeDtypeStruct(shape, kind)


def front_kernel(
    tokens_ref, gains_ref, routers_ref, slots_ref, heavy_ref, low_ref, pair_ref, raw_ref, gate_ref,
):
    inputs = tokens_ref[0].astype(WIDE)
    length = inputs.shape[0]
    normed = inputs * rms_of(inputs) * gains_ref[0:1, :]
    low = normed.astype(LOW)
    low_ref[0] = low
    slots = slots_ref[0]
    hot_query = hot_rows(slots, ROW_QUERY, length)
    hot_key = hot_rows(slots, ROW_KEY, length)
    logits = columns(
        (length, LANES),
        row_dots(normed, routers_ref[0:1, :]),
        row_dots(normed, routers_ref[1:2, :]),
    )
    query_gate = jax.nn.sigmoid(column(exact_pick(hot_query, logits), 0))
    key_gate = jax.nn.sigmoid(column(exact_pick(hot_key, logits), 1))
    gate_ref[0] = columns((slots.shape[0], LANES), query_gate, key_gate)
    query_in = dot(hot_query.astype(LOW), low).astype(LOW)
    key_in = dot(hot_key.astype(LOW), low).astype(LOW)
    query = dot(query_in, heavy_ref[0]).astype(LOW).astype(WIDE)
    key = dot(key_in, heavy_ref[1]).astype(LOW).astype(WIDE)
    raw = dot(key_in, heavy_ref[2])
    raw_ref[0] = raw
    value = (key_gate * raw).astype(LOW).astype(WIDE)
    value = jnp.where(column(slots, OK_KEY) > 0, value, MARK)
    cap = slots.shape[0]
    lane = lanes_of((cap, LANES))
    for head in range(raw.shape[1] // HHD):
        both = jnp.where(lane < HHD, head_low(query, head), head_high(key, head))
        pair_ref[head, :cap, :] = both.astype(LOW)
        pair_ref[head, cap:, :] = fold(head_low(value, head)).astype(LOW)


def front(tokens, gains, routers, slots, heavy, seq_devices):
    seqs, length, width = tokens.shape
    cap = slots.shape[1]
    heavy_cols = heavy.shape[2]
    heads = heavy_cols // HHD
    shapes = [
        like(tokens.shape, LOW),
        like((seq_devices, 3 * cap // 2, LANES), LOW),
        like((seqs, cap, heavy_cols), WIDE),
        like((seqs, cap, LANES), WIDE),
    ]
    specs = [each(s) for s in shapes]
    specs[1] = pl.BlockSpec((heads, 3 * cap // 2, LANES), lambda s: (s, 0, 0))
    return pl.pallas_call(
        front_kernel,
        grid=(seqs,),
        in_specs=[each(tokens), whole(gains), whole(routers), each(slots), whole(heavy)],
        out_specs=specs,
        out_shape=shapes,
        compiler_params=params(),
        cost_estimate=cost(8),
        name="front",
    )(tokens, gains, routers, slots, heavy)


def window_bias(block, length, base, total):
    row = lax.broadcasted_iota(jnp.int32, (WIN, 3 * WIN), 0)
    col = lanes_of((WIN, 3 * WIN))
    place = base + (block - 1) * WIN + col
    near = jnp.abs(col - WIN - row) < WIN
    return jnp.where(near & (place >= 0) & (place < total), 0.0, MASKED)


def light_forward_kernel(
    scale, place_ref, low_ref, before_ref, after_ref, gains_ref, weight_ref, out_ref,
    mix_ref, attn_ref, lse_ref, query_ref, window_ref, wide_ref,
):
    length, heads = low_ref.shape[1], weight_ref.shape[2] // LHD
    spread = spread_matrix(heads)

    def heads_of(rows, kind):
        projected = dot(rows, weight_ref[kind]).astype(LOW)
        return dot(projected, spread).astype(LOW)

    query_ref[0] = heads_of(low_ref[0], 0)
    edges = ((before_ref, slice(0, WIN)), (after_ref, slice(WIN + length, 2 * WIN + length)))
    for ref, rows in edges:
        inputs = ref[0].astype(WIDE)
        low = (inputs * rms_of(inputs) * gains_ref[0:1, :]).astype(LOW)
        for kind in range(2):
            window_ref[0, kind, rows, :] = heads_of(low, 1 + kind)
    for kind in range(2):
        window_ref[0, kind, WIN : WIN + length, :] = heads_of(low_ref[0], 1 + kind)
    for block in range(length // WIN):
        rows = slice(block * WIN, (block + 1) * WIN)
        near = slice(block * WIN, (block + 3) * WIN)
        bias = window_bias(block, length, place_ref[0, 0], place_ref[0, 1])
        lanes = [slice(head * LANES, (head + 1) * LANES) for head in range(heads)]
        scores = jnp.concatenate(
            [
                rows_dot(query_ref[0, rows, at], window_ref[0, 0, near, at]) * scale + bias
                for at in lanes
            ],
            axis=0,
        )
        top = jnp.max(scores, axis=-1, keepdims=True)
        expo = jnp.exp(scores - top)
        total = jnp.sum(expo, axis=-1, keepdims=True)
        lse = top + jnp.log(total)
        share = 1.0 / total
        expo = expo.astype(LOW)
        kept = []
        for head, at in enumerate(lanes):
            mine = slice(head * WIN, (head + 1) * WIN)
            mixed = dot(expo[mine], window_ref[0, 1, near, at]) * share[mine]
            wide_ref[rows, at] = mixed.astype(LOW)
            kept.append(lse[mine])
        lse_ref[0, rows, :] = columns((WIN, LANES), *kept)
    mix = rows_dot(wide_ref[...], spread).astype(LOW)
    mix_ref[0] = mix
    attn_ref[0] = rows_dot(mix, out_ref[...])


def light_forward(place, low, before, after, gains, weight, weight_out):
    seqs, length, _ = low.shape
    light_cols = weight.shape[2]
    heads = light_cols // LHD
    shapes = [
        like((seqs, length, light_cols), LOW),
        like((seqs, length, weight_out.shape[0]), WIDE),
        like((seqs, length, LANES), WIDE),
        like((seqs, length, heads * LANES), LOW),
        like((seqs, 2, length + 2 * WIN, heads * LANES), LOW),
    ]
    return pl.pallas_call(
        lambda *refs: light_forward_kernel(1.0 / math.sqrt(LHD), *refs),
        grid=(seqs,),
        in_specs=[
            pl.BlockSpec(memory_space=pltpu.SMEM),
            each(low),
            each(before),
            each(after),
            whole(gains),
            whole(weight),
            whole(weight_out),
        ],
        out_specs=[each(s) for s in shapes],
        out_shape=shapes,
        scratch_shapes=[pltpu.VMEM((length, heads * LANES), LOW)],
        compiler_params=params(),
        cost_estimate=cost(15),
        name="light_forward",
    )(place, low, before, after, gains, weight, weight_out)


def light_backward_kernel(
    scale, place_ref, query_ref, window_ref, lse_ref, grad_ref, local_ref, early_ref, late_ref, *scratch
):
    wide_ref, dkey_ref, dvalue_ref = scratch
    length, light_cols = grad_ref.shape[1:]
    heads = light_cols // LHD
    spread = spread_matrix(heads)
    grad = dot(grad_ref[0], spread).astype(LOW)
    dkey_ref[...] = jnp.zeros_like(dkey_ref)
    dvalue_ref[...] = jnp.zeros_like(dvalue_ref)
    for block in range(length // WIN):
        rows = slice(block * WIN, (block + 1) * WIN)
        near = slice(block * WIN, (block + 3) * WIN)
        bias = window_bias(block, length, place_ref[0, 0], place_ref[0, 1])
        lse = lse_ref[0, rows, :]
        lanes = [slice(head * LANES, (head + 1) * LANES) for head in range(heads)]
        scores = jnp.concatenate(
            [
                rows_dot(query_ref[0, rows, at], window_ref[0, 0, near, at]) * scale
                + (bias - column(lse, head))
                for head, at in enumerate(lanes)
            ],
            axis=0,
        )
        prob_grad = jnp.concatenate(
            [rows_dot(grad[rows, at], window_ref[0, 1, near, at]) for at in lanes], axis=0
        )
        probs = jnp.exp(scores)
        delta = jnp.sum(probs * prob_grad, axis=-1, keepdims=True)
        score_grad = (probs * (prob_grad - delta)).astype(LOW)
        probs = probs.astype(LOW)
        for head, at in enumerate(lanes):
            mine = slice(head * WIN, (head + 1) * WIN)
            part = score_grad[mine]
            wide_ref[rows, at] = (dot(part, window_ref[0, 0, near, at]) * scale).astype(LOW)
            dkey_ref[near, at] += cols_dot(part, query_ref[0, rows, at]) * scale
            dvalue_ref[near, at] += cols_dot(probs[mine], grad[rows, at])
    local_ref[0, 0] = rows_dot(wide_ref[...], spread).astype(LOW)
    for kind, ref in ((1, dkey_ref), (2, dvalue_ref)):
        all_rows = rows_dot(ref[...].astype(LOW), spread).astype(LOW)
        early_ref[0, kind - 1] = all_rows[:WIN]
        local_ref[0, kind] = all_rows[WIN : WIN + length]
        late_ref[0, kind - 1] = all_rows[WIN + length :]


def light_backward(place, query, window, lse, grad):
    seqs, length, light_cols = grad.shape
    edge = like((seqs, 2, WIN, light_cols), LOW)
    shapes = [like((seqs, 3, length, light_cols), LOW), edge, edge]
    return pl.pallas_call(
        lambda *refs: light_backward_kernel(1.0 / math.sqrt(LHD), *refs),
        grid=(seqs,),
        in_specs=[
            pl.BlockSpec(memory_space=pltpu.SMEM),
            each(query),
            each(window),
            each(lse),
            each(grad),
        ],
        out_specs=[each(s) for s in shapes],
        out_shape=shapes,
        scratch_shapes=[
            pltpu.VMEM(query.shape[1:], LOW),
            pltpu.VMEM(window.shape[2:], WIDE),
            pltpu.VMEM(window.shape[2:], WIDE),
        ],
        compiler_params=params(),
        cost_estimate=cost(14),
        name="light_backward",
    )(place, query, window, lse, grad)


def heavy_forward_kernel(scale, pair_ref, query_ref, key_ref, value_ref, kept_ref, mix_ref):
    devices, rows, _ = pair_ref.shape
    cap = 2 * rows // 3
    tile = kept_ref.shape[0]

    @pl.when(pl.program_id(0) == 0)
    def _():
        def unpack(index, carry):
            lane = lanes_of((cap, LANES))
            at = pl.ds(pl.multiple_of(index * cap, 16), cap)
            both = pair_ref[index, :cap, :].astype(WIDE)
            value = unfold(pair_ref[index, cap:, :].astype(WIDE))
            unused = column(value, 0) > 0.5 * MARK
            bias = jnp.where(unused, MASKED, 0.0)
            query = jnp.where(lane < HHD, both * scale, jnp.where(lane == HHD, 1.0, 0.0))
            key = jnp.where(
                lane < HHD, pltpu.roll(both, HHD, 1), jnp.where(lane == HHD, bias, 0.0)
            )
            query_ref[at, :] = query.astype(LOW)
            key_ref[at, :] = key.astype(LOW)
            value_ref[at, :] = jnp.where(unused, 0.0, value).astype(LOW)
            return carry

        lax.fori_loop(0, devices, unpack, 0, unroll=devices <= 16)

    start = pl.multiple_of(pl.program_id(0) * tile, 16)
    scores = rows_dot(query_ref[pl.ds(start, tile), :], key_ref[...])
    top = jnp.max(scores, axis=-1, keepdims=True)
    expo = jnp.exp(scores - top)
    total = jnp.sum(expo, axis=-1, keepdims=True)
    mix = dot(expo.astype(LOW), value_ref[...]) / total
    lane = lanes_of(mix.shape)
    kept_ref[...] = jnp.where(lane < HHD, mix, top + jnp.log(total))
    for index in range(tile // cap):
        mix_ref[index] = fold(mix[index * cap : (index + 1) * cap]).astype(LOW)


def heavy_backward_kernel(
    scale, query_ref, key_ref, value_ref, kept_ref, grad_ref, triple_ref, dq_ref, dk_ref, dv_ref
):
    step = pl.program_id(0)
    devices, rows, _ = triple_ref.shape
    cap = 2 * rows // 3
    tile = kept_ref.shape[0]

    @pl.when(step == 0)
    def _():
        dk_ref[...] = jnp.zeros_like(dk_ref)
        dv_ref[...] = jnp.zeros_like(dv_ref)

    start = pl.multiple_of(step * tile, 16)
    query = query_ref[pl.ds(start, tile), :]
    grad = jnp.concatenate(
        [unfold(grad_ref[index].astype(WIDE)) for index in range(tile // cap)], axis=0
    )
    kept = kept_ref[...]
    lse = column(kept, HHD)
    delta = jnp.sum(kept * grad, axis=-1, keepdims=True)
    grad = grad.astype(LOW)
    probs = jnp.exp(rows_dot(query, key_ref[...]) - lse)
    prob_grad = rows_dot(grad, value_ref[...])
    score_grad = (probs * (prob_grad - delta)).astype(LOW)
    dq_ref[pl.ds(start, tile), :] = dot(score_grad, key_ref[...]) * scale
    dk_ref[...] += cols_dot(score_grad, query)
    dv_ref[...] += cols_dot(probs.astype(LOW), grad)

    @pl.when(step == pl.num_programs(0) - 1)
    def _():
        def pack(index, carry):
            lane = lanes_of((cap, LANES))
            at = pl.ds(pl.multiple_of(index * cap, 16), cap)
            moved = pltpu.roll(dk_ref[at, :], HHD, 1)
            triple_ref[index, :cap, :] = jnp.where(lane < HHD, dq_ref[at, :], moved).astype(LOW)
            triple_ref[index, cap:, :] = fold(dv_ref[at, :]).astype(LOW)
            return carry

        lax.fori_loop(0, devices, pack, 0, unroll=devices <= 16)


def query_tile(devices, cap):
    return 4 * cap if devices <= 32 else cap


def heavy_forward(pair):
    devices, rows, _ = pair.shape
    cap = 2 * rows // 3
    length, tile = devices * cap, query_tile(devices, cap)
    operand = like((length, LANES), LOW)
    shapes = [operand] * 3 + [
        like((length, LANES), WIDE),
        like((devices, cap // 2, LANES), LOW),
    ]
    return pl.pallas_call(
        lambda *refs: heavy_forward_kernel(1.0 / math.sqrt(HHD), *refs),
        grid=(length // tile,),
        in_specs=[whole(pair)],
        out_specs=[whole(operand)] * 3
        + [
            pl.BlockSpec((tile, LANES), lambda i: (i, 0)),
            pl.BlockSpec((tile // cap, cap // 2, LANES), lambda i: (i, 0, 0)),
        ],
        out_shape=shapes,
        compiler_params=params(60),
        cost_estimate=cost(7),
        name="heavy_forward",
    )(pair)


def heavy_backward(query, key, value, kept, grad):
    devices, half, _ = grad.shape
    cap = 2 * half
    length, tile = devices * cap, query_tile(devices, cap)
    triple = like((devices, cap + half, LANES), LOW)
    return pl.pallas_call(
        lambda *refs: heavy_backward_kernel(1.0 / math.sqrt(HHD), *refs),
        grid=(length // tile,),
        in_specs=[
            whole(query),
            whole(key),
            whole(value),
            pl.BlockSpec((tile, LANES), lambda i: (i, 0)),
            pl.BlockSpec((tile // cap, half, LANES), lambda i: (i, 0, 0)),
        ],
        out_specs=whole(triple),
        out_shape=triple,
        scratch_shapes=[pltpu.VMEM((length, LANES), WIDE)] * 3,
        compiler_params=params(60),
        cost_estimate=cost(10),
        name="heavy_backward",
    )(query, key, value, kept, grad)


def combine_kernel(pairs_ref, attn_ref, out_ref, slots_ref, gate_ref, part_ref, mix_ref):
    slots = slots_ref[0]
    mix = merge_folded(pairs_ref, 0, pairs_ref.shape[0]).astype(LOW)
    mix_ref[0] = mix
    rows = rows_dot(mix, out_ref[...])
    weight = jnp.where(column(slots, OK_QUERY) > 0, column(gate_ref[0], 0), 0.0)
    hot = hot_rows(slots, ROW_QUERY, attn_ref.shape[1]).astype(LOW)
    part_ref[0] = (attn_ref[0] + place_rows(hot, weight * rows)).astype(LOW)


def pair_spec(pairs, heads):
    return pl.BlockSpec((heads,) + pairs.shape[1:], lambda s: (s, 0, 0))


def combine(pairs, attn, weight_out, slots, gate):
    seqs, cap = slots.shape[:2]
    heavy_cols = weight_out.shape[1]
    shapes = [like(attn.shape, LOW), like((seqs, cap, heavy_cols), LOW)]
    return pl.pallas_call(
        combine_kernel,
        grid=(seqs,),
        in_specs=[
            pair_spec(pairs, heavy_cols // HHD),
            each(attn),
            whole(weight_out),
            each(slots),
            each(gate),
        ],
        out_specs=[each(s) for s in shapes],
        out_shape=shapes,
        compiler_params=params(),
        cost_estimate=cost(4),
        name="combine",
    )(pairs, attn, weight_out, slots, gate)


def slots_kernel(
    core_ref, tokens_ref, own_ref, other_ref, up_ref, gains_ref, routers_ref, slots_ref,
    low_ref, rows_ref, slot_ref, ship_ref, gate_ref,
):
    middle = tokens_ref[0].astype(WIDE) + own_ref[0].astype(WIDE) + other_ref[0].astype(WIDE)
    length = middle.shape[0]
    normed = middle * rms_of(middle) * gains_ref[1:2, :]
    low = normed.astype(LOW)
    low_ref[0] = low
    slots = slots_ref[0]
    hot = hot_rows(slots, ROW_MLP, length)
    logits = columns((length, LANES), row_dots(normed, routers_ref[2:3, :]))
    gate = jax.nn.sigmoid(column(exact_pick(hot, logits), 0))
    weight = jnp.where(column(slots, OK_MLP) > 0, gate, 0.0)
    hot = hot.astype(LOW)
    rows = dot(hot, low)
    slot = weight * dot(hot, up_ref[0])
    rows_ref[0] = rows.astype(LOW)
    slot_ref[0] = slot.astype(LOW)
    ship_ref[0] = jnp.where(core_ref[0, 0] == 0, rows, slot).astype(LOW)
    gate_ref[0] = columns((slots.shape[0], LANES), gate, weight)


def mlp_slots(core, tokens, own, other, up, gains, routers, slots):
    seqs, length, width = tokens.shape
    cap = slots.shape[1]
    shapes = [like(tokens.shape, LOW)]
    shapes += [like((seqs, cap, width), LOW)] * 3 + [like((seqs, cap, LANES), WIDE)]
    return pl.pallas_call(
        slots_kernel,
        grid=(seqs,),
        in_specs=[
            pl.BlockSpec(memory_space=pltpu.SMEM),
            each(tokens), each(own), each(other), each(up), whole(gains), whole(routers), each(slots),
        ],
        out_specs=[each(s) for s in shapes],
        out_shape=shapes,
        compiler_params=params(),
        cost_estimate=cost(5),
        name="mlp_slots",
    )(core, tokens, own, other, up, gains, routers, slots)


def pack_wide(ref, value):
    value = value.astype(LOW)
    rows, cols = value.shape[0], ref.shape[1]
    extra = value.shape[1] - cols
    group = rows * extra // cols
    ref[:rows, :] = value[:, :cols]
    for index in range(cols // extra):
        ref[rows:, index * extra : (index + 1) * extra] = value[
            index * group : (index + 1) * group, cols:
        ]


def unpack_wide(store, ref, start, rows, extra):
    cols = ref.shape[1]
    group = rows * extra // cols
    store(slice(0, rows), slice(0, cols), ref[start : start + rows, :])
    for index in range(cols // extra):
        store(
            slice(index * group, (index + 1) * group),
            slice(cols, cols + extra),
            ref[start + rows : start + rows + group, index * extra : (index + 1) * extra],
        )


def feed_kernel(
    low_ref, rows_ref, slot_ref, kept_ref, up_ref, slots_ref, in_ref, out_ref, heavy_in_ref,
    heavy_out_ref, part_ref, weights_ref, down_ref, gate_ref, heavy_acc, back_acc, hidden_ref, dgate_ref, dup_ref,
):
    step = pl.program_id(0)
    seqs, length, width = up_ref.shape
    cap = slots_ref.shape[1]

    @pl.when(step == 0)
    def _():
        heavy_acc[...] = jnp.zeros_like(heavy_acc)
        back_acc[...] = jnp.zeros_like(back_acc)

    first, second, last = heavy_in_ref[0], heavy_in_ref[1], heavy_out_ref[...]
    rows = rows_ref[...]
    hidden, gate_grad, up_grad = gelu_parts(
        dot(rows, first), dot(rows, second), dot(slot_ref[...], last)
    )
    heavy_acc[...] += rows_dot(hidden.astype(LOW), last)
    back_acc[...] += rows_dot(gate_grad.astype(LOW), first) + rows_dot(up_grad.astype(LOW), second)

    @pl.when(step == pl.num_programs(0) - 1)
    def _():
        for s in range(seqs):
            here = slice(s * length, (s + 1) * length)
            mine = slice(s * cap, (s + 1) * cap)
            low = low_ref[s]
            hidden, gate_grad, up_grad = gelu_parts(
                dot(low, in_ref[0]), dot(low, in_ref[1]), dot(up_ref[s], out_ref[...])
            )
            hidden, gate_grad, up_grad = (
                hidden.astype(LOW),
                gate_grad.astype(LOW),
                up_grad.astype(LOW),
            )
            hidden_ref[here, :] = hidden
            dgate_ref[here, :] = gate_grad
            dup_ref[here, :] = up_grad
            hot = hot_rows(slots_ref[s], ROW_MLP, length).astype(LOW)
            kept = kept_ref[s]
            heavy_rows = heavy_acc[mine, :]
            part_ref[0, s] = (
                rows_dot(hidden, out_ref[...]) + place_rows(hot, column(kept, 1) * heavy_rows)
            ).astype(LOW)
            part_ref[1, s] = (
                rows_dot(gate_grad, in_ref[0])
                + rows_dot(up_grad, in_ref[1])
                + place_rows(hot, back_acc[mine, :])
            ).astype(LOW)
            gate_part = jnp.sum(dot(hot, up_ref[s]) * heavy_rows, axis=-1, keepdims=True)
            gate_ref[s] = columns((cap, LANES), column(kept, 0), gate_part)
        low = low_ref[...].reshape(seqs * length, width)
        up = up_ref[...].reshape(seqs * length, width)
        pack_wide(weights_ref.at[0], cols_dot(low, dgate_ref[...]))
        pack_wide(weights_ref.at[1], cols_dot(low, dup_ref[...]))
        pack_wide(down_ref, cols_dot(up, hidden_ref[...]))


def feed(low, rows, slot, kept, up, slots, light_in, light_out, heavy_in, heavy_out, packed_cols):
    seqs, length, width = up.shape
    cap = slots.shape[1]
    hidden = light_out.shape[1]
    cols = 256
    rows, slot = rows.reshape(-1, width), slot.reshape(-1, width)
    shapes = [
        like((2, seqs, length, width), LOW),
        like((2, width * hidden // packed_cols, packed_cols), LOW),
        like((width * hidden // packed_cols, packed_cols), LOW),
        like((seqs, cap, LANES), WIDE),
    ]
    return pl.pallas_call(
        feed_kernel,
        grid=(heavy_out.shape[1] // cols,),
        in_specs=[
            whole(low),
            whole(rows),
            whole(slot),
            whole(kept),
            whole(up),
            whole(slots),
            whole(light_in),
            whole(light_out),
            pl.BlockSpec((2, width, cols), lambda i: (0, 0, i)),
            pl.BlockSpec((width, cols), lambda i: (0, i)),
        ],
        out_specs=[whole(s) for s in shapes],
        out_shape=shapes,
        scratch_shapes=[pltpu.VMEM((seqs * cap, width), WIDE)] * 2
        + [pltpu.VMEM((seqs * length, hidden), LOW)] * 3,
        compiler_params=params(),
        cost_estimate=cost(20),
        name="feed",
    )(low, rows, slot, kept, up, slots, light_in, light_out, heavy_in, heavy_out)


def middle_kernel(
    tokens_ref, own_ref, other_ref, part_ref, beyond_ref, up_ref, gains_ref, routers_ref, slots_ref,
    gate_ref, mlp_ref, mlp_other_ref, mix_ref, heavy_mix_ref, light_out_ref, heavy_out_ref, down_ref,
    mixed_ref, middle_ref, grad_ref, pair_ref, weights_ref, small_ref, logit_ref, weights_acc,
):
    step = pl.program_id(0)

    @pl.when(step == 0)
    def _():
        weights_acc[...] = jnp.zeros_like(weights_acc)
        small_ref[...] = jnp.zeros_like(small_ref)

    slots = slots_ref[0]
    cap = slots.shape[0]
    middle = tokens_ref[0].astype(WIDE) + own_ref[0].astype(WIDE) + other_ref[0].astype(WIDE)
    length = middle.shape[0]
    factor = rms_of(middle)
    scaled = middle * factor
    normed = scaled * gains_ref[1:2, :]
    mixed = middle + (part_ref[0, 0].astype(WIDE) + beyond_ref[0, 0].astype(WIDE))
    mixed_ref[0] = mixed.astype(LOW)
    gate = column(mlp_ref[0], 0)
    gate_grad = column(mlp_ref[0], 1) + column(mlp_other_ref[0], 1)
    logit_grad = jnp.where(column(slots, OK_MLP) > 0, gate_grad * gate * (1.0 - gate), 0.0)
    token_grad = column(
        exact_place(hot_rows(slots, ROW_MLP, length), columns((cap, LANES), logit_grad)), 0
    )
    normed_grad = (
        part_ref[1, 0].astype(WIDE) + beyond_ref[1, 0].astype(WIDE)
    ) + token_grad * routers_ref[2:3, :]
    small_ref[0:1, :] += jnp.sum(normed_grad * scaled, axis=0, keepdims=True)
    small_ref[1:2, :] += jnp.sum(token_grad * normed, axis=0, keepdims=True)
    middle_grad = up_ref[0].astype(WIDE) + norm_back(middle, factor, normed_grad * gains_ref[1:2, :])
    middle_ref[0] = middle_grad
    low = middle_grad.astype(LOW)
    hot = hot_rows(slots, ROW_QUERY, length).astype(LOW)
    up_rows = dot(hot, low)
    weight = jnp.where(column(slots, OK_QUERY) > 0, column(gate_ref[0], 0), 0.0)
    slot = (weight * up_rows).astype(LOW)
    heavy_rows = rows_dot(heavy_mix_ref[0], heavy_out_ref[...])
    logit_ref[0] = columns(
        (cap, LANES), jnp.sum(up_rows * heavy_rows, axis=-1, keepdims=True)
    )
    mix_grad = dot(slot, heavy_out_ref[...]).astype(LOW).astype(WIDE)
    for head in range(mix_grad.shape[1] // HHD):
        pair_ref[head] = fold(head_low(mix_grad, head)).astype(LOW)
    grad_ref[0] = dot(low, light_out_ref[...]).astype(LOW)
    weights_acc[0] += cols_dot(low, mix_ref[0])
    weights_acc[1] += cols_dot(slot, heavy_mix_ref[0])

    @pl.when(step == pl.num_programs(0) - 1)
    def _():
        start, rows = down_ref.shape[0], weights_acc.shape[1]
        weights_ref[:start, :] = down_ref[...]
        for kind in range(2):
            weights_ref[start + kind * rows : start + (kind + 1) * rows, :] = weights_acc[kind].astype(LOW)


def middle_back(
    tokens, own, other, part, beyond, up, gains, routers, slots, gate, mlp, mlp_other,
    mix, heavy_mix, light_out, heavy_out, down, seq_devices,
):
    seqs, length, width = tokens.shape
    cap = slots.shape[1]
    cols = light_out.shape[1]
    heads = heavy_out.shape[1] // HHD
    shapes = [
        like(tokens.shape, LOW),
        like(tokens.shape, WIDE),
        like((seqs, length, cols), LOW),
        like((seq_devices, cap // 2, LANES), LOW),
        like((down.shape[0] + 2 * width, cols), LOW),
        like((8, width), WIDE),
        like((seqs, cap, LANES), WIDE),
    ]
    specs = [
        each(shapes[0]), each(shapes[1]), each(shapes[2]), pair_spec(shapes[3], heads),
        whole(shapes[4]), whole(shapes[5]), each(shapes[6]),
    ]
    both = pl.BlockSpec((2, 1, length, width), lambda s: (0, s, 0, 0))
    return pl.pallas_call(
        middle_kernel,
        grid=(seqs,),
        in_specs=[
            each(tokens), each(own), each(other), both, both, each(up), whole(gains),
            whole(routers), each(slots), each(gate), each(mlp), each(mlp_other), each(mix),
            each(heavy_mix), whole(light_out), whole(heavy_out), whole(down),
        ],
        out_specs=specs,
        out_shape=shapes,
        scratch_shapes=[pltpu.VMEM((2, width, cols), WIDE)],
        compiler_params=params(),
        cost_estimate=cost(11),
        name="middle_back",
    )(
        tokens, own, other, part, beyond, up, gains, routers, slots, gate, mlp, mlp_other,
        mix, heavy_mix, light_out, heavy_out, down,
    )


def light_project_kernel(local_ref, low_ref, light_ref, grad_ref, part_ref):
    @pl.when(pl.program_id(0) == 0)
    def _():
        grad_ref[...] = jnp.zeros_like(grad_ref)

    low = low_ref[0]
    part = None
    for kind in range(3):
        rows = local_ref[0, kind]
        grad_ref[kind] += cols_dot(low, rows)
        more = rows_dot(rows, light_ref[kind])
        part = more if part is None else part + more
    part_ref[0] = part


def light_project(local, low, light):
    shapes = [like(light.shape, WIDE), like(low.shape, WIDE)]
    return pl.pallas_call(
        light_project_kernel,
        grid=(low.shape[0],),
        in_specs=[each(local), each(low), whole(light)],
        out_specs=[whole(shapes[0]), each(shapes[1])],
        out_shape=shapes,
        compiler_params=params(),
        cost_estimate=cost(9),
        name="light_project",
    )(local, low, light)


def heavy_project_kernel(
    light_part_ref, low_ref, pairs_ref, heavy_ref, slots_ref, gate_ref, raw_ref, logit_ref,
    grad_ref, part_ref, both_logit_ref, grad_acc,
):
    step = pl.program_id(0)

    @pl.when(step == 0)
    def _():
        grad_acc[...] = jnp.zeros_like(grad_acc)

    low = low_ref[0]
    length = low.shape[0]
    slots = slots_ref[0]
    cap = slots.shape[0]
    heads = raw_ref.shape[2] // HHD
    key_gate = column(gate_ref[0], 1)
    query_grad = merge_heads(pairs_ref, cap, heads).astype(LOW)
    key_grad = merge_upper(pairs_ref, cap, heads).astype(LOW)
    value_grad = merge_folded(pairs_ref, cap, heads)
    raw_grad = (key_gate * value_grad).astype(LOW)
    key_logit = jnp.sum(value_grad * raw_ref[0], axis=-1, keepdims=True)
    both_logit_ref[0] = columns((cap, LANES), column(logit_ref[0], 0), key_logit)
    hot_query = hot_rows(slots, ROW_QUERY, length).astype(LOW)
    hot_key = hot_rows(slots, ROW_KEY, length).astype(LOW)
    query_in = dot(hot_query, low).astype(LOW)
    key_in = dot(hot_key, low).astype(LOW)
    grad_acc[0] += cols_dot(query_in, query_grad)
    grad_acc[1] += cols_dot(key_in, key_grad)
    grad_acc[2] += cols_dot(key_in, raw_grad)
    part = light_part_ref[0] + place_rows(hot_query, rows_dot(query_grad, heavy_ref[0]))
    part = part + place_rows(
        hot_key, rows_dot(key_grad, heavy_ref[1]) + rows_dot(raw_grad, heavy_ref[2])
    )
    part_ref[0] = part

    @pl.when(step == pl.num_programs(0) - 1)
    def _():
        grad_ref[...] = grad_acc[...].astype(LOW)


def heavy_project(light_part, low, pairs, heavy, slots, gate, raw, logit):
    heads = heavy.shape[2] // HHD
    shapes = [like(heavy.shape, LOW), like(low.shape, WIDE), like(logit.shape, WIDE)]
    return pl.pallas_call(
        heavy_project_kernel,
        grid=(low.shape[0],),
        in_specs=[
            each(light_part), each(low), pair_spec(pairs, heads), whole(heavy), each(slots),
            each(gate), each(raw), each(logit),
        ],
        out_specs=[whole(shapes[0]), each(shapes[1]), each(shapes[2])],
        out_shape=shapes,
        scratch_shapes=[pltpu.VMEM(heavy.shape, WIDE)],
        compiler_params=params(),
        cost_estimate=cost(10),
        name="heavy_project",
    )(light_part, low, pairs, heavy, slots, gate, raw, logit)


def edge_project_kernel(
    part_in_ref, low_ref, lead_ref, tail_ref, light_ref, sum_ref, grad_ref, part_ref, grad_acc
):
    step = pl.program_id(0)

    @pl.when(step == 0)
    def _():
        grad_acc[...] = sum_ref[1:]

    length = low_ref.shape[1]
    part_ref[0, WIN : length - WIN, :] = part_in_ref[0, WIN : length - WIN, :].astype(LOW)
    for ref, rows in ((lead_ref, slice(0, WIN)), (tail_ref, slice(length - WIN, length))):
        for kind in range(2):
            grad_acc[kind] += cols_dot(low_ref[0, rows, :], ref[0, kind])
        more = rows_dot(ref[0, 0], light_ref[1]) + rows_dot(ref[0, 1], light_ref[2])
        part_ref[0, rows, :] = (part_in_ref[0, rows, :] + more).astype(LOW)

    @pl.when(step == pl.num_programs(0) - 1)
    def _():
        grad_ref[0] = sum_ref[0].astype(LOW)
        grad_ref[1:] = grad_acc[...].astype(LOW)


def edge_project(part, low, lead, tail, light, light_sum):
    shapes = [like(light.shape, LOW), like(low.shape, LOW)]
    return pl.pallas_call(
        edge_project_kernel,
        grid=(low.shape[0],),
        in_specs=[each(part), each(low), each(lead), each(tail), whole(light), whole(light_sum)],
        out_specs=[whole(shapes[0]), each(shapes[1])],
        out_shape=shapes,
        scratch_shapes=[pltpu.VMEM((2,) + light.shape[1:], WIDE)],
        compiler_params=params(),
        cost_estimate=cost(5),
        name="edge_project",
    )(part, low, lead, tail, light, light_sum)


def input_kernel(
    part_ref, other_ref, logit_ref, logit_other_ref, gate_ref, slots_ref, tokens_ref, gains_ref,
    routers_ref, middle_ref, small_in_ref, grad_ref, rows_ref, small_ref,
):
    @pl.when(pl.program_id(0) == 0)
    def _():
        small_ref[...] = small_in_ref[...]
        rows_ref[...] = jnp.zeros_like(rows_ref)

    slots = slots_ref[0]
    cap = slots.shape[0]
    inputs = tokens_ref[0].astype(WIDE)
    length = inputs.shape[0]
    factor = rms_of(inputs)
    scaled = inputs * factor
    normed = scaled * gains_ref[0:1, :]
    gates = gate_ref[0]
    grads = (logit_ref[0] + logit_other_ref[0]) * gates * (1.0 - gates)
    query_logit = jnp.where(column(slots, OK_QUERY) > 0, column(grads, 0), 0.0)
    key_logit = jnp.where(column(slots, OK_KEY) > 0, column(grads, 1), 0.0)
    query_token = column(
        exact_place(hot_rows(slots, ROW_QUERY, length), columns((cap, LANES), query_logit)), 0
    )
    key_token = column(
        exact_place(hot_rows(slots, ROW_KEY, length), columns((cap, LANES), key_logit)), 0
    )
    normed_grad = (
        (part_ref[0].astype(WIDE) + other_ref[0].astype(WIDE))
        + query_token * routers_ref[0:1, :]
        + key_token * routers_ref[1:2, :]
    )
    small_ref[2:3, :] += jnp.sum(normed_grad * scaled, axis=0, keepdims=True)
    small_ref[3:4, :] += jnp.sum(query_token * normed, axis=0, keepdims=True)
    small_ref[4:5, :] += jnp.sum(key_token * normed, axis=0, keepdims=True)
    grad_ref[0] = middle_ref[0] + norm_back(inputs, factor, normed_grad * gains_ref[0:1, :])

    @pl.when(pl.program_id(0) == pl.num_programs(0) - 1)
    def _():
        cols = rows_ref.shape[1]
        sums = small_ref[...]
        folded = jnp.concatenate([sums[:, :cols], sums[:, cols:]], axis=0)
        rows_ref[: folded.shape[0], :] = folded.astype(LOW)


def input_back(
    part, other, logit, logit_other, gate, slots, tokens, gains, routers, middle, small, rows
):
    shapes = [like(middle.shape, WIDE), like((rows, small.shape[1] // 2), LOW)]
    return pl.pallas_call(
        input_kernel,
        grid=(tokens.shape[0],),
        in_specs=[
            each(part), each(other), each(logit), each(logit_other), each(gate), each(slots),
            each(tokens), whole(gains), whole(routers), each(middle), whole(small),
        ],
        out_specs=[each(shapes[0]), whole(shapes[1])],
        out_shape=shapes,
        scratch_shapes=[pltpu.VMEM(small.shape, WIDE)],
        compiler_params=params(),
        cost_estimate=cost(6),
        name="input_back",
    )(part, other, logit, logit_other, gate, slots, tokens, gains, routers, middle, small)


def heavy_weights_kernel(tile, core_ref, here_ref, there_ref, in_ref, out_ref, *refs):
    din_ref, dout_ref, rows_ref, grad_ref, hidden_ref, gate_ref, up_ref, sems = refs[-8:]

    starts = range(0, rows_ref.shape[0], tile)
    first = pl.program_id(0) == 0

    def copies(rows_from, grad_from, index):
        part = pl.ds(index * tile, tile)
        return [
            pltpu.make_async_copy(rows_from.at[part, :], rows_ref.at[part, :], sems.at[0, index]),
            pltpu.make_async_copy(grad_from.at[part, :], grad_ref.at[part, :], sems.at[1, index]),
        ]

    def fetch(rows_from, grad_from):
        for index in range(len(starts)):
            for copy in copies(rows_from, grad_from, index):
                copy.start()

    @pl.when(first & (core_ref[0, 0] == 0))
    def _():
        fetch(here_ref, there_ref)

    @pl.when(first & (core_ref[0, 0] != 0))
    def _():
        fetch(there_ref, here_ref)

    def every_tile(waits):
        for index, start in enumerate(starts):
            if waits:
                for copy in copies(here_ref, there_ref, index):
                    copy.wait()
            part = pl.ds(start, tile)
            rows = rows_ref[part, :]
            hidden, gate_grad, up_grad = gelu_parts(
                dot(rows, in_ref[0]), dot(rows, in_ref[1]), dot(grad_ref[part, :], out_ref[...])
            )
            hidden_ref[part, :] = hidden.astype(LOW)
            gate_ref[part, :] = gate_grad.astype(LOW)
            up_ref[part, :] = up_grad.astype(LOW)

    pl.when(first)(lambda: every_tile(True))
    pl.when(jnp.logical_not(first))(lambda: every_tile(False))
    dout_ref[...] = cols_dot(grad_ref[...], hidden_ref[...])
    din_ref[:, 0, :] = cols_dot(rows_ref[...], gate_ref[...])
    din_ref[:, 1, :] = cols_dot(rows_ref[...], up_ref[...])


def heavy_weights(core, here, there, weight_in, weight_out, first_block, count_blocks, done):
    count, width = here.shape
    hidden = weight_out.shape[1]
    cols = 256
    tile = 512 if count % 512 == 0 else count
    out_block = pl.BlockSpec((width, cols), lambda i: (0, first_block + i))
    in_block = pl.BlockSpec((width, 2, cols), lambda i: (0, 0, first_block + i))
    return pl.pallas_call(
        lambda *refs: heavy_weights_kernel(tile, *refs),
        grid=(count_blocks,),
        in_specs=[
            pl.BlockSpec(memory_space=pltpu.SMEM),
            pl.BlockSpec(memory_space=pl.ANY),
            pl.BlockSpec(memory_space=pl.ANY),
            pl.BlockSpec((2, width, cols), lambda i: (0, 0, first_block + i)),
            out_block,
        ]
        + [pl.BlockSpec(memory_space=pl.ANY)] * len(done),
        out_specs=[in_block, out_block],
        out_shape=[like((width, 2, hidden), WIDE), like((width, hidden), WIDE)],
        scratch_shapes=[pltpu.VMEM((count, width), LOW)] * 2
        + [pltpu.VMEM((count, cols), LOW)] * 3
        + [pltpu.SemaphoreType.DMA((2, count // tile))],
        input_output_aliases={5 + i: i for i in range(len(done))},
        compiler_params=params(60),
        cost_estimate=cost(4 + 9 * count_blocks * count / 3072),
        name="heavy_weights",
    )(core, here, there, weight_in, weight_out, *done)


def bit_pairs(bit):
    return [(i, i ^ (1 << bit)) for i in range(lax.axis_size("seq"))]


def bit_here(bit):
    return (lax.axis_index("seq") >> bit) & 1


def after(value, *others):
    return lax.optimization_barrier((value,) + others)[0]


def scatter_start(value, bit):
    halves = value.reshape(2, value.shape[0] // 2, value.shape[1])
    mine = bit_here(bit)
    sent = lax.dynamic_index_in_dim(halves, 1 - mine, 0, keepdims=False)
    kept = lax.dynamic_index_in_dim(halves, mine, 0, keepdims=False)
    return kept, lax.ppermute(sent, "seq", bit_pairs(bit))


def scatter_end(started, *others):
    kept, got = started
    got = after(got, *others)
    return (kept.astype(WIDE) + got.astype(WIDE)).astype(LOW)


def gather_start(value, bit):
    return value, lax.ppermute(value, "seq", bit_pairs(bit)), bit_here(bit)


def gather_end(started, *others):
    value, got, mine = started
    got = after(got, *others)
    return jnp.where(
        mine == 0,
        jnp.concatenate([value, got], axis=0),
        jnp.concatenate([got, value], axis=0),
    )


def interleave(parts, blocks):
    cut = [p.reshape(blocks, -1, p.shape[1]) for p in parts]
    return jnp.concatenate(cut, axis=1).reshape(-1, parts[0].shape[1])


def apart(value, blocks, rows):
    cut = value.reshape(blocks, -1, value.shape[1])
    marks = [sum(rows[:i]) // blocks for i in range(len(rows) + 1)]
    return [
        cut[:, marks[i] : marks[i + 1]].reshape(-1, value.shape[1]) for i in range(len(rows))
    ]


def in_order(bit_ref, mine_ref, got_ref, body):
    pl.when(bit_ref[0, 0] == 0)(lambda: body(mine_ref, got_ref))
    pl.when(bit_ref[0, 0] != 0)(lambda: body(got_ref, mine_ref))


def finish_call(kernel, bit, mine, got, shapes, name):
    shapes = [like(shape, WIDE) for shape in shapes]
    return pl.pallas_call(
        kernel,
        in_specs=[
            pl.BlockSpec(memory_space=pltpu.SMEM),
            pl.BlockSpec(memory_space=pltpu.VMEM),
            pl.BlockSpec(memory_space=pltpu.VMEM),
        ],
        out_shape=shapes,
        compiler_params=params(),
        name=name,
    )(bit_here(bit).astype(jnp.int32).reshape(1, 1), mine, got)


def feed_in_kernel(bit_ref, mine_ref, got_ref, in_ref):
    width, _, hidden = in_ref.shape

    def body(*halves):
        for kind, ref in enumerate(halves):

            def store(rows, cols, value, kind=kind):
                in_ref[rows, kind, cols] = value.astype(WIDE)

            unpack_wide(store, ref, 0, width, hidden - ref.shape[1])

    in_order(bit_ref, mine_ref, got_ref, body)


def outs_kernel(bit_ref, mine_ref, got_ref, feed_ref, light_ref, heavy_ref):
    width, hidden = feed_ref.shape

    def body(first_ref, second_ref):
        half, cols = first_ref.shape

        def store(rows, lanes, value):
            feed_ref[rows, lanes] = value.astype(WIDE)

        unpack_wide(store, first_ref, 0, width, hidden - cols)
        start = width * hidden // cols
        light_ref[: half - start, :] = first_ref[start:, :].astype(WIDE)
        rest = width - (half - start)
        light_ref[half - start :, :] = second_ref[:rest, :].astype(WIDE)
        heavy_ref[...] = second_ref[rest:, :].astype(WIDE)

    in_order(bit_ref, mine_ref, got_ref, body)


def kinds_kernel(bit_ref, mine_ref, got_ref, wide_ref):
    def body(first_ref, second_ref):
        half = first_ref.shape[0]
        wide_ref[:half, :] = first_ref[...].astype(WIDE)
        wide_ref[half:, :] = second_ref[...].astype(WIDE)

    in_order(bit_ref, mine_ref, got_ref, body)


def widen(bit, mine, got, name):
    rows, cols = mine.shape
    half = pl.BlockSpec((rows, LANES), lambda i: (0, i))
    return pl.pallas_call(
        kinds_kernel,
        grid=(cols // LANES,),
        in_specs=[pl.BlockSpec(memory_space=pltpu.SMEM), half, half],
        out_specs=pl.BlockSpec((2 * rows, LANES), lambda i: (0, i)),
        out_shape=like((2 * rows, cols), WIDE),
        compiler_params=params(24),
        name=name,
    )(bit_here(bit).astype(jnp.int32).reshape(1, 1), mine, got)


def other_core(value):
    return lax.ppermute(value, "mp", [(0, 1), (1, 0)])


def to_neighbours(first, last):
    peers = lax.axis_size("seq")
    up = [(i, i + 1) for i in range(peers - 1)]
    down = [(i + 1, i) for i in range(peers - 1)]
    return lax.ppermute(last, "seq", up), lax.ppermute(first, "seq", down)


def exchange(pairs):
    return lax.all_to_all(pairs, "seq", split_axis=0, concat_axis=0, tiled=True)


def by_kind(weights):
    return weights.transpose(1, 0, 2)


def shards(
    tokens,
    out_grad,
    gains,
    routers,
    light_query_key_value_weight,
    light_attention_output_weight,
    heavy_qkv,
    heavy_out,
    light_feedforward_input_weight,
    light_feedforward_output_weight,
    heavy_mlp_in,
    heavy_mlp_out,
    routed_queries,
    routed_keys,
    routed_mlp,
    block_counts,
):
    seq_count, local_len, width = tokens.shape
    seq_devices = lax.axis_size("seq")
    row_base = lax.axis_index("seq") * local_len
    capacity = routed_queries.shape[1]
    light_cols = light_query_key_value_weight.shape[2]
    gain_rows, router_rows = gains.T, routers.T
    slot_ids = jnp.arange(capacity, dtype=jnp.int32)[None, :, None]
    rows = jnp.stack([routed_queries, routed_keys, routed_mlp], axis=2) - row_base
    valid = (slot_ids < block_counts).astype(jnp.int32)
    slots = jnp.concatenate([rows, valid], axis=2)
    place = jnp.stack([row_base, jnp.int32(seq_devices * local_len)]).astype(jnp.int32)[None, :]
    core = lax.axis_index("mp").astype(jnp.int32).reshape(1, 1)
    light_weights = by_kind(light_query_key_value_weight)
    heavy_weights_qkv = by_kind(heavy_qkv)

    own_tokens = lax.dynamic_index_in_dim(tokens, lax.axis_index("mp"), 0, keepdims=False)
    edges = to_neighbours(own_tokens[:WIN], own_tokens[local_len - WIN :])
    low, pairs, raw, gate = front(
        tokens, gain_rows, router_rows, slots, heavy_weights_qkv, seq_devices
    )
    edges = [after(edge, low) for edge in edges]
    first_core = lax.axis_index("mp") == 0
    before, behind = [
        jnp.where(first_core, jnp.stack([mine, more]), jnp.stack([more, mine]))
        for mine, more in zip(edges, [other_core(edge) for edge in edges])
    ]
    pair = exchange(after(pairs, before, behind))
    mix, attn, lse, query, window = light_forward(
        place, low, before, behind, gain_rows, light_weights, light_attention_output_weight
    )
    pair_query, pair_key, pair_value, kept, pair_mix = heavy_forward(after(pair, attn))
    mix_pairs = exchange(pair_mix)
    light_in = by_kind(after(light_feedforward_input_weight, kept))
    heavy_in = by_kind(after(heavy_mlp_in, kept))
    own, heavy_mix = combine(after(mix_pairs, light_in, heavy_in), attn, heavy_out, slots, gate)
    other = other_core(own)
    low_two, rows, slot, ship, gate_two = mlp_slots(
        core, tokens, own, other, out_grad, gain_rows, router_rows, slots
    )
    all_slots = seq_count * capacity * seq_devices
    gather_heavy = 2 * all_slots * width < 4 * (heavy_mlp_in.size + heavy_mlp_out.size)
    here = lax.all_gather(ship, "seq", axis=1, tiled=True) if gather_heavy else ship
    part, feed_grads, down_grad, mlp = feed(
        low_two, rows, slot, gate_two, out_grad, slots, light_in, light_feedforward_output_weight,
        heavy_in, heavy_mlp_out, light_cols,
    )
    beyond, mlp_other = other_core(part), other_core(mlp)
    bits = (seq_devices - 1).bit_length()
    blocks = 1 << (bits - 2)
    first_going = scatter_start(feed_grads.reshape(-1, light_cols), 0)
    mixed, middle_grad, mix_grad, grad_pairs, out_grads, small, query_logit = middle_back(
        tokens, own, other, part, beyond, out_grad, gain_rows, router_rows, slots, gate, mlp,
        mlp_other, mix, heavy_mix, light_attention_output_weight, heavy_out, down_grad, seq_devices,
    )
    pair_grad = exchange(grad_pairs)
    local, early, late = light_backward(place, query, window, lse, mix_grad)
    first_wave = scatter_end(first_going, local)
    lead, tail = to_neighbours(early, late)
    triple = heavy_backward(
        pair_query, pair_key, pair_value, kept, after(pair_grad, local, first_wave)
    )
    triple_pairs = exchange(triple)
    second_going = scatter_start(after(out_grads, triple), 1)
    light_sums, light_part = light_project(after(local, triple), low, light_weights)
    heavy_grads, part_sum, logit = heavy_project(
        light_part, low, triple_pairs, heavy_weights_qkv, slots, gate, raw, query_logit
    )
    second_wave = scatter_end(second_going, part_sum)
    light_grads, low_part = edge_project(
        after(part_sum, second_wave), low, lead, tail, light_weights, light_sums
    )
    heavy_going = scatter_start(heavy_grads.reshape(-1, light_cols), 1)
    light_going = scatter_start(light_grads.reshape(-1, light_cols), 0)
    second_going = scatter_start(after(second_wave, low_part), 0)
    first_going = scatter_start(after(first_wave, low_part), 1)
    low_other, logit_other = other_core(low_part), other_core(logit)
    here = after(here, low_part)
    there = other_core(here).reshape(-1, width)
    here = here.reshape(-1, width)
    blocks_done = [0]
    heavy_sums = []

    def heavy_piece(count, *others):
        heavy_sums[:] = heavy_weights(
            core, after(here, *others), there, heavy_in, heavy_mlp_out, blocks_done[0], count, heavy_sums
        )
        blocks_done[0] += count
        return heavy_sums[1]

    input_grad, small_rows = input_back(
        low_part, low_other, logit, logit_other, gate, slots, tokens, gain_rows,
        router_rows, middle_grad, small, 16 * blocks,
    )
    small_got = lax.ppermute(small_rows, "seq", bit_pairs(1))
    second_wave = scatter_end(second_going, input_grad)
    first_wave = scatter_end(first_going, input_grad)
    early_sizes = [first_wave.shape[0], second_wave.shape[0]]
    wave = interleave([first_wave, second_wave], blocks)
    going = scatter_start(wave, 2)
    mark = heavy_piece(2, input_grad, wave)
    wave = scatter_end(going, mark)
    heavy_wave = scatter_end(heavy_going, mark)
    light_wave = scatter_end(light_going, mark)
    light_going = scatter_start(light_wave, 1)
    small_rows = scatter_end((small_rows, small_got), mark)
    for bit in range(3, bits - 1):
        wave = scatter_end(scatter_start(wave, bit))
    going = scatter_start(wave, bits - 1)
    heavy_going = scatter_start(heavy_wave, 0)
    small_got = lax.ppermute(small_rows, "seq", bit_pairs(0))
    mark = heavy_piece(1, wave, heavy_wave, light_wave, small_rows)
    wave = scatter_end(going, mark)
    heavy_wave = scatter_end(heavy_going, mark)
    light_wave = scatter_end(light_going, mark)
    small_rows = scatter_end((small_rows, small_got), mark)
    for bit in reversed(range(4, bits)):
        wave = gather_end(gather_start(wave, bit))
    going = gather_start(wave, 3)
    late_wave = [light_wave, heavy_wave, small_rows]
    late_sizes = [p.shape[0] for p in late_wave]
    late_wave = interleave(late_wave, blocks)
    late_going = scatter_start(late_wave, 2)
    mark = heavy_piece(1, late_wave, wave)
    wave = gather_end(going, mark)
    late_wave = scatter_end(late_going, mark)
    for bit in range(3, bits - 1):
        late_wave = scatter_end(scatter_start(late_wave, bit))
    going = gather_start(wave, 2)
    late_going = scatter_start(late_wave, bits - 1)
    mark = heavy_piece(1, late_wave, wave)
    wave = apart(gather_end(going, mark), blocks, early_sizes)
    going = [gather_start(p, bit) for p, bit in zip(wave, (1, 0))]
    late_wave = scatter_end(late_going, mark)
    for bit in reversed(range(4, bits)):
        late_wave = gather_end(gather_start(late_wave, bit))
    late_going = gather_start(late_wave, 3)
    mark = heavy_piece(1, late_wave, *wave)
    wave = [gather_end(p, mark) for p in going]
    early_halves = [(p, lax.ppermute(p, "seq", bit_pairs(bit))) for p, bit in zip(wave, (0, 1))]
    late_wave = gather_end(late_going, mark)
    late_going = gather_start(late_wave, 2)
    mark = heavy_piece(1, late_wave, *wave)
    late_wave = apart(gather_end(late_going, mark), blocks, late_sizes)
    small_sum = late_wave.pop().astype(WIDE)
    late_going = [gather_start(p, bit) for p, bit in zip(late_wave, (1, 0))]
    early_halves = [(after(p, *late_wave), after(got, mark)) for p, got in early_halves]
    hidden = light_feedforward_output_weight.shape[1]
    square = (width, light_cols)
    (feed_in,) = finish_call(feed_in_kernel, 0, *early_halves[0], [(width, 2, hidden)], "feed_in")
    feed_out, light_out_sum, heavy_out_sum = finish_call(
        outs_kernel, 1, *early_halves[1], [(width, hidden), square, square], "outs"
    )
    late_wave = [gather_end(p, feed_in, feed_out) for p in late_going]
    late_halves = [
        (p, lax.ppermute(p, "seq", bit_pairs(bit))) for p, bit in zip(late_wave, (0, 1))
    ]
    mark = heavy_piece(1, *late_wave)
    late_halves = [(p, after(got, mark)) for p, got in late_halves]
    heavy_in_grad, heavy_out_grad = heavy_sums
    if not gather_heavy:
        sums = [heavy_in_grad[:, 0], heavy_in_grad[:, 1], heavy_out_grad]
        sums = [p.astype(LOW) for p in sums]
        for bit in range(bits):
            sums = [scatter_end(scatter_start(p, bit)) for p in sums]
        for bit in reversed(range(bits)):
            sums = [gather_end(gather_start(p, bit)) for p in sums]
        heavy_in_grad = jnp.stack(sums[:2], axis=1).astype(WIDE)
        heavy_out_grad = sums[2].astype(WIDE)
    light_sum = widen(0, *late_halves[0], "light_sum")
    heavy_sum = widen(1, *late_halves[1], "heavy_sum")
    small_sum = jnp.concatenate([small_sum[:8], small_sum[8:16]], axis=1)
    return (
        mixed,
        input_grad,
        light_sum.reshape(3, width, light_cols).transpose(1, 0, 2),
        light_out_sum,
        heavy_sum.reshape(3, width, light_cols).transpose(1, 0, 2),
        heavy_out_sum,
        feed_in,
        feed_out,
        heavy_in_grad,
        heavy_out_grad,
        jnp.stack([small_sum[2], small_sum[0]], axis=1),
        jnp.stack([small_sum[3], small_sum[4], small_sum[1]], axis=1),
    )


def solution(mesh):
    rows = P(None, "seq", None)
    by_column = P(None, None, "mp")
    by_hidden = P(None, "mp")
    slots = P(None, "seq")
    weights = (by_column, by_hidden) * 4
    return jax.shard_map(
        shards,
        mesh=mesh,
        in_specs=(rows, rows, P(), P()) + weights + (slots, slots, slots, rows),
        out_specs=(rows, rows) + weights + (P(), P()),
        check_vma=False,
    )
```

```python
import math

import jax
import jax.numpy as jnp
from jax import lax
from jax.experimental import pallas as pl
from jax.experimental.pallas import tpu as pltpu
from jax.sharding import PartitionSpec as P

LHD = 96
HHD = 64
WIN = 128
LANES = 128

EPSILON = 1e-06
MASKED = -1e30
MARK = 1e30
EXACT = lax.Precision.HIGHEST
LOW = jnp.bfloat16
WIDE = jnp.float32

ROW_QUERY, ROW_KEY, ROW_MLP, OK_QUERY, OK_KEY, OK_MLP = range(6)


def lanes_of(shape):
    return lax.broadcasted_iota(jnp.int32, shape, len(shape) - 1)


def dot(a, b):
    return jnp.dot(a, b, preferred_element_type=WIDE)


def rows_dot(a, b):
    return lax.dot_general(a, b, (((1,), (1,)), ((), ())), preferred_element_type=WIDE)


def cols_dot(a, b):
    return lax.dot_general(a, b, (((0,), (0,)), ((), ())), preferred_element_type=WIDE)


def rms_of(values):
    return lax.rsqrt(jnp.mean(values * values, axis=-1, keepdims=True) + EPSILON)


def column(values, index):
    return values[:, index : index + 1]


def columns(shape, *parts):
    lane = lanes_of(shape)
    out = jnp.zeros(shape, WIDE)
    for index, part in enumerate(parts):
        out = jnp.where(lane == index, part, out)
    return out


def hot_rows(slots, index, length):
    rows = column(slots, index)
    return (lanes_of((rows.shape[0], length)) == rows).astype(WIDE)


def place_rows(hot, values):
    high = values.astype(LOW)
    rest = (values - high.astype(WIDE)).astype(LOW)
    return cols_dot(hot, high) + cols_dot(hot, rest)


def exact_place(hot, values):
    return lax.dot_general(
        hot, values, (((0,), (0,)), ((), ())), precision=EXACT, preferred_element_type=WIDE
    )


def exact_pick(hot, values):
    return jnp.dot(hot, values, precision=EXACT, preferred_element_type=WIDE)


def row_dots(values, vector):
    return jnp.sum(values * vector, axis=-1, keepdims=True)


def norm_back(values, factor, weighted):
    inner = jnp.mean(weighted * values, axis=-1, keepdims=True)
    return factor * weighted - values * (factor * factor * factor) * inner


def gelu_parts(gate, up, hidden_grad):
    root = math.sqrt(2.0 / math.pi)
    cube = 0.044715 * root
    square = gate * gate
    bend = jnp.tanh(gate * (root + cube * square))
    half = 0.5 + 0.5 * bend
    value = gate * half
    slope = half + gate * (1.0 - bend * bend) * (0.5 * root + (1.5 * cube) * square)
    return value * up, slope * up * hidden_grad, value * hidden_grad


def merge_heads(ref, rows, heads):
    tiles = []
    for head in range(0, heads, 2):
        first = ref[head, :rows, :].astype(WIDE)
        second = ref[head + 1, :rows, :].astype(WIDE)
        lane = lanes_of(first.shape)
        tiles.append(jnp.where(lane < HHD, first, pltpu.roll(second, HHD, 1)))
    return jnp.concatenate(tiles, axis=1)


def merge_upper(ref, rows, heads):
    tiles = []
    for head in range(0, heads, 2):
        first = ref[head, :rows, :].astype(WIDE)
        second = ref[head + 1, :rows, :].astype(WIDE)
        lane = lanes_of(first.shape)
        tiles.append(jnp.where(lane < HHD, pltpu.roll(first, HHD, 1), second))
    return jnp.concatenate(tiles, axis=1)


def head_low(values, head):
    tile = values[:, head // 2 * LANES : (head // 2 + 1) * LANES]
    return tile if head % 2 == 0 else pltpu.roll(tile, HHD, 1)


def head_high(values, head):
    tile = values[:, head // 2 * LANES : (head // 2 + 1) * LANES]
    return tile if head % 2 == 1 else pltpu.roll(tile, HHD, 1)


def fold(values):
    half = values.shape[0] // 2
    lane = lanes_of((half, LANES))
    return jnp.where(lane < HHD, values[:half], pltpu.roll(values[half:], HHD, 1))


def unfold(folded):
    lane = lanes_of(folded.shape)
    return jnp.concatenate(
        [
            jnp.where(lane < HHD, folded, 0.0),
            jnp.where(lane < HHD, pltpu.roll(folded, HHD, 1), 0.0),
        ],
        axis=0,
    )


def merge_folded(ref, start, heads):
    tiles = []
    for head in range(0, heads, 2):
        first = ref[head, start:, :].astype(WIDE)
        second = ref[head + 1, start:, :].astype(WIDE)
        lane = lanes_of(first.shape)
        upper = jnp.where(lane < HHD, first, pltpu.roll(second, HHD, 1))
        lower = jnp.where(lane < HHD, pltpu.roll(first, HHD, 1), second)
        tiles.append(jnp.concatenate([upper, lower], axis=0))
    return jnp.concatenate(tiles, axis=1)


def spread_matrix(heads):
    row = lax.broadcasted_iota(jnp.int32, (heads * LHD, heads * LANES), 0)
    lane = lanes_of((heads * LHD, heads * LANES))
    inner = lane & (LANES - 1)
    hit = (row == (lane >> 7) * LHD + inner) & (inner < LHD)
    return hit.astype(WIDE).astype(LOW)


def params(mib=56):
    return pltpu.CompilerParams(vmem_limit_bytes=mib * 2**20)


def cost(microseconds):
    return pl.CostEstimate(
        flops=int(microseconds * 2e7), bytes_accessed=2**10, transcendentals=0
    )


def whole(array):
    zeros = (0,) * array.ndim
    return pl.BlockSpec(array.shape, lambda *_: zeros, pipeline_mode=pl.Buffered(1))


def each(array):
    rest = (0,) * (array.ndim - 1)
    return pl.BlockSpec((1,) + array.shape[1:], lambda s: (s,) + rest)


def like(shape, kind):
    return jax.ShapeDtypeStruct(shape, kind)


def front_kernel(
    tokens_ref, gains_ref, routers_ref, slots_ref, heavy_ref, low_ref, pair_ref, raw_ref, gate_ref,
):
    inputs = tokens_ref[0].astype(WIDE)
    length = inputs.shape[0]
    normed = inputs * rms_of(inputs) * gains_ref[0:1, :]
    low = normed.astype(LOW)
    low_ref[0] = low
    slots = slots_ref[0]
    hot_query = hot_rows(slots, ROW_QUERY, length)
    hot_key = hot_rows(slots, ROW_KEY, length)
    logits = columns(
        (length, LANES),
        row_dots(normed, routers_ref[0:1, :]),
        row_dots(normed, routers_ref[1:2, :]),
    )
    query_gate = jax.nn.sigmoid(column(exact_pick(hot_query, logits), 0))
    key_gate = jax.nn.sigmoid(column(exact_pick(hot_key, logits), 1))
    gate_ref[0] = columns((slots.shape[0], LANES), query_gate, key_gate)
    query_in = dot(hot_query.astype(LOW), low).astype(LOW)
    key_in = dot(hot_key.astype(LOW), low).astype(LOW)
    query = dot(query_in, heavy_ref[0]).astype(LOW).astype(WIDE)
    key = dot(key_in, heavy_ref[1]).astype(LOW).astype(WIDE)
    raw = dot(key_in, heavy_ref[2])
    raw_ref[0] = raw
    value = (key_gate * raw).astype(LOW).astype(WIDE)
    value = jnp.where(column(slots, OK_KEY) > 0, value, MARK)
    cap = slots.shape[0]
    lane = lanes_of((cap, LANES))
    for head in range(raw.shape[1] // HHD):
        both = jnp.where(lane < HHD, head_low(query, head), head_high(key, head))
        pair_ref[head, :cap, :] = both.astype(LOW)
        pair_ref[head, cap:, :] = fold(head_low(value, head)).astype(LOW)


def front(tokens, gains, routers, slots, heavy, seq_devices):
    seqs, length, width = tokens.shape
    cap = slots.shape[1]
    heavy_cols = heavy.shape[2]
    heads = heavy_cols // HHD
    shapes = [
        like(tokens.shape, LOW),
        like((seq_devices, 3 * cap // 2, LANES), LOW),
        like((seqs, cap, heavy_cols), WIDE),
        like((seqs, cap, LANES), WIDE),
    ]
    specs = [each(s) for s in shapes]
    specs[1] = pl.BlockSpec((heads, 3 * cap // 2, LANES), lambda s: (s, 0, 0))
    return pl.pallas_call(
        front_kernel,
        grid=(seqs,),
        in_specs=[each(tokens), whole(gains), whole(routers), each(slots), whole(heavy)],
        out_specs=specs,
        out_shape=shapes,
        compiler_params=params(),
        cost_estimate=cost(8),
        name="front",
    )(tokens, gains, routers, slots, heavy)


def window_bias(block, length, base, total):
    row = lax.broadcasted_iota(jnp.int32, (WIN, 3 * WIN), 0)
    col = lanes_of((WIN, 3 * WIN))
    place = base + (block - 1) * WIN + col
    near = jnp.abs(col - WIN - row) < WIN
    return jnp.where(near & (place >= 0) & (place < total), 0.0, MASKED)


def light_forward_kernel(
    scale, place_ref, low_ref, before_ref, after_ref, gains_ref, weight_ref, out_ref,
    mix_ref, attn_ref, lse_ref, query_ref, window_ref, wide_ref,
):
    length, heads = low_ref.shape[1], weight_ref.shape[2] // LHD
    spread = spread_matrix(heads)

    def heads_of(rows, kind):
        projected = dot(rows, weight_ref[kind]).astype(LOW)
        return dot(projected, spread).astype(LOW)

    query_ref[0] = heads_of(low_ref[0], 0)
    edges = ((before_ref, slice(0, WIN)), (after_ref, slice(WIN + length, 2 * WIN + length)))
    for ref, rows in edges:
        inputs = ref[0].astype(WIDE)
        low = (inputs * rms_of(inputs) * gains_ref[0:1, :]).astype(LOW)
        for kind in range(2):
            window_ref[0, kind, rows, :] = heads_of(low, 1 + kind)
    for kind in range(2):
        window_ref[0, kind, WIN : WIN + length, :] = heads_of(low_ref[0], 1 + kind)
    for block in range(length // WIN):
        rows = slice(block * WIN, (block + 1) * WIN)
        near = slice(block * WIN, (block + 3) * WIN)
        bias = window_bias(block, length, place_ref[0, 0], place_ref[0, 1])
        lanes = [slice(head * LANES, (head + 1) * LANES) for head in range(heads)]
        scores = jnp.concatenate(
            [
                rows_dot(query_ref[0, rows, at], window_ref[0, 0, near, at]) * scale + bias
                for at in lanes
            ],
            axis=0,
        )
        top = jnp.max(scores, axis=-1, keepdims=True)
        expo = jnp.exp(scores - top)
        total = jnp.sum(expo, axis=-1, keepdims=True)
        lse = top + jnp.log(total)
        share = 1.0 / total
        expo = expo.astype(LOW)
        kept = []
        for head, at in enumerate(lanes):
            mine = slice(head * WIN, (head + 1) * WIN)
            mixed = dot(expo[mine], window_ref[0, 1, near, at]) * share[mine]
            wide_ref[rows, at] = mixed.astype(LOW)
            kept.append(lse[mine])
        lse_ref[0, rows, :] = columns((WIN, LANES), *kept)
    mix = rows_dot(wide_ref[...], spread).astype(LOW)
    mix_ref[0] = mix
    attn_ref[0] = rows_dot(mix, out_ref[...])


def light_forward(place, low, before, after, gains, weight, weight_out):
    seqs, length, _ = low.shape
    light_cols = weight.shape[2]
    heads = light_cols // LHD
    shapes = [
        like((seqs, length, light_cols), LOW),
        like((seqs, length, weight_out.shape[0]), WIDE),
        like((seqs, length, LANES), WIDE),
        like((seqs, length, heads * LANES), LOW),
        like((seqs, 2, length + 2 * WIN, heads * LANES), LOW),
    ]
    return pl.pallas_call(
        lambda *refs: light_forward_kernel(1.0 / math.sqrt(LHD), *refs),
        grid=(seqs,),
        in_specs=[
            pl.BlockSpec(memory_space=pltpu.SMEM),
            each(low),
            each(before),
            each(after),
            whole(gains),
            whole(weight),
            whole(weight_out),
        ],
        out_specs=[each(s) for s in shapes],
        out_shape=shapes,
        scratch_shapes=[pltpu.VMEM((length, heads * LANES), LOW)],
        compiler_params=params(),
        cost_estimate=cost(15),
        name="light_forward",
    )(place, low, before, after, gains, weight, weight_out)


def light_backward_kernel(
    scale, place_ref, query_ref, window_ref, lse_ref, grad_ref, local_ref, early_ref, late_ref, *scratch
):
    wide_ref, dkey_ref, dvalue_ref = scratch
    length, light_cols = grad_ref.shape[1:]
    heads = light_cols // LHD
    spread = spread_matrix(heads)
    grad = dot(grad_ref[0], spread).astype(LOW)
    dkey_ref[...] = jnp.zeros_like(dkey_ref)
    dvalue_ref[...] = jnp.zeros_like(dvalue_ref)
    for block in range(length // WIN):
        rows = slice(block * WIN, (block + 1) * WIN)
        near = slice(block * WIN, (block + 3) * WIN)
        bias = window_bias(block, length, place_ref[0, 0], place_ref[0, 1])
        lse = lse_ref[0, rows, :]
        lanes = [slice(head * LANES, (head + 1) * LANES) for head in range(heads)]
        scores = jnp.concatenate(
            [
                rows_dot(query_ref[0, rows, at], window_ref[0, 0, near, at]) * scale
                + (bias - column(lse, head))
                for head, at in enumerate(lanes)
            ],
            axis=0,
        )
        prob_grad = jnp.concatenate(
            [rows_dot(grad[rows, at], window_ref[0, 1, near, at]) for at in lanes], axis=0
        )
        probs = jnp.exp(scores)
        delta = jnp.sum(probs * prob_grad, axis=-1, keepdims=True)
        score_grad = (probs * (prob_grad - delta)).astype(LOW)
        probs = probs.astype(LOW)
        for head, at in enumerate(lanes):
            mine = slice(head * WIN, (head + 1) * WIN)
            part = score_grad[mine]
            wide_ref[rows, at] = (dot(part, window_ref[0, 0, near, at]) * scale).astype(LOW)
            dkey_ref[near, at] += cols_dot(part, query_ref[0, rows, at]) * scale
            dvalue_ref[near, at] += cols_dot(probs[mine], grad[rows, at])
    local_ref[0, 0] = rows_dot(wide_ref[...], spread).astype(LOW)
    for kind, ref in ((1, dkey_ref), (2, dvalue_ref)):
        all_rows = rows_dot(ref[...].astype(LOW), spread).astype(LOW)
        early_ref[0, kind - 1] = all_rows[:WIN]
        local_ref[0, kind] = all_rows[WIN : WIN + length]
        late_ref[0, kind - 1] = all_rows[WIN + length :]


def light_backward(place, query, window, lse, grad):
    seqs, length, light_cols = grad.shape
    edge = like((seqs, 2, WIN, light_cols), LOW)
    shapes = [like((seqs, 3, length, light_cols), LOW), edge, edge]
    return pl.pallas_call(
        lambda *refs: light_backward_kernel(1.0 / math.sqrt(LHD), *refs),
        grid=(seqs,),
        in_specs=[
            pl.BlockSpec(memory_space=pltpu.SMEM),
            each(query),
            each(window),
            each(lse),
            each(grad),
        ],
        out_specs=[each(s) for s in shapes],
        out_shape=shapes,
        scratch_shapes=[
            pltpu.VMEM(query.shape[1:], LOW),
            pltpu.VMEM(window.shape[2:], WIDE),
            pltpu.VMEM(window.shape[2:], WIDE),
        ],
        compiler_params=params(),
        cost_estimate=cost(14),
        name="light_backward",
    )(place, query, window, lse, grad)


def heavy_forward_kernel(scale, pair_ref, query_ref, key_ref, value_ref, kept_ref, mix_ref):
    devices, rows, _ = pair_ref.shape
    cap = 2 * rows // 3
    tile = kept_ref.shape[0]

    @pl.when(pl.program_id(0) == 0)
    def _():
        def unpack(index, carry):
            lane = lanes_of((cap, LANES))
            at = pl.ds(pl.multiple_of(index * cap, 16), cap)
            both = pair_ref[index, :cap, :].astype(WIDE)
            value = unfold(pair_ref[index, cap:, :].astype(WIDE))
            unused = column(value, 0) > 0.5 * MARK
            bias = jnp.where(unused, MASKED, 0.0)
            query = jnp.where(lane < HHD, both * scale, jnp.where(lane == HHD, 1.0, 0.0))
            key = jnp.where(
                lane < HHD, pltpu.roll(both, HHD, 1), jnp.where(lane == HHD, bias, 0.0)
            )
            query_ref[at, :] = query.astype(LOW)
            key_ref[at, :] = key.astype(LOW)
            value_ref[at, :] = jnp.where(unused, 0.0, value).astype(LOW)
            return carry

        lax.fori_loop(0, devices, unpack, 0, unroll=devices <= 16)

    start = pl.multiple_of(pl.program_id(0) * tile, 16)
    scores = rows_dot(query_ref[pl.ds(start, tile), :], key_ref[...])
    top = jnp.max(scores, axis=-1, keepdims=True)
    expo = jnp.exp(scores - top)
    total = jnp.sum(expo, axis=-1, keepdims=True)
    mix = dot(expo.astype(LOW), value_ref[...]) / total
    lane = lanes_of(mix.shape)
    kept_ref[...] = jnp.where(lane < HHD, mix, top + jnp.log(total))
    for index in range(tile // cap):
        mix_ref[index] = fold(mix[index * cap : (index + 1) * cap]).astype(LOW)


def heavy_backward_kernel(
    scale, query_ref, key_ref, value_ref, kept_ref, grad_ref, triple_ref, dq_ref, dk_ref, dv_ref
):
    step = pl.program_id(0)
    devices, rows, _ = triple_ref.shape
    cap = 2 * rows // 3
    tile = kept_ref.shape[0]

    @pl.when(step == 0)
    def _():
        dk_ref[...] = jnp.zeros_like(dk_ref)
        dv_ref[...] = jnp.zeros_like(dv_ref)

    start = pl.multiple_of(step * tile, 16)
    query = query_ref[pl.ds(start, tile), :]
    grad = jnp.concatenate(
        [unfold(grad_ref[index].astype(WIDE)) for index in range(tile // cap)], axis=0
    )
    kept = kept_ref[...]
    lse = column(kept, HHD)
    delta = jnp.sum(kept * grad, axis=-1, keepdims=True)
    grad = grad.astype(LOW)
    probs = jnp.exp(rows_dot(query, key_ref[...]) - lse)
    prob_grad = rows_dot(grad, value_ref[...])
    score_grad = (probs * (prob_grad - delta)).astype(LOW)
    dq_ref[pl.ds(start, tile), :] = dot(score_grad, key_ref[...]) * scale
    dk_ref[...] += cols_dot(score_grad, query)
    dv_ref[...] += cols_dot(probs.astype(LOW), grad)

    @pl.when(step == pl.num_programs(0) - 1)
    def _():
        def pack(index, carry):
            lane = lanes_of((cap, LANES))
            at = pl.ds(pl.multiple_of(index * cap, 16), cap)
            moved = pltpu.roll(dk_ref[at, :], HHD, 1)
            triple_ref[index, :cap, :] = jnp.where(lane < HHD, dq_ref[at, :], moved).astype(LOW)
            triple_ref[index, cap:, :] = fold(dv_ref[at, :]).astype(LOW)
            return carry

        lax.fori_loop(0, devices, pack, 0, unroll=devices <= 16)


def query_tile(devices, cap):
    return 4 * cap if devices <= 32 else cap


def heavy_forward(pair):
    devices, rows, _ = pair.shape
    cap = 2 * rows // 3
    length, tile = devices * cap, query_tile(devices, cap)
    operand = like((length, LANES), LOW)
    shapes = [operand] * 3 + [
        like((length, LANES), WIDE),
        like((devices, cap // 2, LANES), LOW),
    ]
    return pl.pallas_call(
        lambda *refs: heavy_forward_kernel(1.0 / math.sqrt(HHD), *refs),
        grid=(length // tile,),
        in_specs=[whole(pair)],
        out_specs=[whole(operand)] * 3
        + [
            pl.BlockSpec((tile, LANES), lambda i: (i, 0)),
            pl.BlockSpec((tile // cap, cap // 2, LANES), lambda i: (i, 0, 0)),
        ],
        out_shape=shapes,
        compiler_params=params(60),
        cost_estimate=cost(7),
        name="heavy_forward",
    )(pair)


def heavy_backward(query, key, value, kept, grad):
    devices, half, _ = grad.shape
    cap = 2 * half
    length, tile = devices * cap, query_tile(devices, cap)
    triple = like((devices, cap + half, LANES), LOW)
    return pl.pallas_call(
        lambda *refs: heavy_backward_kernel(1.0 / math.sqrt(HHD), *refs),
        grid=(length // tile,),
        in_specs=[
            whole(query),
            whole(key),
            whole(value),
            pl.BlockSpec((tile, LANES), lambda i: (i, 0)),
            pl.BlockSpec((tile // cap, half, LANES), lambda i: (i, 0, 0)),
        ],
        out_specs=whole(triple),
        out_shape=triple,
        scratch_shapes=[pltpu.VMEM((length, LANES), WIDE)] * 3,
        compiler_params=params(60),
        cost_estimate=cost(10),
        name="heavy_backward",
    )(query, key, value, kept, grad)


def combine_kernel(pairs_ref, attn_ref, out_ref, slots_ref, gate_ref, part_ref, mix_ref):
    slots = slots_ref[0]
    mix = merge_folded(pairs_ref, 0, pairs_ref.shape[0]).astype(LOW)
    mix_ref[0] = mix
    rows = rows_dot(mix, out_ref[...])
    weight = jnp.where(column(slots, OK_QUERY) > 0, column(gate_ref[0], 0), 0.0)
    hot = hot_rows(slots, ROW_QUERY, attn_ref.shape[1]).astype(LOW)
    part_ref[0] = (attn_ref[0] + place_rows(hot, weight * rows)).astype(LOW)


def pair_spec(pairs, heads):
    return pl.BlockSpec((heads,) + pairs.shape[1:], lambda s: (s, 0, 0))


def combine(pairs, attn, weight_out, slots, gate):
    seqs, cap = slots.shape[:2]
    heavy_cols = weight_out.shape[1]
    shapes = [like(attn.shape, LOW), like((seqs, cap, heavy_cols), LOW)]
    return pl.pallas_call(
        combine_kernel,
        grid=(seqs,),
        in_specs=[
            pair_spec(pairs, heavy_cols // HHD),
            each(attn),
            whole(weight_out),
            each(slots),
            each(gate),
        ],
        out_specs=[each(s) for s in shapes],
        out_shape=shapes,
        compiler_params=params(),
        cost_estimate=cost(4),
        name="combine",
    )(pairs, attn, weight_out, slots, gate)


def slots_kernel(
    core_ref, tokens_ref, own_ref, other_ref, up_ref, gains_ref, routers_ref, slots_ref,
    low_ref, rows_ref, slot_ref, ship_ref, gate_ref,
):
    middle = tokens_ref[0].astype(WIDE) + own_ref[0].astype(WIDE) + other_ref[0].astype(WIDE)
    length = middle.shape[0]
    normed = middle * rms_of(middle) * gains_ref[1:2, :]
    low = normed.astype(LOW)
    low_ref[0] = low
    slots = slots_ref[0]
    hot = hot_rows(slots, ROW_MLP, length)
    logits = columns((length, LANES), row_dots(normed, routers_ref[2:3, :]))
    gate = jax.nn.sigmoid(column(exact_pick(hot, logits), 0))
    weight = jnp.where(column(slots, OK_MLP) > 0, gate, 0.0)
    hot = hot.astype(LOW)
    rows = dot(hot, low)
    slot = weight * dot(hot, up_ref[0])
    rows_ref[0] = rows.astype(LOW)
    slot_ref[0] = slot.astype(LOW)
    ship_ref[0] = jnp.where(core_ref[0, 0] == 0, rows, slot).astype(LOW)
    gate_ref[0] = columns((slots.shape[0], LANES), gate, weight)


def mlp_slots(core, tokens, own, other, up, gains, routers, slots):
    seqs, length, width = tokens.shape
    cap = slots.shape[1]
    shapes = [like(tokens.shape, LOW)]
    shapes += [like((seqs, cap, width), LOW)] * 3 + [like((seqs, cap, LANES), WIDE)]
    return pl.pallas_call(
        slots_kernel,
        grid=(seqs,),
        in_specs=[
            pl.BlockSpec(memory_space=pltpu.SMEM),
            each(tokens), each(own), each(other), each(up), whole(gains), whole(routers), each(slots),
        ],
        out_specs=[each(s) for s in shapes],
        out_shape=shapes,
        compiler_params=params(),
        cost_estimate=cost(5),
        name="mlp_slots",
    )(core, tokens, own, other, up, gains, routers, slots)


def pack_wide(ref, value):
    value = value.astype(LOW)
    rows, cols = value.shape[0], ref.shape[1]
    extra = value.shape[1] - cols
    group = rows * extra // cols
    ref[:rows, :] = value[:, :cols]
    for index in range(cols // extra):
        ref[rows:, index * extra : (index + 1) * extra] = value[
            index * group : (index + 1) * group, cols:
        ]


def unpack_wide(store, ref, start, rows, extra):
    cols = ref.shape[1]
    group = rows * extra // cols
    store(slice(0, rows), slice(0, cols), ref[start : start + rows, :])
    for index in range(cols // extra):
        store(
            slice(index * group, (index + 1) * group),
            slice(cols, cols + extra),
            ref[start + rows : start + rows + group, index * extra : (index + 1) * extra],
        )


def feed_kernel(
    low_ref, rows_ref, slot_ref, kept_ref, up_ref, slots_ref, in_ref, out_ref, heavy_in_ref,
    heavy_out_ref, part_ref, weights_ref, down_ref, gate_ref, heavy_acc, back_acc, hidden_ref, dgate_ref, dup_ref,
):
    step = pl.program_id(0)
    seqs, length, width = up_ref.shape
    cap = slots_ref.shape[1]

    @pl.when(step == 0)
    def _():
        heavy_acc[...] = jnp.zeros_like(heavy_acc)
        back_acc[...] = jnp.zeros_like(back_acc)

    first, second, last = heavy_in_ref[0], heavy_in_ref[1], heavy_out_ref[...]
    rows = rows_ref[...]
    hidden, gate_grad, up_grad = gelu_parts(
        dot(rows, first), dot(rows, second), dot(slot_ref[...], last)
    )
    heavy_acc[...] += rows_dot(hidden.astype(LOW), last)
    back_acc[...] += rows_dot(gate_grad.astype(LOW), first) + rows_dot(up_grad.astype(LOW), second)

    @pl.when(step == pl.num_programs(0) - 1)
    def _():
        for s in range(seqs):
            here = slice(s * length, (s + 1) * length)
            mine = slice(s * cap, (s + 1) * cap)
            low = low_ref[s]
            hidden, gate_grad, up_grad = gelu_parts(
                dot(low, in_ref[0]), dot(low, in_ref[1]), dot(up_ref[s], out_ref[...])
            )
            hidden, gate_grad, up_grad = (
                hidden.astype(LOW),
                gate_grad.astype(LOW),
                up_grad.astype(LOW),
            )
            hidden_ref[here, :] = hidden
            dgate_ref[here, :] = gate_grad
            dup_ref[here, :] = up_grad
            hot = hot_rows(slots_ref[s], ROW_MLP, length).astype(LOW)
            kept = kept_ref[s]
            heavy_rows = heavy_acc[mine, :]
            part_ref[0, s] = (
                rows_dot(hidden, out_ref[...]) + place_rows(hot, column(kept, 1) * heavy_rows)
            ).astype(LOW)
            part_ref[1, s] = (
                rows_dot(gate_grad, in_ref[0])
                + rows_dot(up_grad, in_ref[1])
                + place_rows(hot, back_acc[mine, :])
            ).astype(LOW)
            gate_part = jnp.sum(dot(hot, up_ref[s]) * heavy_rows, axis=-1, keepdims=True)
            gate_ref[s] = columns((cap, LANES), column(kept, 0), gate_part)
        low = low_ref[...].reshape(seqs * length, width)
        up = up_ref[...].reshape(seqs * length, width)
        pack_wide(weights_ref.at[0], cols_dot(low, dgate_ref[...]))
        pack_wide(weights_ref.at[1], cols_dot(low, dup_ref[...]))
        pack_wide(down_ref, cols_dot(up, hidden_ref[...]))


def feed(low, rows, slot, kept, up, slots, light_in, light_out, heavy_in, heavy_out, packed_cols):
    seqs, length, width = up.shape
    cap = slots.shape[1]
    hidden = light_out.shape[1]
    cols = 256
    rows, slot = rows.reshape(-1, width), slot.reshape(-1, width)
    shapes = [
        like((2, seqs, length, width), LOW),
        like((2, width * hidden // packed_cols, packed_cols), LOW),
        like((width * hidden // packed_cols, packed_cols), LOW),
        like((seqs, cap, LANES), WIDE),
    ]
    return pl.pallas_call(
        feed_kernel,
        grid=(heavy_out.shape[1] // cols,),
        in_specs=[
            whole(low),
            whole(rows),
            whole(slot),
            whole(kept),
            whole(up),
            whole(slots),
            whole(light_in),
            whole(light_out),
            pl.BlockSpec((2, width, cols), lambda i: (0, 0, i)),
            pl.BlockSpec((width, cols), lambda i: (0, i)),
        ],
        out_specs=[whole(s) for s in shapes],
        out_shape=shapes,
        scratch_shapes=[pltpu.VMEM((seqs * cap, width), WIDE)] * 2
        + [pltpu.VMEM((seqs * length, hidden), LOW)] * 3,
        compiler_params=params(),
        cost_estimate=cost(20),
        name="feed",
    )(low, rows, slot, kept, up, slots, light_in, light_out, heavy_in, heavy_out)


def middle_kernel(
    tokens_ref, own_ref, other_ref, part_ref, beyond_ref, up_ref, gains_ref, routers_ref, slots_ref,
    gate_ref, mlp_ref, mlp_other_ref, mix_ref, heavy_mix_ref, light_out_ref, heavy_out_ref, down_ref,
    mixed_ref, middle_ref, grad_ref, pair_ref, weights_ref, small_ref, logit_ref, weights_acc,
):
    step = pl.program_id(0)

    @pl.when(step == 0)
    def _():
        weights_acc[...] = jnp.zeros_like(weights_acc)
        small_ref[...] = jnp.zeros_like(small_ref)

    slots = slots_ref[0]
    cap = slots.shape[0]
    middle = tokens_ref[0].astype(WIDE) + own_ref[0].astype(WIDE) + other_ref[0].astype(WIDE)
    length = middle.shape[0]
    factor = rms_of(middle)
    scaled = middle * factor
    normed = scaled * gains_ref[1:2, :]
    mixed = middle + (part_ref[0, 0].astype(WIDE) + beyond_ref[0, 0].astype(WIDE))
    mixed_ref[0] = mixed.astype(LOW)
    gate = column(mlp_ref[0], 0)
    gate_grad = column(mlp_ref[0], 1) + column(mlp_other_ref[0], 1)
    logit_grad = jnp.where(column(slots, OK_MLP) > 0, gate_grad * gate * (1.0 - gate), 0.0)
    token_grad = column(
        exact_place(hot_rows(slots, ROW_MLP, length), columns((cap, LANES), logit_grad)), 0
    )
    normed_grad = (
        part_ref[1, 0].astype(WIDE) + beyond_ref[1, 0].astype(WIDE)
    ) + token_grad * routers_ref[2:3, :]
    small_ref[0:1, :] += jnp.sum(normed_grad * scaled, axis=0, keepdims=True)
    small_ref[1:2, :] += jnp.sum(token_grad * normed, axis=0, keepdims=True)
    middle_grad = up_ref[0].astype(WIDE) + norm_back(middle, factor, normed_grad * gains_ref[1:2, :])
    middle_ref[0] = middle_grad
    low = middle_grad.astype(LOW)
    hot = hot_rows(slots, ROW_QUERY, length).astype(LOW)
    up_rows = dot(hot, low)
    weight = jnp.where(column(slots, OK_QUERY) > 0, column(gate_ref[0], 0), 0.0)
    slot = (weight * up_rows).astype(LOW)
    heavy_rows = rows_dot(heavy_mix_ref[0], heavy_out_ref[...])
    logit_ref[0] = columns(
        (cap, LANES), jnp.sum(up_rows * heavy_rows, axis=-1, keepdims=True)
    )
    mix_grad = dot(slot, heavy_out_ref[...]).astype(LOW).astype(WIDE)
    for head in range(mix_grad.shape[1] // HHD):
        pair_ref[head] = fold(head_low(mix_grad, head)).astype(LOW)
    grad_ref[0] = dot(low, light_out_ref[...]).astype(LOW)
    weights_acc[0] += cols_dot(low, mix_ref[0])
    weights_acc[1] += cols_dot(slot, heavy_mix_ref[0])

    @pl.when(step == pl.num_programs(0) - 1)
    def _():
        start, rows = down_ref.shape[0], weights_acc.shape[1]
        weights_ref[:start, :] = down_ref[...]
        for kind in range(2):
            weights_ref[start + kind * rows : start + (kind + 1) * rows, :] = weights_acc[kind].astype(LOW)


def middle_back(
    tokens, own, other, part, beyond, up, gains, routers, slots, gate, mlp, mlp_other,
    mix, heavy_mix, light_out, heavy_out, down, seq_devices,
):
    seqs, length, width = tokens.shape
    cap = slots.shape[1]
    cols = light_out.shape[1]
    heads = heavy_out.shape[1] // HHD
    shapes = [
        like(tokens.shape, LOW),
        like(tokens.shape, WIDE),
        like((seqs, length, cols), LOW),
        like((seq_devices, cap // 2, LANES), LOW),
        like((down.shape[0] + 2 * width, cols), LOW),
        like((8, width), WIDE),
        like((seqs, cap, LANES), WIDE),
    ]
    specs = [
        each(shapes[0]), each(shapes[1]), each(shapes[2]), pair_spec(shapes[3], heads),
        whole(shapes[4]), whole(shapes[5]), each(shapes[6]),
    ]
    both = pl.BlockSpec((2, 1, length, width), lambda s: (0, s, 0, 0))
    return pl.pallas_call(
        middle_kernel,
        grid=(seqs,),
        in_specs=[
            each(tokens), each(own), each(other), both, both, each(up), whole(gains),
            whole(routers), each(slots), each(gate), each(mlp), each(mlp_other), each(mix),
            each(heavy_mix), whole(light_out), whole(heavy_out), whole(down),
        ],
        out_specs=specs,
        out_shape=shapes,
        scratch_shapes=[pltpu.VMEM((2, width, cols), WIDE)],
        compiler_params=params(),
        cost_estimate=cost(11),
        name="middle_back",
    )(
        tokens, own, other, part, beyond, up, gains, routers, slots, gate, mlp, mlp_other,
        mix, heavy_mix, light_out, heavy_out, down,
    )


def light_project_kernel(local_ref, low_ref, light_ref, first_ref, grad_ref, part_ref, first_acc):
    @pl.when(pl.program_id(0) == 0)
    def _():
        first_acc[...] = jnp.zeros_like(first_acc)
        grad_ref[...] = jnp.zeros_like(grad_ref)

    low = low_ref[0]
    part = None
    for kind in range(3):
        rows = local_ref[0, kind]
        if kind == 0:
            first_acc[...] += cols_dot(low, rows)
        else:
            grad_ref[kind - 1] += cols_dot(low, rows)
        more = rows_dot(rows, light_ref[kind])
        part = more if part is None else part + more
    part_ref[0] = part

    @pl.when(pl.program_id(0) == pl.num_programs(0) - 1)
    def _():
        first_ref[...] = first_acc[...].astype(LOW)


def light_project(local, low, light):
    shapes = [
        like(light.shape[1:], LOW),
        like((2,) + light.shape[1:], WIDE),
        like(low.shape, WIDE),
    ]
    return pl.pallas_call(
        light_project_kernel,
        grid=(low.shape[0],),
        in_specs=[each(local), each(low), whole(light)],
        out_specs=[whole(shapes[0]), whole(shapes[1]), each(shapes[2])],
        out_shape=shapes,
        scratch_shapes=[pltpu.VMEM(light.shape[1:], WIDE)],
        compiler_params=params(),
        cost_estimate=cost(9),
        name="light_project",
    )(local, low, light)


def heavy_project_kernel(
    light_part_ref, low_ref, pairs_ref, heavy_ref, slots_ref, gate_ref, raw_ref, logit_ref,
    grad_ref, part_ref, both_logit_ref, grad_acc,
):
    step = pl.program_id(0)

    @pl.when(step == 0)
    def _():
        grad_acc[...] = jnp.zeros_like(grad_acc)

    low = low_ref[0]
    length = low.shape[0]
    slots = slots_ref[0]
    cap = slots.shape[0]
    heads = raw_ref.shape[2] // HHD
    key_gate = column(gate_ref[0], 1)
    query_grad = merge_heads(pairs_ref, cap, heads).astype(LOW)
    key_grad = merge_upper(pairs_ref, cap, heads).astype(LOW)
    value_grad = merge_folded(pairs_ref, cap, heads)
    raw_grad = (key_gate * value_grad).astype(LOW)
    key_logit = jnp.sum(value_grad * raw_ref[0], axis=-1, keepdims=True)
    both_logit_ref[0] = columns((cap, LANES), column(logit_ref[0], 0), key_logit)
    hot_query = hot_rows(slots, ROW_QUERY, length).astype(LOW)
    hot_key = hot_rows(slots, ROW_KEY, length).astype(LOW)
    query_in = dot(hot_query, low).astype(LOW)
    key_in = dot(hot_key, low).astype(LOW)
    grad_acc[0] += cols_dot(query_in, query_grad)
    grad_acc[1] += cols_dot(key_in, key_grad)
    grad_acc[2] += cols_dot(key_in, raw_grad)
    part = light_part_ref[0] + place_rows(hot_query, rows_dot(query_grad, heavy_ref[0]))
    part = part + place_rows(
        hot_key, rows_dot(key_grad, heavy_ref[1]) + rows_dot(raw_grad, heavy_ref[2])
    )
    part_ref[0] = part

    @pl.when(step == pl.num_programs(0) - 1)
    def _():
        grad_ref[...] = grad_acc[...].astype(LOW)


def heavy_project(light_part, low, pairs, heavy, slots, gate, raw, logit):
    heads = heavy.shape[2] // HHD
    shapes = [like(heavy.shape, LOW), like(low.shape, WIDE), like(logit.shape, WIDE)]
    return pl.pallas_call(
        heavy_project_kernel,
        grid=(low.shape[0],),
        in_specs=[
            each(light_part), each(low), pair_spec(pairs, heads), whole(heavy), each(slots),
            each(gate), each(raw), each(logit),
        ],
        out_specs=[whole(shapes[0]), each(shapes[1]), each(shapes[2])],
        out_shape=shapes,
        scratch_shapes=[pltpu.VMEM(heavy.shape, WIDE)],
        compiler_params=params(),
        cost_estimate=cost(10),
        name="heavy_project",
    )(light_part, low, pairs, heavy, slots, gate, raw, logit)


def edge_project_kernel(
    part_in_ref, low_ref, lead_ref, tail_ref, key_ref, value_ref, first_ref, sum_ref,
    grad_ref, part_ref, grad_acc,
):
    step = pl.program_id(0)

    @pl.when(step == 0)
    def _():
        grad_acc[...] = sum_ref[...]

    length = low_ref.shape[1]
    part_ref[0, WIN : length - WIN, :] = part_in_ref[0, WIN : length - WIN, :].astype(LOW)
    for ref, rows in ((lead_ref, slice(0, WIN)), (tail_ref, slice(length - WIN, length))):
        for kind in range(2):
            grad_acc[kind] += cols_dot(low_ref[0, rows, :], ref[0, kind])
        more = rows_dot(ref[0, 0], key_ref[0]) + rows_dot(ref[0, 1], value_ref[0])
        part_ref[0, rows, :] = (part_in_ref[0, rows, :] + more).astype(LOW)

    @pl.when(step == pl.num_programs(0) - 1)
    def _():
        grad_ref[0] = first_ref[...]
        grad_ref[1:] = grad_acc[...].astype(LOW)


def edge_project(part, low, lead, tail, light, first, light_sum):
    shapes = [like(light.shape, LOW), like(low.shape, LOW)]
    kinds = [
        pl.BlockSpec(
            (1,) + light.shape[1:], lambda s, kind=kind: (kind, 0, 0), pipeline_mode=pl.Buffered(1)
        )
        for kind in (1, 2)
    ]
    return pl.pallas_call(
        edge_project_kernel,
        grid=(low.shape[0],),
        in_specs=[each(part), each(low), each(lead), each(tail)]
        + kinds
        + [whole(first), whole(light_sum)],
        out_specs=[whole(shapes[0]), each(shapes[1])],
        out_shape=shapes,
        scratch_shapes=[pltpu.VMEM((2,) + light.shape[1:], WIDE)],
        compiler_params=params(),
        cost_estimate=cost(5),
        name="edge_project",
    )(part, low, lead, tail, light, light, first, light_sum)


def input_kernel(
    part_ref, other_ref, logit_ref, logit_other_ref, gate_ref, slots_ref, tokens_ref, gains_ref,
    routers_ref, middle_ref, small_in_ref, grad_ref, rows_ref, small_ref,
):
    @pl.when(pl.program_id(0) == 0)
    def _():
        small_ref[...] = small_in_ref[...]
        rows_ref[...] = jnp.zeros_like(rows_ref)

    slots = slots_ref[0]
    cap = slots.shape[0]
    inputs = tokens_ref[0].astype(WIDE)
    length = inputs.shape[0]
    factor = rms_of(inputs)
    scaled = inputs * factor
    normed = scaled * gains_ref[0:1, :]
    gates = gate_ref[0]
    grads = (logit_ref[0] + logit_other_ref[0]) * gates * (1.0 - gates)
    query_logit = jnp.where(column(slots, OK_QUERY) > 0, column(grads, 0), 0.0)
    key_logit = jnp.where(column(slots, OK_KEY) > 0, column(grads, 1), 0.0)
    query_token = column(
        exact_place(hot_rows(slots, ROW_QUERY, length), columns((cap, LANES), query_logit)), 0
    )
    key_token = column(
        exact_place(hot_rows(slots, ROW_KEY, length), columns((cap, LANES), key_logit)), 0
    )
    normed_grad = (
        (part_ref[0].astype(WIDE) + other_ref[0].astype(WIDE))
        + query_token * routers_ref[0:1, :]
        + key_token * routers_ref[1:2, :]
    )
    small_ref[2:3, :] += jnp.sum(normed_grad * scaled, axis=0, keepdims=True)
    small_ref[3:4, :] += jnp.sum(query_token * normed, axis=0, keepdims=True)
    small_ref[4:5, :] += jnp.sum(key_token * normed, axis=0, keepdims=True)
    grad_ref[0] = middle_ref[0] + norm_back(inputs, factor, normed_grad * gains_ref[0:1, :])

    @pl.when(pl.program_id(0) == pl.num_programs(0) - 1)
    def _():
        cols = rows_ref.shape[1]
        sums = small_ref[...]
        folded = jnp.concatenate([sums[:, :cols], sums[:, cols:]], axis=0)
        rows_ref[: folded.shape[0], :] = folded.astype(LOW)


def input_back(
    part, other, logit, logit_other, gate, slots, tokens, gains, routers, middle, small, rows
):
    shapes = [like(middle.shape, WIDE), like((rows, small.shape[1] // 2), LOW)]
    return pl.pallas_call(
        input_kernel,
        grid=(tokens.shape[0],),
        in_specs=[
            each(part), each(other), each(logit), each(logit_other), each(gate), each(slots),
            each(tokens), whole(gains), whole(routers), each(middle), whole(small),
        ],
        out_specs=[each(shapes[0]), whole(shapes[1])],
        out_shape=shapes,
        scratch_shapes=[pltpu.VMEM(small.shape, WIDE)],
        compiler_params=params(),
        cost_estimate=cost(6),
        name="input_back",
    )(part, other, logit, logit_other, gate, slots, tokens, gains, routers, middle, small)


def heavy_weights_kernel(tile, core_ref, here_ref, there_ref, in_ref, out_ref, *refs):
    din_ref, dout_ref, rows_ref, grad_ref, hidden_ref, gate_ref, up_ref, sems = refs[-8:]

    starts = range(0, rows_ref.shape[0], tile)
    first = pl.program_id(0) == 0

    def copies(rows_from, grad_from, index):
        part = pl.ds(index * tile, tile)
        return [
            pltpu.make_async_copy(rows_from.at[part, :], rows_ref.at[part, :], sems.at[0, index]),
            pltpu.make_async_copy(grad_from.at[part, :], grad_ref.at[part, :], sems.at[1, index]),
        ]

    def fetch(rows_from, grad_from):
        for index in range(len(starts)):
            for copy in copies(rows_from, grad_from, index):
                copy.start()

    @pl.when(first & (core_ref[0, 0] == 0))
    def _():
        fetch(here_ref, there_ref)

    @pl.when(first & (core_ref[0, 0] != 0))
    def _():
        fetch(there_ref, here_ref)

    def every_tile(waits):
        for index, start in enumerate(starts):
            if waits:
                for copy in copies(here_ref, there_ref, index):
                    copy.wait()
            part = pl.ds(start, tile)
            rows = rows_ref[part, :]
            hidden, gate_grad, up_grad = gelu_parts(
                dot(rows, in_ref[0]), dot(rows, in_ref[1]), dot(grad_ref[part, :], out_ref[...])
            )
            hidden_ref[part, :] = hidden.astype(LOW)
            gate_ref[part, :] = gate_grad.astype(LOW)
            up_ref[part, :] = up_grad.astype(LOW)

    pl.when(first)(lambda: every_tile(True))
    pl.when(jnp.logical_not(first))(lambda: every_tile(False))
    dout_ref[...] = cols_dot(grad_ref[...], hidden_ref[...])
    din_ref[:, 0, :] = cols_dot(rows_ref[...], gate_ref[...])
    din_ref[:, 1, :] = cols_dot(rows_ref[...], up_ref[...])


def heavy_weights(core, here, there, weight_in, weight_out, first_block, count_blocks, done):
    count, width = here.shape
    hidden = weight_out.shape[1]
    cols = 256
    tile = 512 if count % 512 == 0 else count
    out_block = pl.BlockSpec((width, cols), lambda i: (0, first_block + i))
    in_block = pl.BlockSpec((width, 2, cols), lambda i: (0, 0, first_block + i))
    return pl.pallas_call(
        lambda *refs: heavy_weights_kernel(tile, *refs),
        grid=(count_blocks,),
        in_specs=[
            pl.BlockSpec(memory_space=pltpu.SMEM),
            pl.BlockSpec(memory_space=pl.ANY),
            pl.BlockSpec(memory_space=pl.ANY),
            pl.BlockSpec((2, width, cols), lambda i: (0, 0, first_block + i)),
            out_block,
        ]
        + [pl.BlockSpec(memory_space=pl.ANY)] * len(done),
        out_specs=[in_block, out_block],
        out_shape=[like((width, 2, hidden), WIDE), like((width, hidden), WIDE)],
        scratch_shapes=[pltpu.VMEM((count, width), LOW)] * 2
        + [pltpu.VMEM((count, cols), LOW)] * 3
        + [pltpu.SemaphoreType.DMA((2, count // tile))],
        input_output_aliases={5 + i: i for i in range(len(done))},
        compiler_params=params(60),
        cost_estimate=cost(4 + 9 * count_blocks * count / 3072),
        name="heavy_weights",
    )(core, here, there, weight_in, weight_out, *done)


def bit_pairs(bit):
    return [(i, i ^ (1 << bit)) for i in range(lax.axis_size("seq"))]


def bit_here(bit):
    return (lax.axis_index("seq") >> bit) & 1


def after(value, *others):
    return lax.optimization_barrier((value,) + others)[0]


def scatter_start(value, bit):
    halves = value.reshape(2, value.shape[0] // 2, value.shape[1])
    mine = bit_here(bit)
    sent = lax.dynamic_index_in_dim(halves, 1 - mine, 0, keepdims=False)
    kept = lax.dynamic_index_in_dim(halves, mine, 0, keepdims=False)
    return kept, lax.ppermute(sent, "seq", bit_pairs(bit))


def scatter_end(started, *others):
    kept, got = started
    got = after(got, *others)
    return (kept.astype(WIDE) + got.astype(WIDE)).astype(LOW)


def gather_start(value, bit):
    return value, lax.ppermute(value, "seq", bit_pairs(bit)), bit_here(bit)


def gather_end(started, *others):
    value, got, mine = started
    got = after(got, *others)
    return jnp.where(
        mine == 0,
        jnp.concatenate([value, got], axis=0),
        jnp.concatenate([got, value], axis=0),
    )


def interleave(parts, blocks):
    cut = [p.reshape(blocks, -1, p.shape[1]) for p in parts]
    return jnp.concatenate(cut, axis=1).reshape(-1, parts[0].shape[1])


def apart(value, blocks, rows):
    cut = value.reshape(blocks, -1, value.shape[1])
    marks = [sum(rows[:i]) // blocks for i in range(len(rows) + 1)]
    return [
        cut[:, marks[i] : marks[i + 1]].reshape(-1, value.shape[1]) for i in range(len(rows))
    ]


def in_order(bit_ref, mine_ref, got_ref, body):
    pl.when(bit_ref[0, 0] == 0)(lambda: body(mine_ref, got_ref))
    pl.when(bit_ref[0, 0] != 0)(lambda: body(got_ref, mine_ref))


def finish_call(kernel, bit, mine, got, shapes, name):
    shapes = [like(shape, WIDE) for shape in shapes]
    return pl.pallas_call(
        kernel,
        in_specs=[
            pl.BlockSpec(memory_space=pltpu.SMEM),
            pl.BlockSpec(memory_space=pltpu.VMEM),
            pl.BlockSpec(memory_space=pltpu.VMEM),
        ],
        out_shape=shapes,
        compiler_params=params(),
        name=name,
    )(bit_here(bit).astype(jnp.int32).reshape(1, 1), mine, got)


def feed_in_kernel(bit_ref, mine_ref, got_ref, in_ref):
    width, _, hidden = in_ref.shape

    def body(*halves):
        for kind, ref in enumerate(halves):

            def store(rows, cols, value, kind=kind):
                in_ref[rows, kind, cols] = value.astype(WIDE)

            unpack_wide(store, ref, 0, width, hidden - ref.shape[1])

    in_order(bit_ref, mine_ref, got_ref, body)


def outs_kernel(bit_ref, mine_ref, got_ref, feed_ref, light_ref, heavy_ref):
    width, hidden = feed_ref.shape

    def body(first_ref, second_ref):
        half, cols = first_ref.shape

        def store(rows, lanes, value):
            feed_ref[rows, lanes] = value.astype(WIDE)

        unpack_wide(store, first_ref, 0, width, hidden - cols)
        start = width * hidden // cols
        light_ref[: half - start, :] = first_ref[start:, :].astype(WIDE)
        rest = width - (half - start)
        light_ref[half - start :, :] = second_ref[:rest, :].astype(WIDE)
        heavy_ref[...] = second_ref[rest:, :].astype(WIDE)

    in_order(bit_ref, mine_ref, got_ref, body)


def kinds_kernel(bit_ref, mine_ref, got_ref, wide_ref):
    def body(first_ref, second_ref):
        half = first_ref.shape[0]
        wide_ref[:half, :] = first_ref[...].astype(WIDE)
        wide_ref[half:, :] = second_ref[...].astype(WIDE)

    in_order(bit_ref, mine_ref, got_ref, body)


def widen(bit, mine, got, name):
    rows, cols = mine.shape
    half = pl.BlockSpec((rows, LANES), lambda i: (0, i))
    return pl.pallas_call(
        kinds_kernel,
        grid=(cols // LANES,),
        in_specs=[pl.BlockSpec(memory_space=pltpu.SMEM), half, half],
        out_specs=pl.BlockSpec((2 * rows, LANES), lambda i: (0, i)),
        out_shape=like((2 * rows, cols), WIDE),
        compiler_params=params(24),
        name=name,
    )(bit_here(bit).astype(jnp.int32).reshape(1, 1), mine, got)


def other_core(value):
    return lax.ppermute(value, "mp", [(0, 1), (1, 0)])


def to_neighbours(first, last):
    peers = lax.axis_size("seq")
    up = [(i, i + 1) for i in range(peers - 1)]
    down = [(i + 1, i) for i in range(peers - 1)]
    return lax.ppermute(last, "seq", up), lax.ppermute(first, "seq", down)


def exchange(pairs):
    return lax.all_to_all(pairs, "seq", split_axis=0, concat_axis=0, tiled=True)


def by_kind(weights):
    return weights.transpose(1, 0, 2)


def shards(
    tokens,
    out_grad,
    gains,
    routers,
    light_query_key_value_weight,
    light_attention_output_weight,
    heavy_qkv,
    heavy_out,
    light_feedforward_input_weight,
    light_feedforward_output_weight,
    heavy_mlp_in,
    heavy_mlp_out,
    routed_queries,
    routed_keys,
    routed_mlp,
    block_counts,
):
    seq_count, local_len, width = tokens.shape
    seq_devices = lax.axis_size("seq")
    row_base = lax.axis_index("seq") * local_len
    capacity = routed_queries.shape[1]
    light_cols = light_query_key_value_weight.shape[2]
    gain_rows, router_rows = gains.T, routers.T
    slot_ids = jnp.arange(capacity, dtype=jnp.int32)[None, :, None]
    rows = jnp.stack([routed_queries, routed_keys, routed_mlp], axis=2) - row_base
    valid = (slot_ids < block_counts).astype(jnp.int32)
    slots = jnp.concatenate([rows, valid], axis=2)
    place = jnp.stack([row_base, jnp.int32(seq_devices * local_len)]).astype(jnp.int32)[None, :]
    core = lax.axis_index("mp").astype(jnp.int32).reshape(1, 1)
    light_weights = by_kind(light_query_key_value_weight)
    heavy_weights_qkv = by_kind(heavy_qkv)

    own_tokens = lax.dynamic_index_in_dim(tokens, lax.axis_index("mp"), 0, keepdims=False)
    edges = to_neighbours(own_tokens[:WIN], own_tokens[local_len - WIN :])
    low, pairs, raw, gate = front(
        tokens, gain_rows, router_rows, slots, heavy_weights_qkv, seq_devices
    )
    edges = [after(edge, low) for edge in edges]
    first_core = lax.axis_index("mp") == 0
    before, behind = [
        jnp.where(first_core, jnp.stack([mine, more]), jnp.stack([more, mine]))
        for mine, more in zip(edges, [other_core(edge) for edge in edges])
    ]
    pair = exchange(after(pairs, before, behind))
    mix, attn, lse, query, window = light_forward(
        place, low, before, behind, gain_rows, light_weights, light_attention_output_weight
    )
    pair_query, pair_key, pair_value, kept, pair_mix = heavy_forward(after(pair, attn))
    mix_pairs = exchange(pair_mix)
    light_in = by_kind(after(light_feedforward_input_weight, kept))
    heavy_in = by_kind(after(heavy_mlp_in, kept))
    own, heavy_mix = combine(after(mix_pairs, light_in, heavy_in), attn, heavy_out, slots, gate)
    other = other_core(own)
    low_two, rows, slot, ship, gate_two = mlp_slots(
        core, tokens, own, other, out_grad, gain_rows, router_rows, slots
    )
    all_slots = seq_count * capacity * seq_devices
    gather_heavy = 2 * all_slots * width < 4 * (heavy_mlp_in.size + heavy_mlp_out.size)
    here = lax.all_gather(ship, "seq", axis=1, tiled=True) if gather_heavy else ship
    part, feed_grads, down_grad, mlp = feed(
        low_two, rows, slot, gate_two, out_grad, slots, light_in, light_feedforward_output_weight,
        heavy_in, heavy_mlp_out, light_cols,
    )
    beyond, mlp_other = other_core(part), other_core(mlp)
    bits = (seq_devices - 1).bit_length()
    blocks = 1 << (bits - 2)
    first_going = scatter_start(feed_grads.reshape(-1, light_cols), 0)
    mixed, middle_grad, mix_grad, grad_pairs, out_grads, small, query_logit = middle_back(
        tokens, own, other, part, beyond, out_grad, gain_rows, router_rows, slots, gate, mlp,
        mlp_other, mix, heavy_mix, light_attention_output_weight, heavy_out, down_grad, seq_devices,
    )
    pair_grad = exchange(grad_pairs)
    local, early, late = light_backward(place, query, window, lse, mix_grad)
    first_wave = scatter_end(first_going, local)
    lead, tail = to_neighbours(early, late)
    triple = heavy_backward(
        pair_query, pair_key, pair_value, kept, after(pair_grad, local, first_wave)
    )
    triple_pairs = exchange(triple)
    second_going = scatter_start(after(out_grads, triple), 1)
    light_first, light_sums, light_part = light_project(after(local, triple), low, light_weights)
    heavy_grads, part_sum, logit = heavy_project(
        light_part, low, triple_pairs, heavy_weights_qkv, slots, gate, raw, query_logit
    )
    second_wave = scatter_end(second_going, part_sum)
    light_grads, low_part = edge_project(
        after(part_sum, second_wave), low, lead, tail, light_weights, light_first, light_sums
    )
    heavy_going = scatter_start(heavy_grads.reshape(-1, light_cols), 1)
    light_going = scatter_start(light_grads.reshape(-1, light_cols), 0)
    second_going = scatter_start(after(second_wave, low_part), 0)
    first_going = scatter_start(after(first_wave, low_part), 1)
    low_other, logit_other = other_core(low_part), other_core(logit)
    here = after(here, low_part)
    there = other_core(here).reshape(-1, width)
    here = here.reshape(-1, width)
    blocks_done = [0]
    heavy_sums = []

    def heavy_piece(count, *others):
        heavy_sums[:] = heavy_weights(
            core, after(here, *others), there, heavy_in, heavy_mlp_out, blocks_done[0], count, heavy_sums
        )
        blocks_done[0] += count
        return heavy_sums[1]

    input_grad, small_rows = input_back(
        low_part, low_other, logit, logit_other, gate, slots, tokens, gain_rows,
        router_rows, middle_grad, small, 16 * blocks,
    )
    small_got = lax.ppermute(small_rows, "seq", bit_pairs(1))
    second_wave = scatter_end(second_going, input_grad)
    first_wave = scatter_end(first_going, input_grad)
    early_sizes = [first_wave.shape[0], second_wave.shape[0]]
    wave = interleave([first_wave, second_wave], blocks)
    going = scatter_start(wave, 2)
    mark = heavy_piece(2, input_grad, wave)
    wave = scatter_end(going, mark)
    heavy_wave = scatter_end(heavy_going, mark)
    light_wave = scatter_end(light_going, mark)
    light_going = scatter_start(light_wave, 1)
    small_rows = scatter_end((small_rows, small_got), mark)
    for bit in range(3, bits - 1):
        wave = scatter_end(scatter_start(wave, bit))
    going = scatter_start(wave, bits - 1)
    heavy_going = scatter_start(heavy_wave, 0)
    small_got = lax.ppermute(small_rows, "seq", bit_pairs(0))
    mark = heavy_piece(1, wave, heavy_wave, light_wave, small_rows)
    wave = scatter_end(going, mark)
    heavy_wave = scatter_end(heavy_going, mark)
    light_wave = scatter_end(light_going, mark)
    small_rows = scatter_end((small_rows, small_got), mark)
    for bit in reversed(range(4, bits)):
        wave = gather_end(gather_start(wave, bit))
    going = gather_start(wave, 3)
    late_wave = [light_wave, heavy_wave, small_rows]
    late_sizes = [p.shape[0] for p in late_wave]
    late_wave = interleave(late_wave, blocks)
    late_going = scatter_start(late_wave, 2)
    mark = heavy_piece(1, late_wave, wave)
    wave = gather_end(going, mark)
    late_wave = scatter_end(late_going, mark)
    for bit in range(3, bits - 1):
        late_wave = scatter_end(scatter_start(late_wave, bit))
    going = gather_start(wave, 2)
    late_going = scatter_start(late_wave, bits - 1)
    mark = heavy_piece(1, late_wave, wave)
    wave = apart(gather_end(going, mark), blocks, early_sizes)
    going = [gather_start(p, bit) for p, bit in zip(wave, (1, 0))]
    late_wave = scatter_end(late_going, mark)
    for bit in reversed(range(4, bits)):
        late_wave = gather_end(gather_start(late_wave, bit))
    late_going = gather_start(late_wave, 3)
    mark = heavy_piece(1, late_wave, *wave)
    wave = [gather_end(p, mark) for p in going]
    early_halves = [(p, lax.ppermute(p, "seq", bit_pairs(bit))) for p, bit in zip(wave, (0, 1))]
    late_wave = gather_end(late_going, mark)
    late_going = gather_start(late_wave, 2)
    mark = heavy_piece(1, late_wave, *wave)
    late_wave = apart(gather_end(late_going, mark), blocks, late_sizes)
    small_sum = late_wave.pop().astype(WIDE)
    late_going = [gather_start(p, bit) for p, bit in zip(late_wave, (1, 0))]
    early_halves = [(after(p, *late_wave), after(got, mark)) for p, got in early_halves]
    hidden = light_feedforward_output_weight.shape[1]
    square = (width, light_cols)
    (feed_in,) = finish_call(feed_in_kernel, 0, *early_halves[0], [(width, 2, hidden)], "feed_in")
    feed_out, light_out_sum, heavy_out_sum = finish_call(
        outs_kernel, 1, *early_halves[1], [(width, hidden), square, square], "outs"
    )
    late_wave = [gather_end(p, feed_in, feed_out) for p in late_going]
    late_halves = [
        (p, lax.ppermute(p, "seq", bit_pairs(bit))) for p, bit in zip(late_wave, (0, 1))
    ]
    mark = heavy_piece(1, *late_wave)
    late_halves = [(p, after(got, mark)) for p, got in late_halves]
    heavy_in_grad, heavy_out_grad = heavy_sums
    if not gather_heavy:
        sums = [heavy_in_grad[:, 0], heavy_in_grad[:, 1], heavy_out_grad]
        sums = [p.astype(LOW) for p in sums]
        for bit in range(bits):
            sums = [scatter_end(scatter_start(p, bit)) for p in sums]
        for bit in reversed(range(bits)):
            sums = [gather_end(gather_start(p, bit)) for p in sums]
        heavy_in_grad = jnp.stack(sums[:2], axis=1).astype(WIDE)
        heavy_out_grad = sums[2].astype(WIDE)
    light_sum = widen(0, *late_halves[0], "light_sum")
    heavy_sum = widen(1, *late_halves[1], "heavy_sum")
    small_sum = jnp.concatenate([small_sum[:8], small_sum[8:16]], axis=1)
    return (
        mixed,
        input_grad,
        light_sum.reshape(3, width, light_cols).transpose(1, 0, 2),
        light_out_sum,
        heavy_sum.reshape(3, width, light_cols).transpose(1, 0, 2),
        heavy_out_sum,
        feed_in,
        feed_out,
        heavy_in_grad,
        heavy_out_grad,
        jnp.stack([small_sum[2], small_sum[0]], axis=1),
        jnp.stack([small_sum[3], small_sum[4], small_sum[1]], axis=1),
    )


def solution(mesh):
    rows = P(None, "seq", None)
    by_column = P(None, None, "mp")
    by_hidden = P(None, "mp")
    slots = P(None, "seq")
    weights = (by_column, by_hidden) * 4
    return jax.shard_map(
        shards,
        mesh=mesh,
        in_specs=(rows, rows, P(), P()) + weights + (slots, slots, slots, rows),
        out_specs=(rows, rows) + weights + (P(), P()),
        check_vma=False,
    )
```
